128 devices in a mesh: side: 2 (over y_hi), expert: 8 (over y_lo, z), tp: 8 (over x, core).
Axes of the slice: x: 4, y: 4 (y_hi: 2, y_lo: 2; y = y_hi * 2 + y_lo), z: 4, core: 2. Of those that a mesh axis runs over, the one named last changes fastest.
Arguments:
- resid: bfloat16 [512, 6144], P(('side', 'expert', 'tp')), may hold values from -6 to 6
- query: bfloat16 [512, 6144], P(('side', 'expert', 'tp')), may hold values from -90 to 90
- key_cache: bfloat16 [512, 128, 1024], P(('side', 'expert', 'tp')), may hold values from -4 to 4
- value_cache: bfloat16 [512, 128, 1024], P(('side', 'expert', 'tp')), may hold values from -6 to 6
- new_key: bfloat16 [512, 1024], P(('side', 'expert', 'tp')), may hold values from -5 to 5
- new_value: bfloat16 [512, 1024], P(('side', 'expert', 'tp')), may hold values from -5 to 5
- cache_len: int32 [512], P(('side', 'expert', 'tp')), may hold values from 2 to 128, as said below
- norm_gain: float32 [6144], replicated, may hold values from 0.1 to 1.9
- routes: int32 [512, 4], P(('side', 'expert')), may hold values from 0 to 15, all different within a row; in each aligned block of 4 rows (0 to 3, 4 to 7, ...) at most 2 rows name the same one
- gate_fixed: int32 [512, 4], P(('side', 'expert')), may hold values from 1 to 4095
- w_gate: bfloat16 [16, 5376, 6144], P(('side', 'expert'), 'tp'), may hold values from -0.078125 to 0.078125
- w_up: bfloat16 [16, 5376, 6144], P(('side', 'expert'), 'tp'), may hold values from -0.078125 to 0.078125
- w_down: bfloat16 [16, 5376, 6144], P(('side', 'expert'), 'tp'), may hold values from -0.078125 to 0.078125
Outputs:
- layer_out: bfloat16 [512, 6144], P(('side', 'expert', 'tp'))
The draws below stay inside these ranges and needn't reach their ends.
Inputs may be any that keep to these rules, and one draw needn't show every extreme that they name: `cache_len`: a row's cache holds at least 2 valid positions; in every draw all rows of some device hold 128. `routes`: each row names 4 different experts; within the rows of one device no expert is named by more than 2 rows, a bound that some block reaches.
All inputs are finite; a program needn't handle non-finite values.
Results may differ from the reference program's by a relative error of at most 0.007.
Values may be sent and summed in bfloat16 or wider, within the bound.
A program may use at most 128 MiB of HBM per device.

```python
import math
import jax
import jax.numpy as jnp
import numpy as np
from jax import lax

D = 6144
HEADS = 48
KV_HEADS = 8
HEAD_DIM = 128
TOP = 4
FFW = 5376
ROWS_DEV = 4
CACHE_LEN = 128
EXPERTS = 16
ROWS = 512
CAP_DEV = 2


def shared_keys(key):
    base = jax.random.normal(key, (ROWS, CACHE_LEN, KV_HEADS * HEAD_DIM), jnp.float32)
    return jnp.clip(base, -4.0, 4.0)


def draw_key_cache(key, part):
    base = shared_keys(key)
    return base.astype(jnp.bfloat16)


def draw_query(key, part):
    key = jax.random.fold_in(key, 12)
    values = jnp.clip(jax.random.normal(key, (ROWS, HEADS * HEAD_DIM), jnp.float32), -5.0, 5.0)
    return values.astype(jnp.bfloat16)


def draw_cache_len(key, part):
    key = jax.random.fold_in(key, 13)
    lengths = jax.random.randint(key, (ROWS,), 2, CACHE_LEN + 1)
    full_device = jax.random.randint(jax.random.fold_in(key, 1), (), 0, ROWS // ROWS_DEV)
    owners = jnp.arange(ROWS) // ROWS_DEV
    lengths = jnp.where(owners == full_device, CACHE_LEN, lengths)
    return lengths.astype(jnp.int32)


def with_ends(entries, stream_key, least, high):
    longest = entries.shape.index(max(entries.shape))
    spots = []
    for shift in (0, 1):
        where = [jax.random.randint(jax.random.fold_in(stream_key, axis), (), 0, length) for axis, length in enumerate(entries.shape)]
        where[longest] = (where[longest] + shift) % entries.shape[longest]
        spots.append(tuple(where))
    return entries.at[spots[0]].set(least).at[spots[1]].set(high)


def block_levels(key, dims, cuts, low, high):
    factor_of, own = 1.0, jax.random.fold_in(key, 6)
    for dim, blocks in cuts:
        steps = jnp.exp(jax.random.uniform(jax.random.fold_in(own, dim), (blocks,), jnp.float32, low / len(cuts), high / len(cuts)))
        factor_of = factor_of * jnp.repeat(steps, dims[dim] // blocks).reshape([-1 if axis == dim else 1 for axis in range(len(dims))])
    return factor_of


def assign_block(own_key, own, number, rows, count, top, limit, skew):
    ranking = jax.random.permutation(own_key, count)
    crowded, ordinary = portions_of(count, rows * top, limit, skew, True), portions_of(count, rows * top, limit, skew, False)
    places = jnp.arange(count)

    def named(sizes, offset_by):
        used = int((sizes > 0).sum())
        fixed = max(1, used // 4)
        moved = fixed + (places - fixed + offset_by * (used - fixed)) % max(1, count - fixed)
        return jnp.zeros((count,), jnp.int32).at[ranking[jnp.where(places < fixed, places, moved)]].set(jnp.asarray(sizes, jnp.int32))

    sizes = jnp.where(number % 4 == 0, named(crowded, number // 4), named(ordinary, number - number // 4 - 1))
    mixed = jax.random.permutation(jax.random.fold_in(own, 3), count)
    source_of, sink = mixed[0:count // 2 * 2:2], mixed[1:count // 2 * 2:2]
    slack = jnp.minimum(sizes[source_of] - 1, limit - sizes[sink]) // 2
    slack = jnp.where((source_of == ranking[0]) | (sink == ranking[0]) | (sizes[sink] == 0), 0, jnp.maximum(slack, 0))
    moved = jax.random.randint(jax.random.fold_in(own, 4), (count // 2,), 0, 1 << 20) % (slack + 1)
    sizes = sizes.at[source_of].add(-moved).at[sink].add(moved)
    members = jnp.searchsorted(jnp.cumsum(sizes), jnp.arange(rows * top), side="right").astype(jnp.int32)
    table = members.reshape(top, rows).T
    table = table[jax.random.permutation(jax.random.fold_in(own, 1), rows)]
    offset_by = jax.random.randint(jax.random.fold_in(own, 2), (rows, 1), 0, top)
    return jnp.take_along_axis(table, (jnp.arange(top)[None, :] + offset_by) % top, axis=1)


def portions_of(amount, total, most, slope, full):
    loads = [(1 << 20) // math.isqrt(grade ** slope) + 1 for grade in range(1, amount + 1)]
    largest = most if full else min(most, max(-(-total // amount), total * loads[0] // sum(loads)))
    least = 1 if total - largest >= amount - 1 else 0
    holding, surplus = [largest] + [least] * (amount - 1), total - largest - least * (amount - 1)
    while surplus > 0:
        movable = [i for i in range(1, amount) if holding[i] < largest] or [i for i in range(1, amount) if holding[i] < most]
        mass, left = sum([loads[i] for i in movable]), surplus
        for i in movable:
            extra = min(most - holding[i], max(1, left * loads[i] // mass), surplus)
            holding[i] = holding[i] + extra
            surplus = surplus - extra
    return np.array(holding)


def bell_draw(key, shape, spread, bound, split=(), kind=jnp.bfloat16):
    gain = block_levels(key, shape, split, -0.22, 0.18) if split else 1.0
    entries = jax.random.normal(key, shape, jnp.float32) * spread * gain
    return jnp.minimum(jnp.maximum(entries, -bound), bound).astype(kind)


def setup_inputs(seed: int = 0) -> dict:
    splits = jax.random.split(jax.random.key(seed), 14)
    resid = bell_draw(splits[0], (ROWS, D), 1.0, 6.0, ((0, 128),))
    query = draw_query(jax.random.fold_in(splits[13], 71), 0)
    key_cache = draw_key_cache(jax.random.fold_in(splits[13], 71), 0)
    value_cache = bell_draw(splits[3], (ROWS, CACHE_LEN, KV_HEADS * HEAD_DIM), 1.0, 6.0, ((0, 128),))
    new_key = bell_draw(splits[4], (ROWS, KV_HEADS * HEAD_DIM), 1.0, 5.0, ((0, 128),))
    new_value = bell_draw(splits[5], (ROWS, KV_HEADS * HEAD_DIM), 1.0, 5.0, ((0, 128),))
    cache_len = draw_cache_len(jax.random.fold_in(splits[13], 71), 0)
    norm_gain = jnp.clip(1.0 + 0.18 * jax.random.normal(splits[7], (D,), jnp.float32), 0.1, 1.9)
    routes_keys = jax.random.split(jax.random.fold_in(splits[8], 1), ROWS // ROWS_DEV)
    routes_turns = jax.random.permutation(jax.random.fold_in(splits[8], 3), ROWS // ROWS_DEV)
    routes = jax.vmap(lambda own, number: assign_block(jax.random.fold_in(splits[8], 2), own, number, ROWS_DEV, EXPERTS, TOP, CAP_DEV, 2))(routes_keys, routes_turns).reshape((ROWS, TOP))
    gate_fixed = with_ends(jax.random.randint(splits[9], (ROWS, TOP), 1, 4096), jax.random.fold_in(splits[9], 1), 1, 4095).astype(jnp.int32)
    w_gate = bell_draw(splits[10], (EXPERTS, FFW, D), D ** -0.5, 0.078125, ((0, 16), (1, 8)))
    w_up = bell_draw(splits[11], (EXPERTS, FFW, D), D ** -0.5, 0.078125, ((0, 16), (1, 8)))
    w_down = bell_draw(splits[12], (EXPERTS, FFW, D), FFW ** -0.5, 0.078125, ((0, 16), (1, 8)))
    return {"resid": resid, "query": query, "key_cache": key_cache, "value_cache": value_cache, "new_key": new_key, "new_value": new_value, "cache_len": cache_len, "norm_gain": norm_gain, "routes": routes, "gate_fixed": gate_fixed, "w_gate": w_gate, "w_up": w_up, "w_down": w_down}


def attend(resid, query, key_cache, value_cache, new_key, new_value, cache_len):
    group = HEADS // KV_HEADS
    scale = 1.0 / HEAD_DIM ** 0.5
    q = query.astype(jnp.float32).reshape(ROWS, KV_HEADS, group, HEAD_DIM)
    keys = key_cache.astype(jnp.float32).reshape(ROWS, CACHE_LEN, KV_HEADS, HEAD_DIM)
    values = value_cache.astype(jnp.float32).reshape(ROWS, CACHE_LEN, KV_HEADS, HEAD_DIM)
    knew = new_key.astype(jnp.float32).reshape(ROWS, KV_HEADS, HEAD_DIM)
    vnew = new_value.astype(jnp.float32).reshape(ROWS, KV_HEADS, HEAD_DIM)
    scores = jnp.einsum('rkgd,rpkd->rkgp', q, keys) * scale
    own = jnp.einsum('rkgd,rkd->rkg', q, knew) * scale
    valid = jnp.arange(CACHE_LEN, dtype=jnp.int32)[None, :] < cache_len[:, None]
    scores = jnp.where(valid[:, None, None, :], scores, -1e+30)
    top = jnp.maximum(lax.optimization_barrier(jnp.max(scores, axis=-1)), own)
    expo = jnp.exp(scores - top[..., None])
    expo_own = jnp.exp(own - top)
    total = lax.optimization_barrier(jnp.sum(expo, axis=-1)) + expo_own
    probs = lax.optimization_barrier((expo / total[..., None]).astype(jnp.bfloat16)).astype(jnp.float32)
    prob_own = lax.optimization_barrier((expo_own / total).astype(jnp.bfloat16)).astype(jnp.float32)
    attn = jnp.einsum('rkgp,rpkd->rkgd', probs, values) + prob_own[..., None] * vnew[:, :, None, :]
    return resid.astype(jnp.float32) + attn.reshape(ROWS, D)

def normalize(stream, norm_gain):
    mean = lax.optimization_barrier(jnp.mean(stream, axis=-1, keepdims=True))
    centred = stream - mean
    variance = lax.optimization_barrier(jnp.mean(centred * centred, axis=-1, keepdims=True))
    return (centred * lax.rsqrt(variance + 1e-05) * norm_gain).astype(jnp.bfloat16)

def reference(resid, query, key_cache, value_cache, new_key, new_value, cache_len, norm_gain, routes, gate_fixed, w_gate, w_up, w_down):
    stream = attend(resid, query, key_cache, value_cache, new_key, new_value, cache_len)
    moe_in = normalize(stream, norm_gain)
    fixed = gate_fixed.astype(jnp.float32)
    weights = fixed / lax.optimization_barrier(jnp.sum(fixed, axis=-1, keepdims=True))
    load = ROWS // ROWS_DEV * CAP_DEV
    positions = jnp.arange(ROWS, dtype=jnp.int32)

    def expert_step(carry, inputs):
        number, gate_mat, up_mat, down_mat = inputs
        chosen = routes == number
        share = lax.optimization_barrier(jnp.sum(jnp.where(chosen, weights, 0.0), axis=-1))
        score = jnp.where(jnp.any(chosen, axis=-1), ROWS - positions, 0).astype(jnp.int32)
        picked = lax.top_k(score, load)[1].astype(jnp.int32)
        rows = moe_in[picked]
        gate = jnp.dot(rows, gate_mat.T, preferred_element_type=jnp.float32)
        upper = jnp.dot(rows, up_mat.T, preferred_element_type=jnp.float32)
        hidden = (jax.nn.silu(gate) * upper).astype(jnp.bfloat16)
        output = jnp.dot(hidden, down_mat, preferred_element_type=jnp.float32)
        carry = carry.at[picked].add(output * share[picked][:, None])
        return (carry, None)
    start = jnp.zeros((ROWS, D), jnp.float32)
    numbers = jnp.arange(EXPERTS, dtype=jnp.int32)
    moe, unused = lax.scan(expert_step, start, (numbers, w_gate, w_up, w_down))
    return (stream + moe).astype(jnp.bfloat16)
```

```python
import functools

import jax
import jax.numpy as jnp
from jax import lax
from jax.experimental import pallas as pl
from jax.experimental.pallas import tpu as pltpu
from jax.sharding import PartitionSpec as P

D = 6144
HEADS = 48
KV_HEADS = 8
HEAD_DIM = 128
GROUP = HEADS // KV_HEADS
ROWS = 4
LENGTH = 128
HIDDEN = 672
CHUNK = 1024
A_CHUNKS = 4
A_COLS = A_CHUNKS * CHUNK
F32 = jnp.float32
BF16 = jnp.bfloat16
MESH = pl.DeviceIdType.MESH
W_PARTS = 3
W_ROWS = HIDDEN // W_PARTS


def iota(shape, dim):
    return lax.broadcasted_iota(jnp.int32, shape, dim)


def dot(a, b):
    return lax.dot_general(a, b, (((1,), (0,)), ((), ())), preferred_element_type=F32)


def dot_nt(a, b):
    return lax.dot_general(a, b, (((1,), (1,)), ((), ())), preferred_element_type=F32)


def onehot(condition):
    return jnp.where(condition, 1.0, 0.0).astype(BF16)


def remote(src, dst, send_sem, recv_sem, device):
    return pltpu.make_async_remote_copy(
        src_ref=src,
        dst_ref=dst,
        send_sem=send_sem,
        recv_sem=recv_sem,
        device_id=device,
        device_id_type=MESH,
    )


def kernel(
    clen,
    resid,
    query,
    new_key,
    new_value,
    gain,
    routes,
    gates,
    key_hbm,
    value_hbm,
    wg_hbm,
    wu_hbm,
    wd_hbm,
    out,
    kbuf,
    vbuf,
    wg,
    wu,
    wd,
    qs,
    scores,
    own_key,
    own_value,
    heads_out,
    stream,
    xs,
    apack,
    arecv,
    bmsg,
    xb1,
    bpack,
    xbh,
    xa,
    accg,
    accu,
    hid,
    hidb,
    pa,
    pm,
    cr,
    cs,
    far,
    near,
    y2,
    asend,
    aback,
    pbs,
    pbm,
    cbr,
    bsend,
    bback,
    fsend,
    frecv,
    local_sem,
    a1s,
    a1r,
    b1s,
    b1r,
    b2s,
    b2r,
    bcs,
    bcr,
    ns,
    nr,
    fs,
    fr,
    acs,
    acr,
    rcs,
    rcr,
    rfs,
    rfr,
    rns,
    rnr,
    ras,
    rar,
    rbcs,
    rbcr,
    rbs,
    rbr,
    rfis,
    rfir,
):
    side = lax.axis_index("side")
    expert = lax.axis_index("expert")
    tp = lax.axis_index("tp")
    me = side * 8 + expert
    my_y = me // 4
    my_z = me % 4
    x = tp // 2
    core = tp % 2
    right = lax.rem(x + 1, 4)
    left = lax.rem(x + 3, 4)
    opposite = lax.rem(x + 2, 4)
    other_dev = (side, expert, x * 2 + 1 - core)
    right_dev = (side, expert, right * 2 + core)
    left_dev = (side, expert, left * 2 + core)

    def plane(step):
        y = lax.rem(my_y + step // 4, 4)
        z = lax.rem(my_z + step % 4, 4)
        peer = y * 4 + z
        return peer, (peer // 8, peer % 8, tp)

    def column(step):
        peer = lax.rem(tp + step, 8)
        return peer, (side, expert, peer)

    barrier = pltpu.get_barrier_semaphore()

    def greet_plane(step, carry):
        pl.semaphore_signal(barrier, inc=1, device_id=plane(step)[1], device_id_type=MESH)
        return carry

    def greet_column(step, carry):
        pl.semaphore_signal(barrier, inc=1, device_id=column(step)[1], device_id_type=MESH)
        return carry

    key_copy = pltpu.make_async_copy(key_hbm, kbuf, local_sem.at[0])
    value_copy = pltpu.make_async_copy(value_hbm, vbuf, local_sem.at[1])
    key_copy.start()
    value_copy.start()
    weight_copies = []
    for number, (src, dst) in enumerate(((wg_hbm, wg), (wu_hbm, wu), (wd_hbm, wd))):
        for part in range(W_PARTS):
            rows = pl.ds(part * W_ROWS, W_ROWS)
            weight_copies.append(
                pltpu.make_async_copy(
                    src.at[0, rows, :],
                    dst.at[rows, :],
                    local_sem.at[2 + number * W_PARTS + part],
                )
            )
    for copy in weight_copies:
        copy.start()
    lax.fori_loop(1, 16, greet_plane, 0)
    lax.fori_loop(1, 8, greet_column, 0)

    q32 = query[...].astype(F32)
    for head in range(HEADS):
        qs[head * 4 : head * 4 + 4, :] = q32[:, head * 128 : head * 128 + 128]
    nk32 = new_key[...].astype(F32)
    nv32 = new_value[...].astype(F32)
    for copy_no in range(GROUP):
        own_key[copy_no * 4 : copy_no * 4 + 4, :] = nk32
        own_value[copy_no * 4 : copy_no * 4 + 4, :] = nv32
    block = GROUP * ROWS
    row_of = iota((block, 128), 0) & 3
    key_copy.wait()
    for j in range(KV_HEADS):
        qj = qs[j * block : (j + 1) * block, :].astype(BF16)
        total = jnp.zeros((block, 128), F32)
        for r in range(ROWS):
            part = dot_nt(qj, kbuf[r, :, j * 128 : (j + 1) * 128])
            total = jnp.where(row_of == r, part, total)
        scores[j * block : (j + 1) * block, :] = total

    lane32 = iota((32, 32), 1)
    row32 = iota((32, 32), 0)
    fixed = gates[...].astype(F32)
    weights = fixed / jnp.sum(fixed, axis=-1, keepdims=True)
    chosen = jnp.zeros((32, 32), F32)
    weighted = jnp.zeros((32, 32), F32)
    route = routes[...]
    for k in range(4):
        same = route[:, k : k + 1] == (lane32 >> 1)
        chosen = chosen + jnp.where(same, 1.0, 0.0)
        weighted = weighted + jnp.where(same, weights[:, k : k + 1], 0.0)
    earlier = onehot(((row32 >> 2) == (lane32 >> 2)) & (lane32 < row32))
    before = dot(earlier, chosen.astype(BF16))
    picked = (chosen > 0.5) & (jnp.abs(before - (lane32 & 1).astype(F32)) < 0.5)
    sel = onehot(picked)
    wsel = jnp.where(picked, weighted, 0.0)
    whi = wsel.astype(BF16)
    wlo = (wsel - whi.astype(F32)).astype(BF16)

    rr = iota((256, 32), 0)
    ll = iota((256, 32), 1)
    spread_a = onehot((rr >> 3) == ll)
    spread_b = onehot(ll == ((rr >> 4) * 2 + (rr & 1)))
    rr = iota((96, 32), 0)
    ll = iota((96, 32), 1)
    mine = onehot((ll == tp * 4 + (rr & 7)) & ((rr & 7) < 4))
    rr = iota((128, 32), 0)
    ll = iota((128, 32), 1)
    wide = onehot(ll == ((rr >> 4) * 4 + (rr & 3)))
    pack_a = dot_nt(spread_a, dot(mine, sel).astype(BF16))
    rr = iota((256, 96), 0)
    ll = iota((256, 96), 1)
    pack_a = jnp.where((rr & 7) == (ll >> 3), pack_a, 0.0).astype(BF16)
    rr = iota((16, 96), 0)
    ll = iota((16, 96), 1)
    pack_b1 = onehot(ll == (8 + (rr >> 2)) * 8 + (rr & 3))
    pack_b = dot_nt(spread_b, dot(wide, sel).astype(BF16))
    rr = iota((256, 128), 0)
    ll = iota((256, 128), 1)
    pack_b = jnp.where(((rr & 15) >> 1) == (ll >> 4), pack_b, 0.0)

    pos = iota((HEADS * ROWS, 128), 1)
    row_all = iota((HEADS * ROWS, 128), 0) & 3
    limit = jnp.zeros((HEADS * ROWS, 128), jnp.int32)
    for r in range(ROWS):
        limit = jnp.where(row_all == r, clen[r], limit)
    scale = 1.0 / HEAD_DIM**0.5
    s = jnp.where(pos < limit, scores[...] * scale, -1e30)
    own = jnp.concatenate(
        [
            jnp.sum(
                qs[j * block : (j + 1) * block, :] * own_key[:, j * 128 : (j + 1) * 128],
                axis=-1,
                keepdims=True,
            )
            for j in range(KV_HEADS)
        ],
        axis=0,
    )
    own = own * scale
    top = jnp.maximum(jnp.max(s, axis=-1, keepdims=True), own)
    expo = jnp.exp(s - top)
    expo_own = jnp.exp(own - top)
    total = jnp.sum(expo, axis=-1, keepdims=True) + expo_own
    scores[...] = expo / total
    prob_own = (expo_own / total).astype(BF16).astype(F32)
    value_copy.wait()
    for j in range(KV_HEADS):
        pj = scores[j * block : (j + 1) * block, :]
        acc = prob_own[j * block : (j + 1) * block, :] * own_value[:, j * 128 : (j + 1) * 128]
        for r in range(ROWS):
            pr = jnp.where(row_of == r, pj, 0.0).astype(BF16)
            acc = acc + dot(pr, vbuf[r, :, j * 128 : (j + 1) * 128])
        heads_out[j * block : (j + 1) * block, :] = acc
    stream[...] = jnp.zeros((8, D), F32)
    for head in range(HEADS):
        cols = slice(head * 128, head * 128 + 128)
        stream[0:4, cols] = resid[:, cols].astype(F32) + heads_out[head * 4 : head * 4 + 4, :]
    st = stream[...]
    mean = jnp.sum(st, axis=-1, keepdims=True) * (1.0 / D)
    centred = st - mean
    variance = jnp.sum(centred * centred, axis=-1, keepdims=True) * (1.0 / D)
    normed = centred * lax.rsqrt(variance + 1e-05) * gain[...]
    for p in range(12):
        xs[p * 8 : p * 8 + 8, :] = normed[:, p * 512 : (p + 1) * 512]
    xbf = xs[...].astype(BF16)

    bm = dot(pack_b1, xbf).astype(BF16)
    bmsg[...] = bm
    xb1[tp] = bm
    pl.semaphore_wait(barrier, 22)

    def send_b1(step, carry):
        peer, device = column(step)
        remote(bmsg, xb1.at[tp], b1s.at[step], b1r.at[tp], device).start()
        return carry

    lax.fori_loop(1, 8, send_b1, 0)
    packed = dot(pack_a, xbf).astype(BF16)
    apack[...] = packed.reshape(16, 16, 512)
    arecv[me] = apack[me]

    def send_a1(step, carry):
        peer, device = plane(step)
        remote(apack.at[peer], arecv.at[me], a1s.at[step], a1r.at[me], device).start()
        return carry

    lax.fori_loop(1, 16, send_a1, 0)

    def wait_b1(step, carry):
        peer, device = column(step)
        remote(bmsg, xb1.at[peer], b1s.at[step], b1r.at[peer], device).wait_recv()
        return carry

    lax.fori_loop(1, 8, wait_b1, 0)
    xb_all = xb1[...].reshape(128, 512)
    for i in range(2):
        pick = jnp.where(((ll & 15) >> 2) == core * 2 + i, pack_b, 0.0).astype(BF16)
        bpack[:, :, i * 512 : (i + 1) * 512] = (
            dot(pick, xb_all).astype(BF16).reshape(16, 16, 512)
        )
    xbh[core, me] = bpack[me]

    def send_b2(step, carry):
        peer, device = plane(step)
        remote(bpack.at[peer], xbh.at[core, me], b2s.at[step], b2r.at[me], device).start()
        return carry

    lax.fori_loop(1, 16, send_b2, 0)

    def wait_a1(step, carry):
        peer, device = plane(step)
        remote(apack.at[peer], arecv.at[peer], a1s.at[step], a1r.at[peer], device).wait_recv()
        return carry

    lax.fori_loop(1, 16, wait_a1, 0)
    rr = iota((256, 256), 0)
    ll = iota((256, 256), 1)
    unpack_a = onehot(ll == (rr & 31) * 8 + (rr >> 5))
    got = dot(unpack_a, arecv[...].reshape(256, 512)).astype(BF16)
    for p in range(8):
        xa[p // 2, core, x, :, (p % 2) * 512 : (p % 2) * 512 + 512] = got[p * 32 : p * 32 + 32, :]

    def near_in(n):
        mine_ref = xa.at[n, core, x]
        to_right = remote(mine_ref, mine_ref, ns.at[0, n], nr.at[0, n], right_dev)
        to_left = remote(mine_ref, mine_ref, ns.at[1, n], nr.at[1, n], left_dev)
        return to_right, to_left

    def near_arrivals(n):
        from_left = xa.at[n, core, left]
        from_right = xa.at[n, core, right]
        a = remote(from_left, from_left, ns.at[0, n], nr.at[0, n], right_dev)
        b = remote(from_right, from_right, ns.at[1, n], nr.at[1, n], left_dev)
        return a, b

    def far_sends(n):
        low = xa.at[n, core, left, pl.ds(0, 16), :]
        high = xa.at[n, core, right, pl.ds(16, 16), :]
        a = remote(low, low, fs.at[0, n], fr.at[0, n], right_dev)
        b = remote(high, high, fs.at[1, n], fr.at[1, n], left_dev)
        return a, b

    def far_arrivals(n):
        low = xa.at[n, core, opposite, pl.ds(0, 16), :]
        high = xa.at[n, core, opposite, pl.ds(16, 16), :]
        a = remote(low, low, fs.at[0, n], fr.at[0, n], right_dev)
        b = remote(high, high, fs.at[1, n], fr.at[1, n], left_dev)
        return a, b

    def core_send(n):
        half = xa.at[n, core]
        return remote(half, half, acs.at[n], acr.at[n], other_dev)

    def core_arrival(n):
        half = xa.at[n, 1 - core]
        return remote(half, half, acs.at[n], acr.at[n], other_dev)

    for n in range(A_CHUNKS):
        for copy in near_in(n):
            copy.start()

    accg[...] = jnp.zeros((256, HIDDEN), F32)
    accu[...] = jnp.zeros((256, HIDDEN), F32)
    for copy in weight_copies[: 2 * W_PARTS]:
        copy.wait()

    def project(value, offset):
        cols = pl.ds(offset, CHUNK)
        accg[...] += dot_nt(value, wg[:, cols])
        accu[...] += dot_nt(value, wu[:, cols])

    def project_a(n):
        core_arrival(n).wait_recv()
        project(xa[n].reshape(256, CHUNK), n * CHUNK)

    def relay(n):
        for copy in near_arrivals(n):
            copy.wait_recv()
        for copy in far_sends(n):
            copy.start()

    def forward(n):
        for copy in far_arrivals(n):
            copy.wait_recv()
        core_send(n).start()

    relay(0)
    relay(1)
    forward(0)
    relay(2)
    forward(1)
    project_a(0)

    def wait_b2(step, carry):
        peer, device = plane(step)
        remote(
            bpack.at[peer], xbh.at[core, peer], b2s.at[step], b2r.at[peer], device
        ).wait_recv()
        return carry

    lax.fori_loop(1, 16, wait_b2, 0)
    bcore = remote(xbh.at[core], xbh.at[core], bcs, bcr, other_dev)
    bcore.start()
    relay(3)
    forward(2)
    project_a(1)
    forward(3)
    remote(xbh.at[1 - core], xbh.at[1 - core], bcs, bcr, other_dev).wait_recv()
    tau = rr >> 5
    unpack_b = onehot(
        ll == ((rr & 31) >> 1) * 16 + ((tau & 3) * 2 + (tau >> 2)) * 2 + (rr & 1)
    )
    for h in range(2):
        project(
            dot(unpack_b, xbh[h].reshape(256, CHUNK)).astype(BF16), A_COLS + h * CHUNK
        )
    project_a(2)
    project_a(3)
    g = accg[...]
    hidden = (g * jax.nn.sigmoid(g) * accu[...]).astype(BF16)
    hid[...] = hidden
    t_of = (rr & 15) >> 1
    to_b = onehot(ll == ((t_of & 1) * 4 + (t_of >> 1)) * 32 + (rr >> 4) * 2 + (rr & 1))
    hidb[...] = dot(to_b, hidden).astype(BF16)
    for copy in weight_copies[2 * W_PARTS :]:
        copy.wait()

    def down_a(n):
        y = dot(hid[...], wd[:, n * CHUNK : (n + 1) * CHUNK])
        pa[n] = y.astype(BF16).reshape(2, 128, CHUNK)
        pm[n] = jnp.where(core == 0, y[:128], y[128:])
        remote(pa.at[n, 1 - core], cr.at[n], rcs.at[n], rcr.at[n], other_dev).start()

    def chip_sum(n):
        remote(pa.at[n, 1 - core], cr.at[n], rcs.at[n], rcr.at[n], other_dev).wait_recv()
        both = pm[n] + cr[n].astype(F32)
        pm[n] = both
        cs[n] = both.astype(BF16).reshape(4, 32, CHUNK)
        for copy in ret_far(n):
            copy.start()

    def ret_far(n):
        a = remote(
            cs.at[n, opposite, pl.ds(0, 16), :], far.at[0, n], rfs.at[0, n], rfr.at[0, n], right_dev
        )
        b = remote(
            cs.at[n, opposite, pl.ds(16, 16), :], far.at[1, n], rfs.at[1, n], rfr.at[1, n], left_dev
        )
        return a, b

    def ret_near(n):
        a = remote(cs.at[n, right], near.at[0, n], rns.at[0, n], rnr.at[0, n], right_dev)
        b = remote(cs.at[n, left], near.at[1, n], rns.at[1, n], rnr.at[1, n], left_dev)
        return a, b

    def ret_relay(n):
        for copy in ret_far(n):
            copy.wait_recv()
        to_right = pl.ds(pl.multiple_of(right * 32, 32), 16)
        to_left = pl.ds(pl.multiple_of(left * 32 + 16, 16), 16)
        cs[n, right, 0:16, :] = (pm[n, to_right, :] + far[0, n].astype(F32)).astype(BF16)
        cs[n, left, 16:32, :] = (pm[n, to_left, :] + far[1, n].astype(F32)).astype(BF16)
        for copy in ret_near(n):
            copy.start()

    def ret_sum(n):
        for copy in ret_near(n):
            copy.wait_recv()
        rows = pl.ds(pl.multiple_of(x * 32, 32), 32)
        y = pm[n, rows, :] + near[0, n].astype(F32) + near[1, n].astype(F32)
        y = y.astype(BF16)
        for p in range(2):
            y2[(n * 2 + p) * 32 : (n * 2 + p) * 32 + 32, :] = y[:, p * 512 : p * 512 + 512]

    def b_core():
        return remote(pbs, cbr, rbcs, rbcr, other_dev)

    down_a(0)
    b0 = dot(hidb[...], wd[:, A_COLS : A_COLS + CHUNK])
    b1 = dot(hidb[...], wd[:, A_COLS + CHUNK : A_COLS + 2 * CHUNK])
    pbs[...] = jnp.where(core == 0, b1, b0).astype(BF16)
    pbm[...] = jnp.where(core == 0, b0, b1)
    b_core().start()
    chip_sum(0)
    down_a(1)
    b_core().wait_recv()
    bsend[...] = (pbm[...] + cbr[...].astype(F32)).astype(BF16).reshape(16, 16, CHUNK)
    bback[me] = bsend[me]

    def send_b3(step, carry):
        peer, device = plane(step)
        remote(bsend.at[peer], bback.at[me], rbs.at[step], rbr.at[me], device).start()
        return carry

    lax.fori_loop(1, 16, send_b3, 0)
    ret_relay(0)
    chip_sum(1)
    down_a(2)
    ret_relay(1)
    chip_sum(2)
    down_a(3)
    ret_sum(0)
    ret_relay(2)
    chip_sum(3)
    ret_sum(1)
    ret_relay(3)

    rr = iota((128, 256), 0)
    ll = iota((128, 256), 1)
    wide_hi = dot_nt(dot(wide, whi).astype(BF16), spread_b)
    wide_lo = dot_nt(dot(wide, wlo).astype(BF16), spread_b)

    def wait_b3(step, carry):
        peer, device = plane(step)
        remote(bsend.at[peer], bback.at[peer], rbs.at[step], rbr.at[peer], device).wait_recv()
        return carry

    lax.fori_loop(1, 16, wait_b3, 0)
    partial = jnp.zeros((128, 256), F32)
    for q in range(4):
        keep = ((rr >> 4) == ((ll & 15) >> 1)) & (((rr & 15) >> 2) == q)
        piece = bback[:, :, q * 256 : q * 256 + 256].reshape(256, 256)
        partial = partial + dot(jnp.where(keep, wide_hi, 0.0).astype(BF16), piece)
        partial = partial + dot(jnp.where(keep, wide_lo, 0.0).astype(BF16), piece)
    fsend[...] = partial.astype(BF16).reshape(8, 16, 256)
    frecv[tp] = fsend[tp]

    def send_b4(step, carry):
        peer, device = column(step)
        remote(fsend.at[peer], frecv.at[tp], rfis.at[step], rfir.at[tp], device).start()
        return carry

    lax.fori_loop(1, 8, send_b4, 0)
    ret_sum(2)
    ret_sum(3)
    rr = iota((256, 256), 0)
    ll = iota((256, 256), 1)
    repack_a = onehot(ll == (rr & 7) * 32 + (rr >> 3))
    asend[...] = dot(repack_a, y2[...]).astype(BF16).reshape(16, 16, 512)
    aback[me] = asend[me]

    def send_a2(step, carry):
        peer, device = plane(step)
        remote(asend.at[peer], aback.at[me], ras.at[step], rar.at[me], device).start()
        return carry

    lax.fori_loop(1, 16, send_a2, 0)

    def wait_b4(step, carry):
        peer, device = column(step)
        remote(fsend.at[peer], frecv.at[peer], rfis.at[step], rfir.at[peer], device).wait_recv()
        return carry

    lax.fori_loop(1, 8, wait_b4, 0)
    rr = iota((64, 128), 0)
    ll = iota((64, 128), 1)
    gather = onehot(
        ((rr >> 5) == ((ll >> 4) & 1))
        & (((rr >> 3) & 3) == ((ll & 15) >> 2))
        & ((rr & 7) == (ll & 3))
    )
    home_b = dot(gather, frecv[...].reshape(128, 256))
    for piece in range(8):
        start = A_COLS + piece * 256
        out[:, start : start + 256] = (
            stream[0:4, start : start + 256] + home_b[piece * 8 : piece * 8 + 4, :]
        ).astype(BF16)

    rr = iota((64, 256), 0)
    ll = iota((64, 256), 1)
    keep = (rr >> 3) == (ll & 7)
    home_hi = dot_nt(dot(mine[0:64], whi).astype(BF16), spread_a)
    home_lo = dot_nt(dot(mine[0:64], wlo).astype(BF16), spread_a)
    home_hi = jnp.where(keep, home_hi, 0.0).astype(BF16)
    home_lo = jnp.where(keep, home_lo, 0.0).astype(BF16)

    def wait_a2(step, carry):
        peer, device = plane(step)
        remote(asend.at[peer], aback.at[peer], ras.at[step], rar.at[peer], device).wait_recv()
        return carry

    lax.fori_loop(1, 16, wait_a2, 0)
    back = aback[...].reshape(256, 512)
    home_a = dot(home_hi, back) + dot(home_lo, back)
    for p in range(8):
        cols = slice(p * 512, p * 512 + 512)
        out[:, cols] = (stream[0:4, cols] + home_a[p * 8 : p * 8 + 4, :]).astype(BF16)

    def drain_plane(step, carry):
        peer, device = plane(step)
        remote(apack.at[peer], arecv.at[me], a1s.at[step], a1r.at[me], device).wait_send()
        remote(bpack.at[peer], xbh.at[core, me], b2s.at[step], b2r.at[me], device).wait_send()
        remote(bsend.at[peer], bback.at[me], rbs.at[step], rbr.at[me], device).wait_send()
        remote(asend.at[peer], aback.at[me], ras.at[step], rar.at[me], device).wait_send()
        return carry

    lax.fori_loop(1, 16, drain_plane, 0)

    def drain_column(step, carry):
        peer, device = column(step)
        remote(bmsg, xb1.at[tp], b1s.at[step], b1r.at[tp], device).wait_send()
        remote(fsend.at[peer], frecv.at[tp], rfis.at[step], rfir.at[tp], device).wait_send()
        return carry

    lax.fori_loop(1, 8, drain_column, 0)
    bcore.wait_send()
    b_core().wait_send()
    for n in range(A_CHUNKS):
        for copy in (*near_in(n), *far_sends(n), *ret_far(n), *ret_near(n), core_send(n)):
            copy.wait_send()
        remote(pa.at[n, 1 - core], cr.at[n], rcs.at[n], rcr.at[n], other_dev).wait_send()


def layer(
    resid,
    query,
    key_cache,
    value_cache,
    new_key,
    new_value,
    cache_len,
    norm_gain,
    routes,
    gate_fixed,
    w_gate,
    w_up,
    w_down,
):
    vmem = pl.BlockSpec(memory_space=pltpu.VMEM)
    anywhere = pl.BlockSpec(memory_space=pl.ANY)
    dma = pltpu.SemaphoreType.DMA
    n = A_CHUNKS
    scratch = [
        pltpu.VMEM((ROWS, LENGTH, 1024), BF16),
        pltpu.VMEM((ROWS, LENGTH, 1024), BF16),
        pltpu.VMEM((HIDDEN, D), BF16),
        pltpu.VMEM((HIDDEN, D), BF16),
        pltpu.VMEM((HIDDEN, D), BF16),
        pltpu.VMEM((HEADS * ROWS, 128), F32),
        pltpu.VMEM((HEADS * ROWS, 128), F32),
        pltpu.VMEM((GROUP * ROWS, 1024), F32),
        pltpu.VMEM((GROUP * ROWS, 1024), F32),
        pltpu.VMEM((HEADS * ROWS, 128), F32),
        pltpu.VMEM((8, D), F32),
        pltpu.VMEM((96, 512), F32),
        pltpu.VMEM((16, 16, 512), BF16),
        pltpu.VMEM((16, 16, 512), BF16),
        pltpu.VMEM((16, 512), BF16),
        pltpu.VMEM((8, 16, 512), BF16),
        pltpu.VMEM((16, 16, CHUNK), BF16),
        pltpu.VMEM((2, 16, 16, CHUNK), BF16),
        pltpu.VMEM((n, 2, 4, 32, CHUNK), BF16),
        pltpu.VMEM((256, HIDDEN), F32),
        pltpu.VMEM((256, HIDDEN), F32),
        pltpu.VMEM((256, HIDDEN), BF16),
        pltpu.VMEM((256, HIDDEN), BF16),
        pltpu.VMEM((n, 2, 128, CHUNK), BF16),
        pltpu.VMEM((n, 128, CHUNK), F32),
        pltpu.VMEM((n, 128, CHUNK), BF16),
        pltpu.VMEM((n, 4, 32, CHUNK), BF16),
        pltpu.VMEM((2, n, 16, CHUNK), BF16),
        pltpu.VMEM((2, n, 32, CHUNK), BF16),
        pltpu.VMEM((256, 512), BF16),
        pltpu.VMEM((16, 16, 512), BF16),
        pltpu.VMEM((16, 16, 512), BF16),
        pltpu.VMEM((256, CHUNK), BF16),
        pltpu.VMEM((256, CHUNK), F32),
        pltpu.VMEM((256, CHUNK), BF16),
        pltpu.VMEM((16, 16, CHUNK), BF16),
        pltpu.VMEM((16, 16, CHUNK), BF16),
        pltpu.VMEM((8, 16, 256), BF16),
        pltpu.VMEM((8, 16, 256), BF16),
        dma((2 + 3 * W_PARTS,)),
        dma((16,)),
        dma((16,)),
        dma((8,)),
        dma((8,)),
        dma((16,)),
        dma((16,)),
        dma,
        dma,
        dma((2, n)),
        dma((2, n)),
        dma((2, n)),
        dma((2, n)),
        dma((n,)),
        dma((n,)),
        dma((n,)),
        dma((n,)),
        dma((2, n)),
        dma((2, n)),
        dma((2, n)),
        dma((2, n)),
        dma((16,)),
        dma((16,)),
        dma,
        dma,
        dma((16,)),
        dma((16,)),
        dma((8,)),
        dma((8,)),
    ]
    return pl.pallas_call(
        kernel,
        out_shape=jax.ShapeDtypeStruct((ROWS, D), BF16),
        in_specs=[pl.BlockSpec(memory_space=pltpu.SMEM)] + [vmem] * 7 + [anywhere] * 5,
        out_specs=vmem,
        scratch_shapes=scratch,
        compiler_params=pltpu.CompilerParams(
            collective_id=0, has_side_effects=True, vmem_limit_bytes=60 * 1024 * 1024
        ),
        cost_estimate=pl.CostEstimate(
            flops=2 * 3 * 256 * HIDDEN * D, bytes_accessed=27 * 1024 * 1024, transcendentals=0
        ),
    )(
        cache_len,
        resid,
        query,
        new_key,
        new_value,
        norm_gain.reshape(1, D),
        routes,
        gate_fixed,
        key_cache,
        value_cache,
        w_gate,
        w_up,
        w_down,
    )


def solution(mesh):
    placed = (
        P(("side", "expert", "tp"), None),
        P(("side", "expert", "tp"), None),
        P(("side", "expert", "tp"), None, None),
        P(("side", "expert", "tp"), None, None),
        P(("side", "expert", "tp"), None),
        P(("side", "expert", "tp"), None),
        P(("side", "expert", "tp")),
        P(),
        P(("side", "expert"), None),
        P(("side", "expert"), None),
        P(("side", "expert"), "tp", None),
        P(("side", "expert"), "tp", None),
        P(("side", "expert"), "tp", None),
    )
    return jax.shard_map(
        layer,
        mesh=mesh,
        in_specs=placed,
        out_specs=P(("side", "expert", "tp"), None),
        check_vma=False,
    )
```

```python
import functools

import jax
import jax.numpy as jnp
from jax import lax
from jax.experimental import pallas as pl
from jax.experimental.pallas import tpu as pltpu
from jax.sharding import PartitionSpec as P

D = 6144
HEADS = 48
KV_HEADS = 8
HEAD_DIM = 128
GROUP = HEADS // KV_HEADS
ROWS = 4
LENGTH = 128
HIDDEN = 672
CHUNK = 1024
A_CHUNKS = 4
A_COLS = A_CHUNKS * CHUNK
F32 = jnp.float32
BF16 = jnp.bfloat16
MESH = pl.DeviceIdType.MESH
W_PARTS = 3
W_ROWS = HIDDEN // W_PARTS
PLANE = ((1, 0), (0, 1), (3, 0), (0, 3), (1, 1), (3, 3), (1, 3), (3, 1), (2, 0), (0, 2), (2, 1), (1, 2), (2, 3), (3, 2), (2, 2))


def iota(shape, dim):
    return lax.broadcasted_iota(jnp.int32, shape, dim)


def dot(a, b):
    return lax.dot_general(a, b, (((1,), (0,)), ((), ())), preferred_element_type=F32)


def dot_nt(a, b):
    return lax.dot_general(a, b, (((1,), (1,)), ((), ())), preferred_element_type=F32)


def onehot(condition):
    return jnp.where(condition, 1.0, 0.0).astype(BF16)


def remote(src, dst, send_sem, recv_sem, device):
    return pltpu.make_async_remote_copy(
        src_ref=src,
        dst_ref=dst,
        send_sem=send_sem,
        recv_sem=recv_sem,
        device_id=device,
        device_id_type=MESH,
    )


def kernel(
    clen,
    resid,
    query,
    new_key,
    new_value,
    gain,
    routes,
    gates,
    key_hbm,
    value_hbm,
    wg_hbm,
    wu_hbm,
    wd_hbm,
    out,
    kbuf,
    vbuf,
    wg,
    wu,
    wd,
    qs,
    scores,
    own_key,
    own_value,
    heads_out,
    stream,
    xs,
    apack,
    arecv,
    bmsg,
    xb1,
    bpack,
    xbh,
    xa,
    accg,
    accu,
    hid,
    hidb,
    pa,
    pm,
    cr,
    cs,
    far,
    near,
    y2,
    asend,
    aback,
    pbs,
    pbm,
    cbr,
    bsend,
    bback,
    fsend,
    frecv,
    local_sem,
    a1s,
    a1r,
    b1s,
    b1r,
    b2s,
    b2r,
    bcs,
    bcr,
    ns,
    nr,
    fs,
    fr,
    acs,
    acr,
    rcs,
    rcr,
    rfs,
    rfr,
    rns,
    rnr,
    ras,
    rar,
    rbcs,
    rbcr,
    rbs,
    rbr,
    rfis,
    rfir,
):
    side = lax.axis_index("side")
    expert = lax.axis_index("expert")
    tp = lax.axis_index("tp")
    me = side * 8 + expert
    my_y = me // 4
    my_z = me % 4
    x = tp // 2
    core = tp % 2
    right = lax.rem(x + 1, 4)
    left = lax.rem(x + 3, 4)
    opposite = lax.rem(x + 2, 4)
    other_dev = (side, expert, x * 2 + 1 - core)
    right_dev = (side, expert, right * 2 + core)
    left_dev = (side, expert, left * 2 + core)

    def plane(step):
        y = lax.rem(my_y + step // 4, 4)
        z = lax.rem(my_z + step % 4, 4)
        peer = y * 4 + z
        return peer, (peer // 8, peer % 8, tp)

    def column(step):
        peer = lax.rem(tp + step, 8)
        return peer, (side, expert, peer)

    def whole(buffer, count, send_sem, recv_sem):
        part = buffer.at[pl.ds(0, count)]
        return remote(part, part, send_sem, recv_sem, other_dev)

    barrier = pltpu.get_barrier_semaphore()

    def greet_plane(step, carry):
        pl.semaphore_signal(barrier, inc=1, device_id=plane(step)[1], device_id_type=MESH)
        return carry

    def greet_column(step, carry):
        pl.semaphore_signal(barrier, inc=1, device_id=column(step)[1], device_id_type=MESH)
        return carry

    key_copy = pltpu.make_async_copy(key_hbm, kbuf, local_sem.at[0])
    value_copy = pltpu.make_async_copy(value_hbm, vbuf, local_sem.at[1])
    key_copy.start()
    value_copy.start()
    weight_copies = []
    for number, (src, dst) in enumerate(((wg_hbm, wg), (wu_hbm, wu), (wd_hbm, wd))):
        for part in range(W_PARTS):
            rows = pl.ds(part * W_ROWS, W_ROWS)
            weight_copies.append(
                pltpu.make_async_copy(
                    src.at[0, rows, :],
                    dst.at[rows, :],
                    local_sem.at[2 + number],
                )
            )
    for copy in weight_copies:
        copy.start()
    lax.fori_loop(1, 16, greet_plane, 0)
    lax.fori_loop(1, 8, greet_column, 0)

    q32 = query[...].astype(F32)
    for head in range(HEADS):
        qs[head * 4 : head * 4 + 4, :] = q32[:, head * 128 : head * 128 + 128]
    nk32 = new_key[...].astype(F32)
    nv32 = new_value[...].astype(F32)
    for copy_no in range(GROUP):
        own_key[copy_no * 4 : copy_no * 4 + 4, :] = nk32
        own_value[copy_no * 4 : copy_no * 4 + 4, :] = nv32
    block = GROUP * ROWS
    row_of = iota((block, 128), 0) & 3
    key_copy.wait()
    for j in range(KV_HEADS):
        qj = qs[j * block : (j + 1) * block, :].astype(BF16)
        total = jnp.zeros((block, 128), F32)
        for r in range(ROWS):
            part = dot_nt(qj, kbuf[r, :, j * 128 : (j + 1) * 128])
            total = jnp.where(row_of == r, part, total)
        scores[j * block : (j + 1) * block, :] = total

    lane32 = iota((32, 32), 1)
    row32 = iota((32, 32), 0)
    fixed = gates[...].astype(F32)
    weights = fixed / jnp.sum(fixed, axis=0, keepdims=True)
    chosen = jnp.zeros((32, 32), F32)
    weighted = jnp.zeros((32, 32), F32)
    route = routes[...]
    for k in range(4):
        same = route[k : k + 1, :] == (row32 >> 1)
        chosen = chosen + jnp.where(same, 1.0, 0.0)
        weighted = weighted + jnp.where(same, weights[k : k + 1, :], 0.0)
    earlier = onehot(((row32 >> 2) == (lane32 >> 2)) & (row32 < lane32))
    before = dot(chosen.astype(BF16), earlier)
    picked = (chosen > 0.5) & (jnp.abs(before - (row32 & 1).astype(F32)) < 0.5)
    sel = onehot(picked)
    wsel = jnp.where(picked, weighted, 0.0)
    whi = wsel.astype(BF16)
    wlo = (wsel - whi.astype(F32)).astype(BF16)

    rr = iota((256, 32), 0)
    ll = iota((256, 32), 1)
    spread_a = onehot((rr >> 3) == ll)
    spread_b = onehot(ll == ((rr >> 4) * 2 + (rr & 1)))
    rr = iota((96, 32), 0)
    ll = iota((96, 32), 1)
    mine = onehot((ll == tp * 4 + (rr & 7)) & ((rr & 7) < 4))
    rr = iota((128, 32), 0)
    ll = iota((128, 32), 1)
    wide = onehot(ll == ((rr >> 4) * 4 + (rr & 3)))
    pack_a = dot_nt(spread_a, dot_nt(mine, sel).astype(BF16))
    rr = iota((256, 96), 0)
    ll = iota((256, 96), 1)
    pack_a = jnp.where((rr & 7) == (ll >> 3), pack_a, 0.0).astype(BF16)
    rr = iota((16, 96), 0)
    ll = iota((16, 96), 1)
    pack_b1 = onehot(ll == (8 + (rr >> 2)) * 8 + (rr & 3))
    pack_b = dot_nt(spread_b, dot_nt(wide, sel).astype(BF16))
    rr = iota((256, 128), 0)
    ll = iota((256, 128), 1)
    pack_b = jnp.where(((rr & 15) >> 1) == (ll >> 4), pack_b, 0.0)

    pos = iota((HEADS * ROWS, 128), 1)
    row_all = iota((HEADS * ROWS, 128), 0) & 3
    limit = jnp.zeros((HEADS * ROWS, 128), jnp.int32)
    for r in range(ROWS):
        limit = jnp.where(row_all == r, clen[r], limit)
    scale = 1.0 / HEAD_DIM**0.5
    s = jnp.where(pos < limit, scores[...] * scale, -1e30)
    own = jnp.concatenate(
        [
            jnp.sum(
                qs[j * block : (j + 1) * block, :] * own_key[:, j * 128 : (j + 1) * 128],
                axis=-1,
                keepdims=True,
            )
            for j in range(KV_HEADS)
        ],
        axis=0,
    )
    own = own * scale
    top = jnp.maximum(jnp.max(s, axis=-1, keepdims=True), own)
    expo = jnp.exp(s - top)
    expo_own = jnp.exp(own - top)
    total = jnp.sum(expo, axis=-1, keepdims=True) + expo_own
    scores[...] = expo / total
    prob_own = (expo_own / total).astype(BF16).astype(F32)
    value_copy.wait()
    for j in range(KV_HEADS):
        pj = scores[j * block : (j + 1) * block, :]
        acc = prob_own[j * block : (j + 1) * block, :] * own_value[:, j * 128 : (j + 1) * 128]
        for r in range(ROWS):
            pr = jnp.where(row_of == r, pj, 0.0).astype(BF16)
            acc = acc + dot(pr, vbuf[r, :, j * 128 : (j + 1) * 128])
        heads_out[j * block : (j + 1) * block, :] = acc
    stream[...] = jnp.zeros((8, D), F32)
    for head in range(HEADS):
        cols = slice(head * 128, head * 128 + 128)
        stream[0:4, cols] = resid[:, cols].astype(F32) + heads_out[head * 4 : head * 4 + 4, :]
    st = stream[...]
    mean = jnp.sum(st, axis=-1, keepdims=True) * (1.0 / D)
    centred = st - mean
    variance = jnp.sum(centred * centred, axis=-1, keepdims=True) * (1.0 / D)
    normed = centred * lax.rsqrt(variance + 1e-05) * gain[...]
    for p in range(12):
        xs[p * 8 : p * 8 + 8, :] = normed[:, p * 512 : (p + 1) * 512]
    xbf = xs[...].astype(BF16)

    bm = dot(pack_b1, xbf).astype(BF16)
    bmsg[...] = bm
    xb1[tp] = bm
    pl.semaphore_wait(barrier, 22)

    def send_b1(step, carry):
        peer, device = column(step)
        remote(bmsg, xb1.at[tp], b1s, b1r, device).start()
        return carry

    lax.fori_loop(1, 8, send_b1, 0)
    packed = dot(pack_a, xbf).astype(BF16)
    apack[...] = packed.reshape(16, 16, 512)
    arecv[me] = apack[me]

    for dy, dz in PLANE:
        step = dy * 4 + dz
        peer, device = plane(step)
        remote(apack.at[peer], arecv.at[me], a1s, a1r, device).start()

    whole(xb1, 7, b1s, b1r).wait_recv()
    xb_all = xb1[...].reshape(128, 512)
    for i in range(2):
        pick = jnp.where(((ll & 15) >> 2) == core * 2 + i, pack_b, 0.0).astype(BF16)
        bpack[:, :, i * 512 : (i + 1) * 512] = (
            dot(pick, xb_all).astype(BF16).reshape(16, 16, 512)
        )
    xbh[core, me] = bpack[me]

    for dy, dz in PLANE:
        step = dy * 4 + dz
        peer, device = plane(step)
        remote(bpack.at[peer], xbh.at[core, me], b2s, b2r, device).start()

    whole(arecv, 15, a1s, a1r).wait_recv()
    rr = iota((256, 256), 0)
    ll = iota((256, 256), 1)
    unpack_a = onehot(ll == (rr & 31) * 8 + (rr >> 5))
    got = dot(unpack_a, arecv[...].reshape(256, 512)).astype(BF16)
    for p in range(8):
        xa[p // 2, core, x, :, (p % 2) * 512 : (p % 2) * 512 + 512] = got[p * 32 : p * 32 + 32, :]

    def near_in(n):
        mine_ref = xa.at[n, core, x]
        to_right = remote(mine_ref, mine_ref, ns, nr.at[0, n], right_dev)
        to_left = remote(mine_ref, mine_ref, ns, nr.at[1, n], left_dev)
        return to_right, to_left

    def near_arrivals(n):
        from_left = xa.at[n, core, left]
        from_right = xa.at[n, core, right]
        a = remote(from_left, from_left, ns, nr.at[0, n], right_dev)
        b = remote(from_right, from_right, ns, nr.at[1, n], left_dev)
        return a, b

    def far_sends(n):
        low = xa.at[n, core, left, pl.ds(0, 16), :]
        high = xa.at[n, core, right, pl.ds(16, 16), :]
        a = remote(low, low, fs, fr.at[0, n], right_dev)
        b = remote(high, high, fs, fr.at[1, n], left_dev)
        return a, b

    def far_arrivals(n):
        low = xa.at[n, core, opposite, pl.ds(0, 16), :]
        high = xa.at[n, core, opposite, pl.ds(16, 16), :]
        a = remote(low, low, fs, fr.at[0, n], right_dev)
        b = remote(high, high, fs, fr.at[1, n], left_dev)
        return a, b

    def core_send(n):
        half = xa.at[n, core]
        return remote(half, half, acs, acr.at[n], other_dev)

    def core_arrival(n):
        half = xa.at[n, 1 - core]
        return remote(half, half, acs, acr.at[n], other_dev)

    for n in range(A_CHUNKS):
        for copy in near_in(n):
            copy.start()

    accg[...] = jnp.zeros((256, HIDDEN), F32)
    accu[...] = jnp.zeros((256, HIDDEN), F32)
    pltpu.make_async_copy(wg_hbm.at[0], wg, local_sem.at[2]).wait()
    pltpu.make_async_copy(wu_hbm.at[0], wu, local_sem.at[3]).wait()

    def project(value, offset):
        cols = pl.ds(offset, CHUNK)
        accg[...] += dot_nt(value, wg[:, cols])
        accu[...] += dot_nt(value, wu[:, cols])

    def project_a(n):
        core_arrival(n).wait_recv()
        project(xa[n].reshape(256, CHUNK), n * CHUNK)

    def relay(n):
        for copy in near_arrivals(n):
            copy.wait_recv()
        for copy in far_sends(n):
            copy.start()

    def forward(n):
        for copy in far_arrivals(n):
            copy.wait_recv()
        core_send(n).start()

    for n in range(A_CHUNKS):
        relay(n)
    forward(0)

    whole(xbh.at[core], 15, b2s, b2r).wait_recv()
    bcore = remote(xbh.at[core], xbh.at[core], bcs, bcr, other_dev)
    bcore.start()
    forward(1)
    tau = rr >> 5
    unpack_b = onehot(
        ll == ((rr & 31) >> 1) * 16 + ((tau & 3) * 2 + (tau >> 2)) * 2 + (rr & 1)
    )

    def project_b(half):
        offset = pl.multiple_of(A_COLS + half * CHUNK, CHUNK)
        project(dot(unpack_b, xbh[half].reshape(256, CHUNK)).astype(BF16), offset)

    project_a(0)
    project_b(core)
    forward(2)
    project_a(1)
    forward(3)
    remote(xbh.at[1 - core], xbh.at[1 - core], bcs, bcr, other_dev).wait_recv()
    project_b(1 - core)
    project_a(2)
    project_a(3)
    g = accg[...]
    hidden = (g * jax.nn.sigmoid(g) * accu[...]).astype(BF16)
    hid[...] = hidden
    t_of = (rr & 15) >> 1
    to_b = onehot(ll == ((t_of & 1) * 4 + (t_of >> 1)) * 32 + (rr >> 4) * 2 + (rr & 1))
    hidb[...] = dot(to_b, hidden).astype(BF16)
    pltpu.make_async_copy(wd_hbm.at[0], wd, local_sem.at[4]).wait()

    def drain():
        whole(xb1, 7, b1s, b1r).wait_send()
        whole(arecv, 15, a1s, a1r).wait_send()
        whole(xbh.at[core], 15, b2s, b2r).wait_send()
        bcore.wait_send()
        remote(xa.at[0], xa.at[0], ns, nr.at[0, 0], other_dev).wait_send()
        remote(xa.at[0, 0], xa.at[0, 0], fs, fr.at[0, 0], other_dev).wait_send()
        remote(xa.at[0:2], xa.at[0:2], acs, acr.at[0], other_dev).wait_send()
        remote(cr, cr, rcs, rcr.at[0], other_dev).wait_send()
        b_core().wait_send()
        whole(bback, 15, rbs, rbr).wait_send()
        remote(far, far, rfs, rfr.at[0, 0], other_dev).wait_send()
        remote(near, near, rns, rnr.at[0, 0], other_dev).wait_send()
        whole(frecv, 7, rfis, rfir).wait_send()

    def down_a(n):
        y = dot(hid[...], wd[:, n * CHUNK : (n + 1) * CHUNK])
        pa[n] = y.astype(BF16).reshape(2, 128, CHUNK)
        pm[n] = jnp.where(core == 0, y[:128], y[128:])
        remote(pa.at[n, 1 - core], cr.at[n], rcs, rcr.at[n], other_dev).start()

    def chip_sum(n):
        remote(pa.at[n, 1 - core], cr.at[n], rcs, rcr.at[n], other_dev).wait_recv()
        both = pm[n] + cr[n].astype(F32)
        pm[n] = both
        cs[n] = both.astype(BF16).reshape(4, 32, CHUNK)
        for copy in ret_far(n):
            copy.start()

    def ret_far(n):
        a = remote(
            cs.at[n, opposite, pl.ds(0, 16), :], far.at[0, n], rfs, rfr.at[0, n], right_dev
        )
        b = remote(
            cs.at[n, opposite, pl.ds(16, 16), :], far.at[1, n], rfs, rfr.at[1, n], left_dev
        )
        return a, b

    def ret_near(n):
        a = remote(cs.at[n, right], near.at[0, n], rns, rnr.at[0, n], right_dev)
        b = remote(cs.at[n, left], near.at[1, n], rns, rnr.at[1, n], left_dev)
        return a, b

    def ret_relay(n):
        for copy in ret_far(n):
            copy.wait_recv()
        to_right = pl.ds(pl.multiple_of(right * 32, 32), 16)
        to_left = pl.ds(pl.multiple_of(left * 32 + 16, 16), 16)
        cs[n, right, 0:16, :] = (pm[n, to_right, :] + far[0, n].astype(F32)).astype(BF16)
        cs[n, left, 16:32, :] = (pm[n, to_left, :] + far[1, n].astype(F32)).astype(BF16)
        for copy in ret_near(n):
            copy.start()

    def ret_sum(n):
        for copy in ret_near(n):
            copy.wait_recv()
        rows = pl.ds(pl.multiple_of(x * 32, 32), 32)
        y = pm[n, rows, :] + near[0, n].astype(F32) + near[1, n].astype(F32)
        y = y.astype(BF16)
        for p in range(2):
            y2[(n * 2 + p) * 32 : (n * 2 + p) * 32 + 32, :] = y[:, p * 512 : p * 512 + 512]

    def b_core():
        return remote(pbs, cbr, rbcs, rbcr, other_dev)

    b0 = dot(hidb[...], wd[:, A_COLS : A_COLS + CHUNK])
    b1 = dot(hidb[...], wd[:, A_COLS + CHUNK : A_COLS + 2 * CHUNK])
    pbs[...] = jnp.where(core == 0, b1, b0).astype(BF16)
    pbm[...] = jnp.where(core == 0, b0, b1)
    b_core().start()
    down_a(0)
    down_a(1)
    chip_sum(0)
    b_core().wait_recv()
    bsend[...] = (pbm[...] + cbr[...].astype(F32)).astype(BF16).reshape(16, 16, CHUNK)
    bback[me] = bsend[me]
    for dy, dz in PLANE:
        step = dy * 4 + dz
        peer, device = plane(step)
        remote(bsend.at[peer], bback.at[me], rbs, rbr, device).start()
    down_a(2)
    chip_sum(1)
    down_a(3)
    chip_sum(2)
    chip_sum(3)
    for n in range(A_CHUNKS):
        ret_relay(n)
    for n in range(A_CHUNKS):
        ret_sum(n)
    rr = iota((256, 256), 0)
    ll = iota((256, 256), 1)
    repack_a = onehot(ll == (rr & 7) * 32 + (rr >> 3))
    asend[...] = dot(repack_a, y2[...]).astype(BF16).reshape(16, 16, 512)
    aback[me] = asend[me]
    for dy, dz in PLANE:
        step = dy * 4 + dz
        peer, device = plane(step)
        remote(asend.at[peer], aback.at[me], ras, rar, device).start()

    rr = iota((128, 256), 0)
    ll = iota((128, 256), 1)
    wide_hi = dot_nt(dot_nt(wide, whi).astype(BF16), spread_b)
    wide_lo = dot_nt(dot_nt(wide, wlo).astype(BF16), spread_b)

    whole(bback, 15, rbs, rbr).wait_recv()
    partial = jnp.zeros((128, 256), F32)
    for q in range(4):
        keep = ((rr >> 4) == ((ll & 15) >> 1)) & (((rr & 15) >> 2) == q)
        piece = bback[:, :, q * 256 : q * 256 + 256].reshape(256, 256)
        partial = partial + dot(jnp.where(keep, wide_hi, 0.0).astype(BF16), piece)
        partial = partial + dot(jnp.where(keep, wide_lo, 0.0).astype(BF16), piece)
    fsend[...] = partial.astype(BF16).reshape(8, 16, 256)
    frecv[tp] = fsend[tp]

    def send_b4(step, carry):
        peer, device = column(step)
        remote(fsend.at[peer], frecv.at[tp], rfis, rfir, device).start()
        return carry

    lax.fori_loop(1, 8, send_b4, 0)
    whole(frecv, 7, rfis, rfir).wait_recv()
    rr = iota((64, 128), 0)
    ll = iota((64, 128), 1)
    gather = onehot(
        ((rr >> 5) == ((ll >> 4) & 1))
        & (((rr >> 3) & 3) == ((ll & 15) >> 2))
        & ((rr & 7) == (ll & 3))
    )
    home_b = dot(gather, frecv[...].reshape(128, 256))
    for piece in range(8):
        start = A_COLS + piece * 256
        out[:, start : start + 256] = (
            stream[0:4, start : start + 256] + home_b[piece * 8 : piece * 8 + 4, :]
        ).astype(BF16)

    rr = iota((64, 256), 0)
    ll = iota((64, 256), 1)
    keep = (rr >> 3) == (ll & 7)
    home_hi = dot_nt(dot_nt(mine[0:64], whi).astype(BF16), spread_a)
    home_lo = dot_nt(dot_nt(mine[0:64], wlo).astype(BF16), spread_a)
    home_hi = jnp.where(keep, home_hi, 0.0).astype(BF16)
    home_lo = jnp.where(keep, home_lo, 0.0).astype(BF16)

    drain()
    whole(aback, 15, ras, rar).wait_recv()
    back = aback[...].reshape(256, 512)
    home_a = dot(home_hi, back) + dot(home_lo, back)
    for p in range(8):
        cols = slice(p * 512, p * 512 + 512)
        out[:, cols] = (stream[0:4, cols] + home_a[p * 8 : p * 8 + 4, :]).astype(BF16)

    whole(aback, 15, ras, rar).wait_send()


def layer(
    resid,
    query,
    key_cache,
    value_cache,
    new_key,
    new_value,
    cache_len,
    norm_gain,
    routes,
    gate_fixed,
    w_gate,
    w_up,
    w_down,
):
    vmem = pl.BlockSpec(memory_space=pltpu.VMEM)
    anywhere = pl.BlockSpec(memory_space=pl.ANY)
    dma = pltpu.SemaphoreType.DMA
    n = A_CHUNKS
    scratch = [
        pltpu.VMEM((ROWS, LENGTH, 1024), BF16),
        pltpu.VMEM((ROWS, LENGTH, 1024), BF16),
        pltpu.VMEM((HIDDEN, D), BF16),
        pltpu.VMEM((HIDDEN, D), BF16),
        pltpu.VMEM((HIDDEN, D), BF16),
        pltpu.VMEM((HEADS * ROWS, 128), F32),
        pltpu.VMEM((HEADS * ROWS, 128), F32),
        pltpu.VMEM((GROUP * ROWS, 1024), F32),
        pltpu.VMEM((GROUP * ROWS, 1024), F32),
        pltpu.VMEM((HEADS * ROWS, 128), F32),
        pltpu.VMEM((8, D), F32),
        pltpu.VMEM((96, 512), F32),
        pltpu.VMEM((16, 16, 512), BF16),
        pltpu.VMEM((16, 16, 512), BF16),
        pltpu.VMEM((16, 512), BF16),
        pltpu.VMEM((8, 16, 512), BF16),
        pltpu.VMEM((16, 16, CHUNK), BF16),
        pltpu.VMEM((2, 16, 16, CHUNK), BF16),
        pltpu.VMEM((n, 2, 4, 32, CHUNK), BF16),
        pltpu.VMEM((256, HIDDEN), F32),
        pltpu.VMEM((256, HIDDEN), F32),
        pltpu.VMEM((256, HIDDEN), BF16),
        pltpu.VMEM((256, HIDDEN), BF16),
        pltpu.VMEM((n, 2, 128, CHUNK), BF16),
        pltpu.VMEM((n, 128, CHUNK), F32),
        pltpu.VMEM((n, 128, CHUNK), BF16),
        pltpu.VMEM((n, 4, 32, CHUNK), BF16),
        pltpu.VMEM((2, n, 16, CHUNK), BF16),
        pltpu.VMEM((2, n, 32, CHUNK), BF16),
        pltpu.VMEM((256, 512), BF16),
        pltpu.VMEM((16, 16, 512), BF16),
        pltpu.VMEM((16, 16, 512), BF16),
        pltpu.VMEM((256, CHUNK), BF16),
        pltpu.VMEM((256, CHUNK), F32),
        pltpu.VMEM((256, CHUNK), BF16),
        pltpu.VMEM((16, 16, CHUNK), BF16),
        pltpu.VMEM((16, 16, CHUNK), BF16),
        pltpu.VMEM((8, 16, 256), BF16),
        pltpu.VMEM((8, 16, 256), BF16),
        dma((5,)),
        dma,
        dma,
        dma,
        dma,
        dma,
        dma,
        dma,
        dma,
        dma,
        dma((2, n)),
        dma,
        dma((2, n)),
        dma,
        dma((n,)),
        dma,
        dma((n,)),
        dma,
        dma((2, n)),
        dma,
        dma((2, n)),
        dma,
        dma,
        dma,
        dma,
        dma,
        dma,
        dma,
        dma,
    ]
    return pl.pallas_call(
        kernel,
        out_shape=jax.ShapeDtypeStruct((ROWS, D), BF16),
        in_specs=[pl.BlockSpec(memory_space=pltpu.SMEM)] + [vmem] * 7 + [anywhere] * 5,
        out_specs=vmem,
        scratch_shapes=scratch,
        compiler_params=pltpu.CompilerParams(
            collective_id=0, has_side_effects=True, vmem_limit_bytes=60 * 1024 * 1024
        ),
        cost_estimate=pl.CostEstimate(
            flops=2 * 3 * 256 * HIDDEN * D, bytes_accessed=27 * 1024 * 1024, transcendentals=0
        ),
    )(
        cache_len,
        resid,
        query,
        new_key,
        new_value,
        norm_gain.reshape(1, D),
        routes.T,
        gate_fixed.T,
        key_cache,
        value_cache,
        w_gate,
        w_up,
        w_down,
    )


def solution(mesh):
    placed = (
        P(("side", "expert", "tp"), None),
        P(("side", "expert", "tp"), None),
        P(("side", "expert", "tp"), None, None),
        P(("side", "expert", "tp"), None, None),
        P(("side", "expert", "tp"), None),
        P(("side", "expert", "tp"), None),
        P(("side", "expert", "tp")),
        P(),
        P(("side", "expert"), None),
        P(("side", "expert"), None),
        P(("side", "expert"), "tp", None),
        P(("side", "expert"), "tp", None),
        P(("side", "expert"), "tp", None),
    )
    return jax.shard_map(
        layer,
        mesh=mesh,
        in_specs=placed,
        out_specs=P(("side", "expert", "tp"), None),
        check_vma=False,
    )
```

```python
import functools

import jax
import jax.numpy as jnp
from jax import lax
from jax.experimental import pallas as pl
from jax.experimental.pallas import tpu as pltpu
from jax.sharding import PartitionSpec as P

D = 6144
HEADS = 48
KV_HEADS = 8
HEAD_DIM = 128
GROUP = HEADS // KV_HEADS
ROWS = 4
LENGTH = 128
HIDDEN = 672
CHUNK = 1024
IN_CHUNKS = 3
IN_A = IN_CHUNKS * CHUNK
IN_PARTS = ((0, 1), (1, 2))
PIECE = (D - IN_A) // 4
A_CHUNKS = 4
A_COLS = A_CHUNKS * CHUNK
F32 = jnp.float32
BF16 = jnp.bfloat16
MESH = pl.DeviceIdType.MESH
W_PARTS = 3
W_ROWS = HIDDEN // W_PARTS
PLANE = ((1, 0), (0, 1), (3, 0), (0, 3), (1, 1), (3, 3), (1, 3), (3, 1), (2, 0), (0, 2), (2, 1), (1, 2), (2, 3), (3, 2), (2, 2))


def iota(shape, dim):
    return lax.broadcasted_iota(jnp.int32, shape, dim)


def dot(a, b):
    return lax.dot_general(a, b, (((1,), (0,)), ((), ())), preferred_element_type=F32)


def dot_nt(a, b):
    return lax.dot_general(a, b, (((1,), (1,)), ((), ())), preferred_element_type=F32)


def onehot(condition):
    return jnp.where(condition, 1.0, 0.0).astype(BF16)


def remote(src, dst, send_sem, recv_sem, device):
    return pltpu.make_async_remote_copy(
        src_ref=src,
        dst_ref=dst,
        send_sem=send_sem,
        recv_sem=recv_sem,
        device_id=device,
        device_id_type=MESH,
    )


def kernel(
    clen_hbm,
    resid_hbm,
    query_hbm,
    new_key_hbm,
    new_value_hbm,
    gain_hbm,
    routes_hbm,
    gates_hbm,
    key_hbm,
    value_hbm,
    wg_hbm,
    wu_hbm,
    wd_hbm,
    out,
    clen,
    resid,
    query,
    new_key,
    new_value,
    gain,
    routes,
    gates,
    kbuf,
    vbuf,
    wg,
    wu,
    wd,
    qs,
    scores,
    own_key,
    own_value,
    heads_out,
    stream,
    xsa0,
    xsa1,
    xsb,
    apack0,
    apack1,
    arecv0,
    arecv1,
    bmsg,
    xb1,
    bpack,
    xbh,
    xa,
    accg,
    accu,
    hid,
    hidb,
    pa,
    pm,
    cr,
    cs,
    far,
    near,
    y2,
    asend,
    aback,
    pbs,
    pbm,
    cbr,
    bsend,
    bback,
    fsend,
    frecv,
    local_sem,
    a1s,
    a1r,
    b1s,
    b1r,
    b2s,
    b2r,
    bcs,
    bcr,
    ns,
    nr,
    fs,
    fr,
    acs,
    acr,
    rcs,
    rcr,
    rfs,
    rfr,
    rns,
    rnr,
    ras,
    rar,
    rbcs,
    rbcr,
    rbs,
    rbr,
    rfis,
    rfir,
):
    side = lax.axis_index("side")
    expert = lax.axis_index("expert")
    tp = lax.axis_index("tp")
    me = side * 8 + expert
    my_y = me // 4
    my_z = me % 4
    x = tp // 2
    core = tp % 2
    right = lax.rem(x + 1, 4)
    left = lax.rem(x + 3, 4)
    opposite = lax.rem(x + 2, 4)
    other_dev = (side, expert, x * 2 + 1 - core)
    right_dev = (side, expert, right * 2 + core)
    left_dev = (side, expert, left * 2 + core)

    def plane(step):
        y = lax.rem(my_y + step // 4, 4)
        z = lax.rem(my_z + step % 4, 4)
        peer = y * 4 + z
        return peer, (peer // 8, peer % 8, tp)

    def column(step):
        peer = lax.rem(tp + step, 8)
        return peer, (side, expert, peer)

    def whole(buffer, count, send_sem, recv_sem):
        part = buffer.at[pl.ds(0, count)]
        return remote(part, part, send_sem, recv_sem, other_dev)

    barrier = pltpu.get_barrier_semaphore()

    def greet_plane(step, carry):
        pl.semaphore_signal(barrier, inc=1, device_id=plane(step)[1], device_id_type=MESH)
        return carry

    def greet_column(step, carry):
        pl.semaphore_signal(barrier, inc=1, device_id=column(step)[1], device_id_type=MESH)
        return carry

    small_copies = [
        pltpu.make_async_copy(src, dst, local_sem.at[5 + number])
        for number, (src, dst) in enumerate(
            (
                (query_hbm, query),
                (new_key_hbm, new_key),
                (new_value_hbm, new_value),
                (routes_hbm, routes),
                (gates_hbm, gates),
                (clen_hbm, clen),
                (resid_hbm, resid),
                (gain_hbm, gain),
            )
        )
    ]
    for copy in small_copies[:6]:
        copy.start()
    key_copy = pltpu.make_async_copy(key_hbm, kbuf, local_sem.at[0])
    value_copy = pltpu.make_async_copy(value_hbm, vbuf, local_sem.at[1])
    key_copy.start()
    value_copy.start()
    for copy in small_copies[6:]:
        copy.start()
    lax.fori_loop(1, 16, greet_plane, 0)
    lax.fori_loop(1, 8, greet_column, 0)
    weight_copies = []
    for number, (src, dst) in enumerate(((wg_hbm, wg), (wu_hbm, wu), (wd_hbm, wd))):
        for part in range(W_PARTS):
            rows = pl.ds(part * W_ROWS, W_ROWS)
            weight_copies.append(
                pltpu.make_async_copy(
                    src.at[0, rows, :],
                    dst.at[rows, :],
                    local_sem.at[2 + number],
                )
            )
    for copy in weight_copies:
        copy.start()

    for copy in small_copies[:3]:
        copy.wait()
    q32 = query[...].astype(F32)
    for head in range(HEADS):
        qs[head * 4 : head * 4 + 4, :] = q32[:, head * 128 : head * 128 + 128]
    nk32 = new_key[...].astype(F32)
    nv32 = new_value[...].astype(F32)
    for copy_no in range(GROUP):
        own_key[copy_no * 4 : copy_no * 4 + 4, :] = nk32
        own_value[copy_no * 4 : copy_no * 4 + 4, :] = nv32
    for copy in small_copies[3:6]:
        copy.wait()
    lane32 = iota((32, 32), 1)
    row32 = iota((32, 32), 0)
    fixed = gates[...].astype(F32)
    weights = fixed / jnp.sum(fixed, axis=0, keepdims=True)
    chosen = jnp.zeros((32, 32), F32)
    weighted = jnp.zeros((32, 32), F32)
    route = routes[...]
    for k in range(4):
        same = route[k : k + 1, :] == (row32 >> 1)
        chosen = chosen + jnp.where(same, 1.0, 0.0)
        weighted = weighted + jnp.where(same, weights[k : k + 1, :], 0.0)
    earlier = onehot(((row32 >> 2) == (lane32 >> 2)) & (row32 < lane32))
    before = dot(chosen.astype(BF16), earlier)
    picked = (chosen > 0.5) & (jnp.abs(before - (row32 & 1).astype(F32)) < 0.5)
    sel = onehot(picked)
    wsel = jnp.where(picked, weighted, 0.0)
    whi = wsel.astype(BF16)
    wlo = (wsel - whi.astype(F32)).astype(BF16)

    rr = iota((256, 32), 0)
    ll = iota((256, 32), 1)
    spread_a = onehot((rr >> 3) == ll)
    spread_b = onehot(ll == ((rr >> 4) * 2 + (rr & 1)))
    rr = iota((64, 32), 0)
    ll = iota((64, 32), 1)
    mine = onehot((ll == tp * 4 + (rr & 7)) & ((rr & 7) < 4))
    rr = iota((128, 32), 0)
    ll = iota((128, 32), 1)
    wide = onehot(ll == ((rr >> 4) * 4 + (rr & 3)))
    pack_a = dot_nt(spread_a, dot_nt(mine, sel).astype(BF16))
    rr = iota((256, 64), 0)
    ll = iota((256, 64), 1)
    pack_a = jnp.where((rr & 7) == (ll >> 3), pack_a, 0.0).astype(BF16)
    rr = iota((16, 32), 0)
    ll = iota((16, 32), 1)
    pack_b1 = onehot(ll == (rr >> 2) * 8 + (rr & 3))
    pack_b = dot_nt(spread_b, dot_nt(wide, sel).astype(BF16))
    rr = iota((256, 128), 0)
    ll = iota((256, 128), 1)
    pack_b = jnp.where(((rr & 15) >> 1) == (ll >> 4), pack_b, 0.0)

    block = GROUP * ROWS
    row_of = iota((block, 128), 0) & 3
    key_copy.wait()
    for j in range(KV_HEADS):
        qj = qs[j * block : (j + 1) * block, :].astype(BF16)
        total = jnp.zeros((block, 128), F32)
        for r in range(ROWS):
            part = dot_nt(qj, kbuf[r, :, j * 128 : (j + 1) * 128])
            total = jnp.where(row_of == r, part, total)
        scores[j * block : (j + 1) * block, :] = total

    pos = iota((HEADS * ROWS, 128), 1)
    row_all = iota((HEADS * ROWS, 128), 0) & 3
    limit = jnp.zeros((HEADS * ROWS, 128), jnp.int32)
    for r in range(ROWS):
        limit = jnp.where(row_all == r, clen[r], limit)
    scale = 1.0 / HEAD_DIM**0.5
    s = jnp.where(pos < limit, scores[...] * scale, -1e30)
    own = jnp.concatenate(
        [
            jnp.sum(
                qs[j * block : (j + 1) * block, :] * own_key[:, j * 128 : (j + 1) * 128],
                axis=-1,
                keepdims=True,
            )
            for j in range(KV_HEADS)
        ],
        axis=0,
    )
    own = own * scale
    top = jnp.maximum(jnp.max(s, axis=-1, keepdims=True), own)
    expo = jnp.exp(s - top)
    expo_own = jnp.exp(own - top)
    total = jnp.sum(expo, axis=-1, keepdims=True) + expo_own
    scores[...] = expo / total
    prob_own = (expo_own / total).astype(BF16).astype(F32)
    value_copy.wait()
    for j in range(KV_HEADS):
        pj = scores[j * block : (j + 1) * block, :]
        acc = prob_own[j * block : (j + 1) * block, :] * own_value[:, j * 128 : (j + 1) * 128]
        for r in range(ROWS):
            pr = jnp.where(row_of == r, pj, 0.0).astype(BF16)
            acc = acc + dot(pr, vbuf[r, :, j * 128 : (j + 1) * 128])
        heads_out[j * block : (j + 1) * block, :] = acc
    for copy in small_copies[6:]:
        copy.wait()
    stream[...] = jnp.zeros((8, D), F32)
    for head in range(HEADS):
        cols = slice(head * 128, head * 128 + 128)
        stream[0:4, cols] = resid[:, cols].astype(F32) + heads_out[head * 4 : head * 4 + 4, :]
    st = stream[...]
    mean = jnp.sum(st, axis=-1, keepdims=True) * (1.0 / D)
    centred = st - mean
    variance = jnp.sum(centred * centred, axis=-1, keepdims=True) * (1.0 / D)
    normed = centred * lax.rsqrt(variance + 1e-05) * gain[...]
    for xs, (first, chunks) in zip((xsa0, xsa1), IN_PARTS):
        width = chunks * CHUNK // 8
        for p in range(8):
            start = first * CHUNK + p * width
            xs[p * 8 : p * 8 + 8, :] = normed[:, start : start + width]
    for p in range(4):
        start = IN_A + p * PIECE
        xsb[p * 8 : p * 8 + 8, :] = normed[:, start : start + PIECE]

    bm = dot(pack_b1, xsb[...].astype(BF16)).astype(BF16)
    bmsg[...] = bm
    xb1[tp] = bm
    pl.semaphore_wait(barrier, 22)

    def send_b1(step, carry):
        peer, device = column(step)
        remote(bmsg, xb1.at[tp], b1s, b1r, device).start()
        return carry

    lax.fori_loop(1, 8, send_b1, 0)
    for h, (xs, apack, arecv) in enumerate(((xsa0, apack0, arecv0), (xsa1, apack1, arecv1))):
        packed = dot(pack_a, xs[...].astype(BF16)).astype(BF16)
        apack[...] = packed.reshape(16, 16, packed.shape[1])
        arecv[me] = apack[me]
        for dy, dz in PLANE:
            peer, device = plane(dy * 4 + dz)
            remote(apack.at[peer], arecv.at[me], a1s.at[h], a1r.at[h], device).start()

    rr = iota((256, 256), 0)
    ll = iota((256, 256), 1)
    unpack_a = onehot(ll == (rr & 31) * 8 + (rr >> 5))

    def arrive_a(h):
        arecv = (arecv0, arecv1)[h]
        first, chunks = IN_PARTS[h]
        width = chunks * CHUNK // 8
        whole(arecv, 15, a1s.at[h], a1r.at[h]).wait_recv()
        got = dot(unpack_a, arecv[...].reshape(256, width)).astype(BF16)
        for p in range(8):
            n, start = divmod(p * width, CHUNK)
            xa[first + n, core, x, :, start : start + width] = got[p * 32 : p * 32 + 32, :]

    def near_in(n):
        mine_ref = xa.at[n, core, x]
        to_right = remote(mine_ref, mine_ref, ns, nr.at[0, n], right_dev)
        to_left = remote(mine_ref, mine_ref, ns, nr.at[1, n], left_dev)
        return to_right, to_left

    def near_arrivals(n):
        from_left = xa.at[n, core, left]
        from_right = xa.at[n, core, right]
        a = remote(from_left, from_left, ns, nr.at[0, n], right_dev)
        b = remote(from_right, from_right, ns, nr.at[1, n], left_dev)
        return a, b

    def far_sends(n):
        low = xa.at[n, core, left, pl.ds(0, 16), :]
        high = xa.at[n, core, right, pl.ds(16, 16), :]
        a = remote(low, low, fs, fr.at[0, n], right_dev)
        b = remote(high, high, fs, fr.at[1, n], left_dev)
        return a, b

    def far_arrivals(n):
        low = xa.at[n, core, opposite, pl.ds(0, 16), :]
        high = xa.at[n, core, opposite, pl.ds(16, 16), :]
        a = remote(low, low, fs, fr.at[0, n], right_dev)
        b = remote(high, high, fs, fr.at[1, n], left_dev)
        return a, b

    def core_send(n, place):
        block = xa.at[n, core, place]
        remote(block, block, acs, acr.at[n], other_dev).start()

    def core_arrival(n):
        half = xa.at[n, 1 - core]
        return remote(half, half, acs, acr.at[n], other_dev)

    def near_send(n):
        for copy in near_in(n):
            copy.start()
        core_send(n, x)

    def wait_rows():
        whole(xb1, 7, b1s, b1r).wait_recv()

    def send_b2(i):
        lane = iota((256, 128), 1)
        pick = jnp.where(((lane & 15) >> 2) == core * 2 + i, pack_b, 0.0).astype(BF16)
        bpack[i] = dot(pick, xb1[...].reshape(128, PIECE)).astype(BF16).reshape(16, 16, PIECE)
        xbh[i, core, me] = bpack[i, me]
        for dy, dz in PLANE:
            peer, device = plane(dy * 4 + dz)
            remote(
                bpack.at[i, peer], xbh.at[i, core, me], b2s.at[i], b2r.at[i], device
            ).start()

    arrive_a(0)
    near_send(0)
    wait_rows()
    send_b2(0)
    arrive_a(1)
    near_send(1)
    accg[...] = jnp.zeros((HIDDEN, 256), F32)
    accu[...] = jnp.zeros((HIDDEN, 256), F32)
    pltpu.make_async_copy(wg_hbm.at[0], wg, local_sem.at[2]).wait()
    pltpu.make_async_copy(wu_hbm.at[0], wu, local_sem.at[3]).wait()

    def project(value, offset):
        cols = pl.ds(offset, value.shape[1])
        accg[...] += dot_nt(wg[:, cols], value)
        accu[...] += dot_nt(wu[:, cols], value)

    def project_a(n):
        core_arrival(n).wait_recv()
        project(xa[n].reshape(256, CHUNK), n * CHUNK)

    def relay(n):
        for arrival, send, place in zip(near_arrivals(n), far_sends(n), (left, right)):
            arrival.wait_recv()
            send.start()
            core_send(n, place)

    def forward(n):
        for copy in far_arrivals(n):
            copy.wait_recv()
        core_send(n, opposite)

    def b2_core(i):
        return remote(xbh.at[i, core], xbh.at[i, core], bcs, bcr.at[i], other_dev)

    def forward_b(i):
        whole(xbh.at[i, core], 15, b2s.at[i], b2r.at[i]).wait_recv()
        b2_core(i).start()

    tau = rr >> 5
    unpack_b = onehot(
        ll == ((rr & 31) >> 1) * 16 + ((tau & 3) * 2 + (tau >> 2)) * 2 + (rr & 1)
    )

    def project_b(half, i):
        offset = pl.multiple_of(IN_A + half * 2 * PIECE + i * PIECE, PIECE)
        project(dot(unpack_b, xbh[i, half].reshape(256, PIECE)).astype(BF16), offset)

    def project_own(i):
        project_b(core, i)

    def project_other(i):
        remote(
            xbh.at[i, 1 - core], xbh.at[i, 1 - core], bcs, bcr.at[i], other_dev
        ).wait_recv()
        project_b(1 - core, i)

    relay(0)
    near_send(2)
    send_b2(1)
    relay(1)
    forward(0)
    forward_b(0)
    relay(2)
    project_a(0)
    project_own(0)
    forward(1)
    project_other(0)
    project_a(1)
    forward(2)
    forward_b(1)
    project_own(1)
    project_a(2)
    project_other(1)
    g = accg[...]
    hidden = (g * jax.nn.sigmoid(g) * accu[...]).astype(BF16)
    hid[...] = dot_nt(onehot(rr == ll), hidden).astype(BF16)
    t_of = (rr & 15) >> 1
    to_b = onehot(ll == ((t_of & 1) * 4 + (t_of >> 1)) * 32 + (rr >> 4) * 2 + (rr & 1))
    pltpu.make_async_copy(wd_hbm.at[0], wd, local_sem.at[4]).wait()

    def drain():
        whole(xb1, 7, b1s, b1r).wait_send()
        whole(arecv0, 15, a1s.at[0], a1r.at[0]).wait_send()
        whole(arecv1, 15, a1s.at[1], a1r.at[1]).wait_send()
        for i in range(2):
            whole(xbh.at[i, core], 15, b2s.at[i], b2r.at[i]).wait_send()
        remote(xbh.at[0:2, 0], xbh.at[0:2, 0], bcs, bcr.at[0], other_dev).wait_send()
        sent = xa.at[0:IN_CHUNKS, 0, 0:2]
        remote(sent, sent, ns, nr.at[0, 0], other_dev).wait_send()
        sent = xa.at[0:IN_CHUNKS, 0, 0]
        remote(sent, sent, fs, fr.at[0, 0], other_dev).wait_send()
        sent = xa.at[0:IN_CHUNKS, 0]
        remote(sent, sent, acs, acr.at[0], other_dev).wait_send()
        remote(cr, cr, rcs, rcr.at[0], other_dev).wait_send()
        b_core().wait_send()
        whole(bback, 15, rbs, rbr).wait_send()
        remote(far, far, rfs, rfr.at[0, 0], other_dev).wait_send()
        remote(near, near, rns, rnr.at[0, 0], other_dev).wait_send()
        whole(frecv, 7, rfis, rfir).wait_send()

    def down_a(n):
        y = dot(hid[...], wd[:, n * CHUNK : (n + 1) * CHUNK])
        pa[n] = y.astype(BF16).reshape(2, 128, CHUNK)
        pm[n] = jnp.where(core == 0, y[:128], y[128:])
        remote(pa.at[n, 1 - core], cr.at[n], rcs, rcr.at[n], other_dev).start()

    def chip_sum(n):
        remote(pa.at[n, 1 - core], cr.at[n], rcs, rcr.at[n], other_dev).wait_recv()
        both = pm[n] + cr[n].astype(F32)
        pm[n] = both
        cs[n] = both.astype(BF16).reshape(4, 32, CHUNK)
        for copy in ret_far(n):
            copy.start()

    def ret_far(n):
        a = remote(
            cs.at[n, opposite, pl.ds(0, 16), :], far.at[0, n], rfs, rfr.at[0, n], right_dev
        )
        b = remote(
            cs.at[n, opposite, pl.ds(16, 16), :], far.at[1, n], rfs, rfr.at[1, n], left_dev
        )
        return a, b

    def ret_near(n):
        a = remote(cs.at[n, right], near.at[0, n], rns, rnr.at[0, n], right_dev)
        b = remote(cs.at[n, left], near.at[1, n], rns, rnr.at[1, n], left_dev)
        return a, b

    def ret_relay(n):
        for copy in ret_far(n):
            copy.wait_recv()
        to_right = pl.ds(pl.multiple_of(right * 32, 32), 16)
        to_left = pl.ds(pl.multiple_of(left * 32 + 16, 16), 16)
        cs[n, right, 0:16, :] = (pm[n, to_right, :] + far[0, n].astype(F32)).astype(BF16)
        cs[n, left, 16:32, :] = (pm[n, to_left, :] + far[1, n].astype(F32)).astype(BF16)
        for copy in ret_near(n):
            copy.start()

    def ret_sum(n):
        for copy in ret_near(n):
            copy.wait_recv()
        rows = pl.ds(pl.multiple_of(x * 32, 32), 32)
        y = pm[n, rows, :] + near[0, n].astype(F32) + near[1, n].astype(F32)
        y = y.astype(BF16)
        for q in range(4):
            row = ((n % 2) * 4 + q) * 32
            y2[n // 2, row : row + 32, :] = y[:, q * 256 : q * 256 + 256]

    def b_core():
        return remote(pbs, cbr, rbcs, rbcr, other_dev)

    def down_b(half):
        cols = pl.ds(pl.multiple_of(A_COLS + half * CHUNK, CHUNK), CHUNK)
        return dot(hidb[...], wd[:, cols])

    def b_other():
        hidb[...] = dot_nt(to_b, hidden).astype(BF16)
        pbs[...] = down_b(1 - core).astype(BF16)
        b_core().start()

    def b_mine():
        pbm[...] = down_b(core)

    def b_home():
        b_core().wait_recv()
        bsend[...] = (pbm[...] + cbr[...].astype(F32)).astype(BF16).reshape(16, 16, CHUNK)
        bback[me] = bsend[me]
        for dy, dz in PLANE:
            peer, device = plane(dy * 4 + dz)
            remote(bsend.at[peer], bback.at[me], rbs, rbr, device).start()

    rr = iota((256, 256), 0)
    ll = iota((256, 256), 1)
    repack_a = onehot(ll == (rr & 7) * 32 + (rr >> 3))

    def a_home(h):
        asend[h] = dot(repack_a, y2[h]).astype(BF16).reshape(16, 16, 256)
        aback[h, me] = asend[h, me]
        for dy, dz in PLANE:
            peer, device = plane(dy * 4 + dz)
            remote(asend.at[h, peer], aback.at[h, me], ras.at[h], rar.at[h], device).start()

    down_a(0)
    down_a(1)
    chip_sum(0)
    b_other()
    down_a(2)
    chip_sum(1)
    down_a(3)
    chip_sum(2)
    ret_relay(0)
    b_mine()
    chip_sum(3)
    b_home()
    ret_relay(1)
    ret_relay(2)
    ret_relay(3)
    ret_sum(0)
    ret_sum(1)
    a_home(0)
    ret_sum(2)
    ret_sum(3)
    a_home(1)

    rr = iota((128, 256), 0)
    ll = iota((128, 256), 1)
    wide_hi = dot_nt(dot_nt(wide, whi).astype(BF16), spread_b)
    wide_lo = dot_nt(dot_nt(wide, wlo).astype(BF16), spread_b)

    whole(bback, 15, rbs, rbr).wait_recv()
    partial = jnp.zeros((128, 256), F32)
    for q in range(4):
        keep = ((rr >> 4) == ((ll & 15) >> 1)) & (((rr & 15) >> 2) == q)
        piece = bback[:, :, q * 256 : q * 256 + 256].reshape(256, 256)
        partial = partial + dot(jnp.where(keep, wide_hi, 0.0).astype(BF16), piece)
        partial = partial + dot(jnp.where(keep, wide_lo, 0.0).astype(BF16), piece)
    fsend[...] = partial.astype(BF16).reshape(8, 16, 256)
    frecv[tp] = fsend[tp]

    def send_b4(step, carry):
        peer, device = column(step)
        remote(fsend.at[peer], frecv.at[tp], rfis, rfir, device).start()
        return carry

    lax.fori_loop(1, 8, send_b4, 0)
    whole(frecv, 7, rfis, rfir).wait_recv()
    rr = iota((64, 128), 0)
    ll = iota((64, 128), 1)
    gather = onehot(
        ((rr >> 5) == ((ll >> 4) & 1))
        & (((rr >> 3) & 3) == ((ll & 15) >> 2))
        & ((rr & 7) == (ll & 3))
    )
    home_b = dot(gather, frecv[...].reshape(128, 256))
    for piece in range(8):
        start = A_COLS + piece * 256
        out[:, start : start + 256] = (
            stream[0:4, start : start + 256] + home_b[piece * 8 : piece * 8 + 4, :]
        ).astype(BF16)

    rr = iota((64, 256), 0)
    ll = iota((64, 256), 1)
    keep = (rr >> 3) == (ll & 7)
    home_hi = dot_nt(dot_nt(mine, whi).astype(BF16), spread_a)
    home_lo = dot_nt(dot_nt(mine, wlo).astype(BF16), spread_a)
    home_hi = jnp.where(keep, home_hi, 0.0).astype(BF16)
    home_lo = jnp.where(keep, home_lo, 0.0).astype(BF16)

    drain()
    for h in range(2):
        whole(aback.at[h], 15, ras.at[h], rar.at[h]).wait_recv()
        back = aback[h].reshape(256, 256)
        home_a = dot(home_hi, back) + dot(home_lo, back)
        for p in range(8):
            cols = slice(h * 2048 + p * 256, h * 2048 + p * 256 + 256)
            out[:, cols] = (stream[0:4, cols] + home_a[p * 8 : p * 8 + 4, :]).astype(BF16)
    for h in range(2):
        whole(aback.at[h], 15, ras.at[h], rar.at[h]).wait_send()


def layer(
    resid,
    query,
    key_cache,
    value_cache,
    new_key,
    new_value,
    cache_len,
    norm_gain,
    routes,
    gate_fixed,
    w_gate,
    w_up,
    w_down,
):
    vmem = pl.BlockSpec(memory_space=pltpu.VMEM)
    anywhere = pl.BlockSpec(memory_space=pl.ANY)
    dma = pltpu.SemaphoreType.DMA
    n = A_CHUNKS
    scratch = [
        pltpu.SMEM((ROWS,), jnp.int32),
        pltpu.VMEM((ROWS, D), BF16),
        pltpu.VMEM((ROWS, D), BF16),
        pltpu.VMEM((ROWS, 1024), BF16),
        pltpu.VMEM((ROWS, 1024), BF16),
        pltpu.VMEM((1, D), F32),
        pltpu.VMEM((4, 32), jnp.int32),
        pltpu.VMEM((4, 32), jnp.int32),
        pltpu.VMEM((ROWS, LENGTH, 1024), BF16),
        pltpu.VMEM((ROWS, LENGTH, 1024), BF16),
        pltpu.VMEM((HIDDEN, D), BF16),
        pltpu.VMEM((HIDDEN, D), BF16),
        pltpu.VMEM((HIDDEN, D), BF16),
        pltpu.VMEM((HEADS * ROWS, 128), F32),
        pltpu.VMEM((HEADS * ROWS, 128), F32),
        pltpu.VMEM((GROUP * ROWS, 1024), F32),
        pltpu.VMEM((GROUP * ROWS, 1024), F32),
        pltpu.VMEM((HEADS * ROWS, 128), F32),
        pltpu.VMEM((8, D), F32),
        pltpu.VMEM((64, 128), F32),
        pltpu.VMEM((64, 256), F32),
        pltpu.VMEM((32, PIECE), F32),
        pltpu.VMEM((16, 16, 128), BF16),
        pltpu.VMEM((16, 16, 256), BF16),
        pltpu.VMEM((16, 16, 128), BF16),
        pltpu.VMEM((16, 16, 256), BF16),
        pltpu.VMEM((16, PIECE), BF16),
        pltpu.VMEM((8, 16, PIECE), BF16),
        pltpu.VMEM((2, 16, 16, PIECE), BF16),
        pltpu.VMEM((2, 2, 16, 16, PIECE), BF16),
        pltpu.VMEM((IN_CHUNKS, 2, 4, 32, CHUNK), BF16),
        pltpu.VMEM((HIDDEN, 256), F32),
        pltpu.VMEM((HIDDEN, 256), F32),
        pltpu.VMEM((256, HIDDEN), BF16),
        pltpu.VMEM((256, HIDDEN), BF16),
        pltpu.VMEM((n, 2, 128, CHUNK), BF16),
        pltpu.VMEM((n, 128, CHUNK), F32),
        pltpu.VMEM((n, 128, CHUNK), BF16),
        pltpu.VMEM((n, 4, 32, CHUNK), BF16),
        pltpu.VMEM((2, n, 16, CHUNK), BF16),
        pltpu.VMEM((2, n, 32, CHUNK), BF16),
        pltpu.VMEM((2, 256, 256), BF16),
        pltpu.VMEM((2, 16, 16, 256), BF16),
        pltpu.VMEM((2, 16, 16, 256), BF16),
        pltpu.VMEM((256, CHUNK), BF16),
        pltpu.VMEM((256, CHUNK), F32),
        pltpu.VMEM((256, CHUNK), BF16),
        pltpu.VMEM((16, 16, CHUNK), BF16),
        pltpu.VMEM((16, 16, CHUNK), BF16),
        pltpu.VMEM((8, 16, 256), BF16),
        pltpu.VMEM((8, 16, 256), BF16),
        dma((13,)),
        dma((2,)),
        dma((2,)),
        dma,
        dma,
        dma((2,)),
        dma((2,)),
        dma,
        dma((2,)),
        dma,
        dma((2, n)),
        dma,
        dma((2, n)),
        dma,
        dma((n,)),
        dma,
        dma((n,)),
        dma,
        dma((2, n)),
        dma,
        dma((2, n)),
        dma((2,)),
        dma((2,)),
        dma,
        dma,
        dma,
        dma,
        dma,
        dma,
    ]
    return pl.pallas_call(
        kernel,
        out_shape=jax.ShapeDtypeStruct((ROWS, D), BF16),
        in_specs=[anywhere] * 13,
        out_specs=vmem,
        scratch_shapes=scratch,
        compiler_params=pltpu.CompilerParams(
            collective_id=0, has_side_effects=True, vmem_limit_bytes=60 * 1024 * 1024
        ),
        cost_estimate=pl.CostEstimate(
            flops=2 * 3 * 256 * HIDDEN * D, bytes_accessed=27 * 1024 * 1024, transcendentals=0
        ),
    )(
        cache_len,
        resid,
        query,
        new_key,
        new_value,
        norm_gain.reshape(1, D),
        routes.T,
        gate_fixed.T,
        key_cache,
        value_cache,
        w_gate,
        w_up,
        w_down,
    )


def solution(mesh):
    placed = (
        P(("side", "expert", "tp"), None),
        P(("side", "expert", "tp"), None),
        P(("side", "expert", "tp"), None, None),
        P(("side", "expert", "tp"), None, None),
        P(("side", "expert", "tp"), None),
        P(("side", "expert", "tp"), None),
        P(("side", "expert", "tp")),
        P(),
        P(("side", "expert"), None),
        P(("side", "expert"), None),
        P(("side", "expert"), "tp", None),
        P(("side", "expert"), "tp", None),
        P(("side", "expert"), "tp", None),
    )
    return jax.shard_map(
        layer,
        mesh=mesh,
        in_specs=placed,
        out_specs=P(("side", "expert", "tp"), None),
        check_vma=False,
    )
```

```python
import functools

import jax
import jax.numpy as jnp
from jax import lax
from jax.experimental import pallas as pl
from jax.experimental.pallas import tpu as pltpu
from jax.sharding import PartitionSpec as P

D = 6144
HEADS = 48
KV_HEADS = 8
HEAD_DIM = 128
GROUP = HEADS // KV_HEADS
ROWS = 4
LENGTH = 128
HIDDEN = 672
CHUNK = 1024
IN_CHUNKS = 3
IN_A = IN_CHUNKS * CHUNK
IN_PARTS = ((0, 1), (1, 2))
PIECE = (D - IN_A) // 4
B_PARTS = ((0, 0, 256), (0, 256, 512), (1, 0, 768))
A_CHUNKS = 4
A_COLS = A_CHUNKS * CHUNK
F32 = jnp.float32
BF16 = jnp.bfloat16
MESH = pl.DeviceIdType.MESH
W_PARTS = 3
W_ROWS = HIDDEN // W_PARTS
PLANE = ((1, 0), (0, 1), (3, 0), (0, 3), (1, 1), (3, 3), (1, 3), (3, 1), (2, 0), (0, 2), (2, 1), (1, 2), (2, 3), (3, 2), (2, 2))


def iota(shape, dim):
    return lax.broadcasted_iota(jnp.int32, shape, dim)


def dot(a, b):
    return lax.dot_general(a, b, (((1,), (0,)), ((), ())), preferred_element_type=F32)


def dot_nt(a, b):
    return lax.dot_general(a, b, (((1,), (1,)), ((), ())), preferred_element_type=F32)


def onehot(condition):
    return jnp.where(condition, 1.0, 0.0).astype(BF16)


def remote(src, dst, send_sem, recv_sem, device):
    return pltpu.make_async_remote_copy(
        src_ref=src,
        dst_ref=dst,
        send_sem=send_sem,
        recv_sem=recv_sem,
        device_id=device,
        device_id_type=MESH,
    )


def kernel(
    clen_hbm,
    resid_hbm,
    query_hbm,
    new_key_hbm,
    new_value_hbm,
    gain_hbm,
    routes_hbm,
    gates_hbm,
    key_hbm,
    value_hbm,
    wg_hbm,
    wu_hbm,
    wd_hbm,
    out,
    clen,
    resid,
    query,
    new_key,
    new_value,
    gain,
    routes,
    gates,
    kbuf,
    vbuf,
    wg,
    wu,
    wd,
    qs,
    scores,
    own_key,
    own_value,
    heads_out,
    stream,
    xsa0,
    xsa1,
    xsb,
    apack0,
    apack1,
    arecv0,
    arecv1,
    bmsg,
    xb1,
    bpack0,
    bpack1,
    bpack2,
    xbh0,
    xbh1,
    xbh2,
    xa,
    accg,
    accu,
    hid,
    hidb,
    pa,
    pm,
    cr,
    cs,
    far,
    near,
    y2,
    asend,
    aback,
    pbs,
    pbm,
    cbr,
    bsend,
    bback,
    fsend,
    frecv,
    local_sem,
    a1s,
    a1r,
    b1s,
    b1r,
    b2s,
    b2r,
    bcs,
    bcr,
    ns,
    nr,
    fs,
    fr,
    acs,
    acr,
    rcs,
    rcr,
    rfs,
    rfr,
    rns,
    rnr,
    ras,
    rar,
    rbcs,
    rbcr,
    rbs,
    rbr,
    rfis,
    rfir,
):
    side = lax.axis_index("side")
    expert = lax.axis_index("expert")
    tp = lax.axis_index("tp")
    me = side * 8 + expert
    my_y = me // 4
    my_z = me % 4
    x = tp // 2
    core = tp % 2
    right = lax.rem(x + 1, 4)
    left = lax.rem(x + 3, 4)
    opposite = lax.rem(x + 2, 4)
    other_dev = (side, expert, x * 2 + 1 - core)
    right_dev = (side, expert, right * 2 + core)
    left_dev = (side, expert, left * 2 + core)

    def plane(step):
        y = lax.rem(my_y + step // 4, 4)
        z = lax.rem(my_z + step % 4, 4)
        peer = y * 4 + z
        return peer, (peer // 8, peer % 8, tp)

    def column(step):
        peer = lax.rem(tp + step, 8)
        return peer, (side, expert, peer)

    def whole(buffer, count, send_sem, recv_sem):
        part = buffer.at[pl.ds(0, count)]
        return remote(part, part, send_sem, recv_sem, other_dev)

    bpacks = (bpack0, bpack1, bpack2)
    xbhs = (xbh0, xbh1, xbh2)
    barrier = pltpu.get_barrier_semaphore()

    def greet_plane(step, carry):
        pl.semaphore_signal(barrier, inc=1, device_id=plane(step)[1], device_id_type=MESH)
        return carry

    def greet_column(step, carry):
        pl.semaphore_signal(barrier, inc=1, device_id=column(step)[1], device_id_type=MESH)
        return carry

    small_copies = [
        pltpu.make_async_copy(src, dst, local_sem.at[5 + number])
        for number, (src, dst) in enumerate(
            (
                (query_hbm, query),
                (new_key_hbm, new_key),
                (new_value_hbm, new_value),
                (routes_hbm, routes),
                (gates_hbm, gates),
                (clen_hbm, clen),
                (resid_hbm, resid),
                (gain_hbm, gain),
            )
        )
    ]
    for copy in small_copies[:6]:
        copy.start()
    key_copy = pltpu.make_async_copy(key_hbm, kbuf, local_sem.at[0])
    value_copy = pltpu.make_async_copy(value_hbm, vbuf, local_sem.at[1])
    key_copy.start()
    value_copy.start()
    for copy in small_copies[6:]:
        copy.start()
    lax.fori_loop(1, 16, greet_plane, 0)
    lax.fori_loop(1, 8, greet_column, 0)
    weight_copies = []
    for number, (src, dst) in enumerate(((wg_hbm, wg), (wu_hbm, wu), (wd_hbm, wd))):
        for part in range(W_PARTS):
            rows = pl.ds(part * W_ROWS, W_ROWS)
            weight_copies.append(
                pltpu.make_async_copy(
                    src.at[0, rows, :],
                    dst.at[rows, :],
                    local_sem.at[2 + number],
                )
            )
    for copy in weight_copies:
        copy.start()

    for copy in small_copies[:3]:
        copy.wait()
    q32 = query[...].astype(F32)
    for head in range(HEADS):
        qs[head * 4 : head * 4 + 4, :] = q32[:, head * 128 : head * 128 + 128]
    nk32 = new_key[...].astype(F32)
    nv32 = new_value[...].astype(F32)
    for copy_no in range(GROUP):
        own_key[copy_no * 4 : copy_no * 4 + 4, :] = nk32
        own_value[copy_no * 4 : copy_no * 4 + 4, :] = nv32
    for copy in small_copies[3:6]:
        copy.wait()
    lane32 = iota((32, 32), 1)
    row32 = iota((32, 32), 0)
    fixed = gates[...].astype(F32)
    weights = fixed / jnp.sum(fixed, axis=0, keepdims=True)
    chosen = jnp.zeros((32, 32), F32)
    weighted = jnp.zeros((32, 32), F32)
    route = routes[...]
    for k in range(4):
        same = route[k : k + 1, :] == (row32 >> 1)
        chosen = chosen + jnp.where(same, 1.0, 0.0)
        weighted = weighted + jnp.where(same, weights[k : k + 1, :], 0.0)
    earlier = onehot(((row32 >> 2) == (lane32 >> 2)) & (row32 < lane32))
    before = dot(chosen.astype(BF16), earlier)
    picked = (chosen > 0.5) & (jnp.abs(before - (row32 & 1).astype(F32)) < 0.5)
    sel = onehot(picked)
    wsel = jnp.where(picked, weighted, 0.0)
    whi = wsel.astype(BF16)
    wlo = (wsel - whi.astype(F32)).astype(BF16)

    rr = iota((256, 32), 0)
    ll = iota((256, 32), 1)
    spread_a = onehot((rr >> 3) == ll)
    spread_b = onehot(ll == ((rr >> 4) * 2 + (rr & 1)))
    rr = iota((64, 32), 0)
    ll = iota((64, 32), 1)
    mine = onehot((ll == tp * 4 + (rr & 7)) & ((rr & 7) < 4))
    rr = iota((128, 32), 0)
    ll = iota((128, 32), 1)
    wide = onehot(ll == ((rr >> 4) * 4 + (rr & 3)))
    pack_a = dot_nt(spread_a, dot_nt(mine, sel).astype(BF16))
    rr = iota((256, 64), 0)
    ll = iota((256, 64), 1)
    pack_a = jnp.where((rr & 7) == (ll >> 3), pack_a, 0.0).astype(BF16)
    rr = iota((16, 32), 0)
    ll = iota((16, 32), 1)
    pack_b1 = onehot(ll == (rr >> 2) * 8 + (rr & 3))
    pack_b = dot_nt(spread_b, dot_nt(wide, sel).astype(BF16))
    rr = iota((256, 128), 0)
    ll = iota((256, 128), 1)
    pack_b = jnp.where(((rr & 15) >> 1) == (ll >> 4), pack_b, 0.0)

    block = GROUP * ROWS
    row_of = iota((block, 128), 0) & 3
    key_copy.wait()
    for j in range(KV_HEADS):
        qj = qs[j * block : (j + 1) * block, :].astype(BF16)
        total = jnp.zeros((block, 128), F32)
        for r in range(ROWS):
            part = dot_nt(qj, kbuf[r, :, j * 128 : (j + 1) * 128])
            total = jnp.where(row_of == r, part, total)
        scores[j * block : (j + 1) * block, :] = total

    pos = iota((HEADS * ROWS, 128), 1)
    row_all = iota((HEADS * ROWS, 128), 0) & 3
    limit = jnp.zeros((HEADS * ROWS, 128), jnp.int32)
    for r in range(ROWS):
        limit = jnp.where(row_all == r, clen[r], limit)
    scale = 1.0 / HEAD_DIM**0.5
    s = jnp.where(pos < limit, scores[...] * scale, -1e30)
    own = jnp.concatenate(
        [
            jnp.sum(
                qs[j * block : (j + 1) * block, :] * own_key[:, j * 128 : (j + 1) * 128],
                axis=-1,
                keepdims=True,
            )
            for j in range(KV_HEADS)
        ],
        axis=0,
    )
    own = own * scale
    top = jnp.maximum(jnp.max(s, axis=-1, keepdims=True), own)
    expo = jnp.exp(s - top)
    expo_own = jnp.exp(own - top)
    total = jnp.sum(expo, axis=-1, keepdims=True) + expo_own
    scores[...] = expo / total
    prob_own = (expo_own / total).astype(BF16).astype(F32)
    value_copy.wait()
    for j in range(KV_HEADS):
        pj = scores[j * block : (j + 1) * block, :]
        acc = prob_own[j * block : (j + 1) * block, :] * own_value[:, j * 128 : (j + 1) * 128]
        for r in range(ROWS):
            pr = jnp.where(row_of == r, pj, 0.0).astype(BF16)
            acc = acc + dot(pr, vbuf[r, :, j * 128 : (j + 1) * 128])
        heads_out[j * block : (j + 1) * block, :] = acc
    for copy in small_copies[6:]:
        copy.wait()
    stream[...] = jnp.zeros((8, D), F32)
    for head in range(HEADS):
        cols = slice(head * 128, head * 128 + 128)
        stream[0:4, cols] = resid[:, cols].astype(F32) + heads_out[head * 4 : head * 4 + 4, :]
    st = stream[...]
    mean = jnp.sum(st, axis=-1, keepdims=True) * (1.0 / D)
    centred = st - mean
    variance = jnp.sum(centred * centred, axis=-1, keepdims=True) * (1.0 / D)
    normed = centred * lax.rsqrt(variance + 1e-05) * gain[...]
    for xs, (first, chunks) in zip((xsa0, xsa1), IN_PARTS):
        width = chunks * CHUNK // 8
        for p in range(8):
            start = first * CHUNK + p * width
            xs[p * 8 : p * 8 + 8, :] = normed[:, start : start + width]
    for p in range(4):
        start = IN_A + p * PIECE
        xsb[p * 8 : p * 8 + 8, :] = normed[:, start : start + PIECE]

    bm = dot(pack_b1, xsb[...].astype(BF16)).astype(BF16)
    bmsg[...] = bm
    xb1[tp] = bm
    pl.semaphore_wait(barrier, 22)

    def send_b1(step, carry):
        peer, device = column(step)
        remote(bmsg, xb1.at[tp], b1s, b1r, device).start()
        return carry

    lax.fori_loop(1, 8, send_b1, 0)
    for h, (xs, apack, arecv) in enumerate(((xsa0, apack0, arecv0), (xsa1, apack1, arecv1))):
        packed = dot(pack_a, xs[...].astype(BF16)).astype(BF16)
        apack[...] = packed.reshape(16, 16, packed.shape[1])
        arecv[me] = apack[me]
        for dy, dz in PLANE:
            peer, device = plane(dy * 4 + dz)
            remote(apack.at[peer], arecv.at[me], a1s.at[h], a1r.at[h], device).start()

    rr = iota((256, 256), 0)
    ll = iota((256, 256), 1)
    unpack_a = onehot(ll == (rr & 31) * 8 + (rr >> 5))

    def arrive_a(h):
        arecv = (arecv0, arecv1)[h]
        first, chunks = IN_PARTS[h]
        width = chunks * CHUNK // 8
        whole(arecv, 15, a1s.at[h], a1r.at[h]).wait_recv()
        got = dot(unpack_a, arecv[...].reshape(256, width)).astype(BF16)
        for p in range(8):
            n, start = divmod(p * width, CHUNK)
            xa[first + n, core, x, :, start : start + width] = got[p * 32 : p * 32 + 32, :]

    def near_in(n):
        mine_ref = xa.at[n, core, x]
        to_right = remote(mine_ref, mine_ref, ns, nr.at[0, n], right_dev)
        to_left = remote(mine_ref, mine_ref, ns, nr.at[1, n], left_dev)
        return to_right, to_left

    def near_arrivals(n):
        from_left = xa.at[n, core, left]
        from_right = xa.at[n, core, right]
        a = remote(from_left, from_left, ns, nr.at[0, n], right_dev)
        b = remote(from_right, from_right, ns, nr.at[1, n], left_dev)
        return a, b

    def far_sends(n):
        low = xa.at[n, core, left, pl.ds(0, 16), :]
        high = xa.at[n, core, right, pl.ds(16, 16), :]
        a = remote(low, low, fs, fr.at[0, n], right_dev)
        b = remote(high, high, fs, fr.at[1, n], left_dev)
        return a, b

    def far_arrivals(n):
        low = xa.at[n, core, opposite, pl.ds(0, 16), :]
        high = xa.at[n, core, opposite, pl.ds(16, 16), :]
        a = remote(low, low, fs, fr.at[0, n], right_dev)
        b = remote(high, high, fs, fr.at[1, n], left_dev)
        return a, b

    def core_send(n, place):
        block = xa.at[n, core, place]
        remote(block, block, acs, acr.at[n], other_dev).start()

    def core_arrival(n):
        half = xa.at[n, 1 - core]
        return remote(half, half, acs, acr.at[n], other_dev)

    def near_send(n):
        for copy in near_in(n):
            copy.start()
        core_send(n, x)

    def wait_rows():
        whole(xb1, 7, b1s, b1r).wait_recv()

    def send_b2(k):
        i, start, width = B_PARTS[k]
        bpack, xbh = bpacks[k], xbhs[k]
        lane = iota((256, 128), 1)
        pick = jnp.where(((lane & 15) >> 2) == core * 2 + i, pack_b, 0.0).astype(BF16)
        piece = xb1[:, :, start : start + width].reshape(128, width)
        bpack[...] = dot(pick, piece).astype(BF16).reshape(16, 16, width)
        xbh[core, me] = bpack[me]
        for dy, dz in PLANE:
            peer, device = plane(dy * 4 + dz)
            remote(bpack.at[peer], xbh.at[core, me], b2s.at[k], b2r.at[k], device).start()

    arrive_a(0)
    near_send(0)
    wait_rows()
    send_b2(0)
    arrive_a(1)
    near_send(1)
    send_b2(1)
    accg[...] = jnp.zeros((HIDDEN, 256), F32)
    accu[...] = jnp.zeros((HIDDEN, 256), F32)
    pltpu.make_async_copy(wg_hbm.at[0], wg, local_sem.at[2]).wait()
    pltpu.make_async_copy(wu_hbm.at[0], wu, local_sem.at[3]).wait()

    def project(value, offset):
        cols = pl.ds(offset, value.shape[1])
        accg[...] += dot_nt(wg[:, cols], value)
        accu[...] += dot_nt(wu[:, cols], value)

    def project_a(n):
        core_arrival(n).wait_recv()
        project(xa[n].reshape(256, CHUNK), n * CHUNK)

    def relay(n):
        for arrival, send, place in zip(near_arrivals(n), far_sends(n), (left, right)):
            arrival.wait_recv()
            send.start()
            core_send(n, place)

    def forward(n):
        for copy in far_arrivals(n):
            copy.wait_recv()
        core_send(n, opposite)

    def b2_core(k, half):
        block = xbhs[k].at[half]
        return remote(block, block, bcs.at[k], bcr.at[k], other_dev)

    def forward_b(k):
        whole(xbhs[k].at[core], 15, b2s.at[k], b2r.at[k]).wait_recv()
        b2_core(k, core).start()

    tau = rr >> 5
    unpack_b = onehot(
        ll == ((rr & 31) >> 1) * 16 + ((tau & 3) * 2 + (tau >> 2)) * 2 + (rr & 1)
    )

    def project_b(half, k):
        i, start, width = B_PARTS[k]
        offset = pl.multiple_of(IN_A + half * 2 * PIECE + i * PIECE + start, 256)
        project(dot(unpack_b, xbhs[k][half].reshape(256, width)).astype(BF16), offset)

    def project_own(k):
        project_b(core, k)

    def project_other(k):
        b2_core(k, 1 - core).wait_recv()
        project_b(1 - core, k)

    relay(0)
    near_send(2)
    send_b2(2)
    relay(1)
    forward_b(0)
    project_own(0)
    forward(0)
    relay(2)
    forward_b(1)
    project_other(0)
    project_own(1)
    forward(1)
    project_a(0)
    project_other(1)
    forward(2)
    project_a(1)
    forward_b(2)
    project_own(2)
    project_a(2)
    project_other(2)
    g = accg[...]
    hidden = (g * jax.nn.sigmoid(g) * accu[...]).astype(BF16)
    hid[...] = dot_nt(onehot(rr == ll), hidden).astype(BF16)
    t_of = (rr & 15) >> 1
    to_b = onehot(ll == ((t_of & 1) * 4 + (t_of >> 1)) * 32 + (rr >> 4) * 2 + (rr & 1))
    pltpu.make_async_copy(wd_hbm.at[0], wd, local_sem.at[4]).wait()

    def drain():
        whole(xb1, 7, b1s, b1r).wait_send()
        whole(arecv0, 15, a1s.at[0], a1r.at[0]).wait_send()
        whole(arecv1, 15, a1s.at[1], a1r.at[1]).wait_send()
        for k in range(3):
            whole(xbhs[k].at[core], 15, b2s.at[k], b2r.at[k]).wait_send()
            b2_core(k, core).wait_send()
        sent = xa.at[0:IN_CHUNKS, 0, 0:2]
        remote(sent, sent, ns, nr.at[0, 0], other_dev).wait_send()
        sent = xa.at[0:IN_CHUNKS, 0, 0]
        remote(sent, sent, fs, fr.at[0, 0], other_dev).wait_send()
        sent = xa.at[0:IN_CHUNKS, 0]
        remote(sent, sent, acs, acr.at[0], other_dev).wait_send()
        remote(cr, cr, rcs, rcr.at[0], other_dev).wait_send()
        b_core().wait_send()
        whole(bback, 15, rbs, rbr).wait_send()
        remote(far, far, rfs, rfr.at[0, 0], other_dev).wait_send()
        remote(near, near, rns, rnr.at[0, 0], other_dev).wait_send()
        whole(frecv, 7, rfis, rfir).wait_send()

    def down_a(n):
        y = dot(hid[...], wd[:, n * CHUNK : (n + 1) * CHUNK])
        pa[n] = y.astype(BF16).reshape(2, 128, CHUNK)
        pm[n] = jnp.where(core == 0, y[:128], y[128:])
        remote(pa.at[n, 1 - core], cr.at[n], rcs, rcr.at[n], other_dev).start()

    def chip_sum(n):
        remote(pa.at[n, 1 - core], cr.at[n], rcs, rcr.at[n], other_dev).wait_recv()
        both = pm[n] + cr[n].astype(F32)
        pm[n] = both
        cs[n] = both.astype(BF16).reshape(4, 32, CHUNK)
        for copy in ret_far(n):
            copy.start()

    def ret_far(n):
        a = remote(
            cs.at[n, opposite, pl.ds(0, 16), :], far.at[0, n], rfs, rfr.at[0, n], right_dev
        )
        b = remote(
            cs.at[n, opposite, pl.ds(16, 16), :], far.at[1, n], rfs, rfr.at[1, n], left_dev
        )
        return a, b

    def ret_near(n):
        a = remote(cs.at[n, right], near.at[0, n], rns, rnr.at[0, n], right_dev)
        b = remote(cs.at[n, left], near.at[1, n], rns, rnr.at[1, n], left_dev)
        return a, b

    def ret_relay(n):
        for copy in ret_far(n):
            copy.wait_recv()
        to_right = pl.ds(pl.multiple_of(right * 32, 32), 16)
        to_left = pl.ds(pl.multiple_of(left * 32 + 16, 16), 16)
        cs[n, right, 0:16, :] = (pm[n, to_right, :] + far[0, n].astype(F32)).astype(BF16)
        cs[n, left, 16:32, :] = (pm[n, to_left, :] + far[1, n].astype(F32)).astype(BF16)
        for copy in ret_near(n):
            copy.start()

    def ret_sum(n):
        for copy in ret_near(n):
            copy.wait_recv()
        rows = pl.ds(pl.multiple_of(x * 32, 32), 32)
        y = pm[n, rows, :] + near[0, n].astype(F32) + near[1, n].astype(F32)
        y = y.astype(BF16)
        for q in range(4):
            row = ((n % 2) * 4 + q) * 32
            y2[n // 2, row : row + 32, :] = y[:, q * 256 : q * 256 + 256]

    def b_core():
        return remote(pbs, cbr, rbcs, rbcr, other_dev)

    def down_b(half):
        cols = pl.ds(pl.multiple_of(A_COLS + half * CHUNK, CHUNK), CHUNK)
        return dot(hidb[...], wd[:, cols])

    def b_other():
        hidb[...] = dot_nt(to_b, hidden).astype(BF16)
        pbs[...] = down_b(1 - core).astype(BF16)
        b_core().start()

    def b_mine():
        pbm[...] = down_b(core)

    def b_home():
        b_core().wait_recv()
        bsend[...] = (pbm[...] + cbr[...].astype(F32)).astype(BF16).reshape(16, 16, CHUNK)
        bback[me] = bsend[me]
        for dy, dz in PLANE:
            peer, device = plane(dy * 4 + dz)
            remote(bsend.at[peer], bback.at[me], rbs, rbr, device).start()

    rr = iota((256, 256), 0)
    ll = iota((256, 256), 1)
    repack_a = onehot(ll == (rr & 7) * 32 + (rr >> 3))

    def a_home(h):
        asend[h] = dot(repack_a, y2[h]).astype(BF16).reshape(16, 16, 256)
        aback[h, me] = asend[h, me]
        for dy, dz in PLANE:
            peer, device = plane(dy * 4 + dz)
            remote(asend.at[h, peer], aback.at[h, me], ras.at[h], rar.at[h], device).start()

    b_other()
    down_a(0)
    down_a(1)
    b_mine()
    chip_sum(0)
    down_a(2)
    chip_sum(1)
    b_home()
    down_a(3)
    chip_sum(2)
    chip_sum(3)
    ret_relay(0)
    ret_relay(1)
    ret_relay(2)
    ret_relay(3)
    ret_sum(0)
    ret_sum(1)
    a_home(0)
    ret_sum(2)

    rr = iota((128, 256), 0)
    ll = iota((128, 256), 1)
    wide_hi = dot_nt(dot_nt(wide, whi).astype(BF16), spread_b)
    wide_lo = dot_nt(dot_nt(wide, wlo).astype(BF16), spread_b)

    whole(bback, 15, rbs, rbr).wait_recv()
    partial = jnp.zeros((128, 256), F32)
    for q in range(4):
        keep = ((rr >> 4) == ((ll & 15) >> 1)) & (((rr & 15) >> 2) == q)
        piece = bback[:, :, q * 256 : q * 256 + 256].reshape(256, 256)
        partial = partial + dot(jnp.where(keep, wide_hi, 0.0).astype(BF16), piece)
        partial = partial + dot(jnp.where(keep, wide_lo, 0.0).astype(BF16), piece)
    fsend[...] = partial.astype(BF16).reshape(8, 16, 256)
    frecv[tp] = fsend[tp]

    def send_b4(step, carry):
        peer, device = column(step)
        remote(fsend.at[peer], frecv.at[tp], rfis, rfir, device).start()
        return carry

    lax.fori_loop(1, 8, send_b4, 0)
    ret_sum(3)
    a_home(1)
    whole(frecv, 7, rfis, rfir).wait_recv()
    rr = iota((64, 128), 0)
    ll = iota((64, 128), 1)
    gather = onehot(
        ((rr >> 5) == ((ll >> 4) & 1))
        & (((rr >> 3) & 3) == ((ll & 15) >> 2))
        & ((rr & 7) == (ll & 3))
    )
    home_b = dot(gather, frecv[...].reshape(128, 256))
    for piece in range(8):
        start = A_COLS + piece * 256
        out[:, start : start + 256] = (
            stream[0:4, start : start + 256] + home_b[piece * 8 : piece * 8 + 4, :]
        ).astype(BF16)

    rr = iota((64, 256), 0)
    ll = iota((64, 256), 1)
    keep = (rr >> 3) == (ll & 7)
    home_hi = dot_nt(dot_nt(mine, whi).astype(BF16), spread_a)
    home_lo = dot_nt(dot_nt(mine, wlo).astype(BF16), spread_a)
    home_hi = jnp.where(keep, home_hi, 0.0).astype(BF16)
    home_lo = jnp.where(keep, home_lo, 0.0).astype(BF16)

    drain()
    for h in range(2):
        whole(aback.at[h], 15, ras.at[h], rar.at[h]).wait_recv()
        back = aback[h].reshape(256, 256)
        home_a = dot(home_hi, back) + dot(home_lo, back)
        for p in range(8):
            cols = slice(h * 2048 + p * 256, h * 2048 + p * 256 + 256)
            out[:, cols] = (stream[0:4, cols] + home_a[p * 8 : p * 8 + 4, :]).astype(BF16)
    for h in range(2):
        whole(aback.at[h], 15, ras.at[h], rar.at[h]).wait_send()


def layer(
    resid,
    query,
    key_cache,
    value_cache,
    new_key,
    new_value,
    cache_len,
    norm_gain,
    routes,
    gate_fixed,
    w_gate,
    w_up,
    w_down,
):
    vmem = pl.BlockSpec(memory_space=pltpu.VMEM)
    anywhere = pl.BlockSpec(memory_space=pl.ANY)
    dma = pltpu.SemaphoreType.DMA
    n = A_CHUNKS
    scratch = [
        pltpu.SMEM((ROWS,), jnp.int32),
        pltpu.VMEM((ROWS, D), BF16),
        pltpu.VMEM((ROWS, D), BF16),
        pltpu.VMEM((ROWS, 1024), BF16),
        pltpu.VMEM((ROWS, 1024), BF16),
        pltpu.VMEM((1, D), F32),
        pltpu.VMEM((4, 32), jnp.int32),
        pltpu.VMEM((4, 32), jnp.int32),
        pltpu.VMEM((ROWS, LENGTH, 1024), BF16),
        pltpu.VMEM((ROWS, LENGTH, 1024), BF16),
        pltpu.VMEM((HIDDEN, D), BF16),
        pltpu.VMEM((HIDDEN, D), BF16),
        pltpu.VMEM((HIDDEN, D), BF16),
        pltpu.VMEM((HEADS * ROWS, 128), F32),
        pltpu.VMEM((HEADS * ROWS, 128), F32),
        pltpu.VMEM((GROUP * ROWS, 1024), F32),
        pltpu.VMEM((GROUP * ROWS, 1024), F32),
        pltpu.VMEM((HEADS * ROWS, 128), F32),
        pltpu.VMEM((8, D), F32),
        pltpu.VMEM((64, 128), F32),
        pltpu.VMEM((64, 256), F32),
        pltpu.VMEM((32, PIECE), F32),
        pltpu.VMEM((16, 16, 128), BF16),
        pltpu.VMEM((16, 16, 256), BF16),
        pltpu.VMEM((16, 16, 128), BF16),
        pltpu.VMEM((16, 16, 256), BF16),
        pltpu.VMEM((16, PIECE), BF16),
        pltpu.VMEM((8, 16, PIECE), BF16),
        *[pltpu.VMEM((16, 16, width), BF16) for _, _, width in B_PARTS],
        *[pltpu.VMEM((2, 16, 16, width), BF16) for _, _, width in B_PARTS],
        pltpu.VMEM((IN_CHUNKS, 2, 4, 32, CHUNK), BF16),
        pltpu.VMEM((HIDDEN, 256), F32),
        pltpu.VMEM((HIDDEN, 256), F32),
        pltpu.VMEM((256, HIDDEN), BF16),
        pltpu.VMEM((256, HIDDEN), BF16),
        pltpu.VMEM((n, 2, 128, CHUNK), BF16),
        pltpu.VMEM((n, 128, CHUNK), F32),
        pltpu.VMEM((n, 128, CHUNK), BF16),
        pltpu.VMEM((n, 4, 32, CHUNK), BF16),
        pltpu.VMEM((2, n, 16, CHUNK), BF16),
        pltpu.VMEM((2, n, 32, CHUNK), BF16),
        pltpu.VMEM((2, 256, 256), BF16),
        pltpu.VMEM((2, 16, 16, 256), BF16),
        pltpu.VMEM((2, 16, 16, 256), BF16),
        pltpu.VMEM((256, CHUNK), BF16),
        pltpu.VMEM((256, CHUNK), F32),
        pltpu.VMEM((256, CHUNK), BF16),
        pltpu.VMEM((16, 16, CHUNK), BF16),
        pltpu.VMEM((16, 16, CHUNK), BF16),
        pltpu.VMEM((8, 16, 256), BF16),
        pltpu.VMEM((8, 16, 256), BF16),
        dma((13,)),
        dma((2,)),
        dma((2,)),
        dma,
        dma,
        dma((3,)),
        dma((3,)),
        dma((3,)),
        dma((3,)),
        dma,
        dma((2, n)),
        dma,
        dma((2, n)),
        dma,
        dma((n,)),
        dma,
        dma((n,)),
        dma,
        dma((2, n)),
        dma,
        dma((2, n)),
        dma((2,)),
        dma((2,)),
        dma,
        dma,
        dma,
        dma,
        dma,
        dma,
    ]
    return pl.pallas_call(
        kernel,
        out_shape=jax.ShapeDtypeStruct((ROWS, D), BF16),
        in_specs=[anywhere] * 13,
        out_specs=vmem,
        scratch_shapes=scratch,
        compiler_params=pltpu.CompilerParams(
            collective_id=0, has_side_effects=True, vmem_limit_bytes=60 * 1024 * 1024
        ),
        cost_estimate=pl.CostEstimate(
            flops=2 * 3 * 256 * HIDDEN * D, bytes_accessed=27 * 1024 * 1024, transcendentals=0
        ),
    )(
        cache_len,
        resid,
        query,
        new_key,
        new_value,
        norm_gain.reshape(1, D),
        routes.T,
        gate_fixed.T,
        key_cache,
        value_cache,
        w_gate,
        w_up,
        w_down,
    )


def solution(mesh):
    placed = (
        P(("side", "expert", "tp"), None),
        P(("side", "expert", "tp"), None),
        P(("side", "expert", "tp"), None, None),
        P(("side", "expert", "tp"), None, None),
        P(("side", "expert", "tp"), None),
        P(("side", "expert", "tp"), None),
        P(("side", "expert", "tp")),
        P(),
        P(("side", "expert"), None),
        P(("side", "expert"), None),
        P(("side", "expert"), "tp", None),
        P(("side", "expert"), "tp", None),
        P(("side", "expert"), "tp", None),
    )
    return jax.shard_map(
        layer,
        mesh=mesh,
        in_specs=placed,
        out_specs=P(("side", "expert", "tp"), None),
        check_vma=False,
    )
```

```python
import functools

import jax
import jax.numpy as jnp
from jax import lax
from jax.experimental import pallas as pl
from jax.experimental.pallas import tpu as pltpu
from jax.sharding import PartitionSpec as P

D = 6144
HEADS = 48
KV_HEADS = 8
HEAD_DIM = 128
GROUP = HEADS // KV_HEADS
ROWS = 4
LENGTH = 128
HIDDEN = 672
CHUNK = 1024
IN_CHUNKS = 3
IN_A = IN_CHUNKS * CHUNK
IN_PARTS = ((0, 1), (1, 2))
PIECE = (D - IN_A) // 4
B_PARTS = ((0, 0, 256), (0, 256, 512), (1, 0, 768))
A_CHUNKS = 4
A_COLS = A_CHUNKS * CHUNK
OUT_PARTS = ((0, 2), (2, 1), (3, 1))
F32 = jnp.float32
BF16 = jnp.bfloat16
MESH = pl.DeviceIdType.MESH
W_PARTS = 3
W_ROWS = HIDDEN // W_PARTS
PLANE = ((1, 0), (0, 1), (3, 0), (0, 3), (1, 1), (3, 3), (1, 3), (3, 1), (2, 0), (0, 2), (2, 1), (1, 2), (2, 3), (3, 2), (2, 2))


def iota(shape, dim):
    return lax.broadcasted_iota(jnp.int32, shape, dim)


def dot(a, b):
    return lax.dot_general(a, b, (((1,), (0,)), ((), ())), preferred_element_type=F32)


def dot_nt(a, b):
    return lax.dot_general(a, b, (((1,), (1,)), ((), ())), preferred_element_type=F32)


def onehot(condition):
    return jnp.where(condition, 1.0, 0.0).astype(BF16)


def remote(src, dst, send_sem, recv_sem, device):
    return pltpu.make_async_remote_copy(
        src_ref=src,
        dst_ref=dst,
        send_sem=send_sem,
        recv_sem=recv_sem,
        device_id=device,
        device_id_type=MESH,
    )


def kernel(
    clen_hbm,
    resid_hbm,
    query_hbm,
    new_key_hbm,
    new_value_hbm,
    gain_hbm,
    routes_hbm,
    gates_hbm,
    key_hbm,
    value_hbm,
    wg_hbm,
    wu_hbm,
    wd_hbm,
    out,
    clen,
    resid,
    query,
    new_key,
    new_value,
    gain,
    routes,
    gates,
    kbuf,
    vbuf,
    wg,
    wu,
    wd,
    qs,
    scores,
    own_key,
    own_value,
    heads_out,
    stream,
    xsa0,
    xsa1,
    xsb,
    apack0,
    apack1,
    arecv0,
    arecv1,
    bmsg,
    xb1,
    bpack0,
    bpack1,
    bpack2,
    xbh0,
    xbh1,
    xbh2,
    xa,
    accg,
    accu,
    hid,
    hidb,
    pa,
    pm,
    cr,
    cs,
    far,
    near,
    y20,
    y21,
    y22,
    asend0,
    asend1,
    asend2,
    aback0,
    aback1,
    aback2,
    pbs,
    pbm,
    cbr,
    bsend,
    bback,
    fsend,
    frecv,
    mix_a,
    mix_b,
    gather,
    local_sem,
    a1s,
    a1r,
    b1s,
    b1r,
    b2s,
    b2r,
    bcs,
    bcr,
    ns,
    nr,
    fs,
    fr,
    acs,
    acr,
    rcs,
    rcr,
    rfs,
    rfr,
    rns,
    rnr,
    ras,
    rar,
    rbcs,
    rbcr,
    rbs,
    rbr,
    rfis,
    rfir,
):
    side = lax.axis_index("side")
    expert = lax.axis_index("expert")
    tp = lax.axis_index("tp")
    me = side * 8 + expert
    my_y = me // 4
    my_z = me % 4
    x = tp // 2
    core = tp % 2
    right = lax.rem(x + 1, 4)
    left = lax.rem(x + 3, 4)
    opposite = lax.rem(x + 2, 4)
    other_dev = (side, expert, x * 2 + 1 - core)
    right_dev = (side, expert, right * 2 + core)
    left_dev = (side, expert, left * 2 + core)

    def plane(step):
        y = lax.rem(my_y + step // 4, 4)
        z = lax.rem(my_z + step % 4, 4)
        peer = y * 4 + z
        return peer, (peer // 8, peer % 8, tp)

    def column(step):
        peer = lax.rem(tp + step, 8)
        return peer, (side, expert, peer)

    def whole(buffer, count, send_sem, recv_sem):
        part = buffer.at[pl.ds(0, count)]
        return remote(part, part, send_sem, recv_sem, other_dev)

    bpacks = (bpack0, bpack1, bpack2)
    y2s = (y20, y21, y22)
    asends = (asend0, asend1, asend2)
    abacks = (aback0, aback1, aback2)
    xbhs = (xbh0, xbh1, xbh2)
    barrier = pltpu.get_barrier_semaphore()

    def greet_plane(step, carry):
        pl.semaphore_signal(barrier, inc=1, device_id=plane(step)[1], device_id_type=MESH)
        return carry

    def greet_column(step, carry):
        pl.semaphore_signal(barrier, inc=1, device_id=column(step)[1], device_id_type=MESH)
        return carry

    small_copies = [
        pltpu.make_async_copy(src, dst, local_sem.at[5 + number])
        for number, (src, dst) in enumerate(
            (
                (query_hbm, query),
                (new_key_hbm, new_key),
                (new_value_hbm, new_value),
                (routes_hbm, routes),
                (gates_hbm, gates),
                (clen_hbm, clen),
                (resid_hbm, resid),
                (gain_hbm, gain),
            )
        )
    ]
    for copy in small_copies[:6]:
        copy.start()
    key_copy = pltpu.make_async_copy(key_hbm, kbuf, local_sem.at[0])
    value_copy = pltpu.make_async_copy(value_hbm, vbuf, local_sem.at[1])
    key_copy.start()
    value_copy.start()
    for copy in small_copies[6:]:
        copy.start()
    lax.fori_loop(1, 16, greet_plane, 0)
    lax.fori_loop(1, 8, greet_column, 0)
    weight_copies = []
    for number, (src, dst) in enumerate(((wg_hbm, wg), (wu_hbm, wu), (wd_hbm, wd))):
        for part in range(W_PARTS):
            rows = pl.ds(part * W_ROWS, W_ROWS)
            weight_copies.append(
                pltpu.make_async_copy(
                    src.at[0, rows, :],
                    dst.at[rows, :],
                    local_sem.at[2 + number],
                )
            )
    for copy in weight_copies:
        copy.start()

    for copy in small_copies[:3]:
        copy.wait()
    q32 = query[...].astype(F32)
    for head in range(HEADS):
        qs[head * 4 : head * 4 + 4, :] = q32[:, head * 128 : head * 128 + 128]
    nk32 = new_key[...].astype(F32)
    nv32 = new_value[...].astype(F32)
    for copy_no in range(GROUP):
        own_key[copy_no * 4 : copy_no * 4 + 4, :] = nk32
        own_value[copy_no * 4 : copy_no * 4 + 4, :] = nv32
    for copy in small_copies[3:6]:
        copy.wait()
    lane32 = iota((32, 32), 1)
    row32 = iota((32, 32), 0)
    fixed = gates[...].astype(F32)
    weights = fixed / jnp.sum(fixed, axis=0, keepdims=True)
    chosen = jnp.zeros((32, 32), F32)
    weighted = jnp.zeros((32, 32), F32)
    route = routes[...]
    for k in range(4):
        same = route[k : k + 1, :] == (row32 >> 1)
        chosen = chosen + jnp.where(same, 1.0, 0.0)
        weighted = weighted + jnp.where(same, weights[k : k + 1, :], 0.0)
    earlier = onehot(((row32 >> 2) == (lane32 >> 2)) & (row32 < lane32))
    before = dot(chosen.astype(BF16), earlier)
    picked = (chosen > 0.5) & (jnp.abs(before - (row32 & 1).astype(F32)) < 0.5)
    sel = onehot(picked)
    wsel = jnp.where(picked, weighted, 0.0)
    whi = wsel.astype(BF16)
    wlo = (wsel - whi.astype(F32)).astype(BF16)

    rr = iota((256, 32), 0)
    ll = iota((256, 32), 1)
    spread_a = onehot((rr >> 3) == ll)
    spread_b = onehot(ll == ((rr >> 4) * 2 + (rr & 1)))
    rr = iota((64, 32), 0)
    ll = iota((64, 32), 1)
    mine = onehot((ll == tp * 4 + (rr & 7)) & ((rr & 7) < 4))
    rr = iota((128, 32), 0)
    ll = iota((128, 32), 1)
    wide = onehot(ll == ((rr >> 4) * 4 + (rr & 3)))
    pack_a = dot_nt(spread_a, dot_nt(mine, sel).astype(BF16))
    rr = iota((256, 64), 0)
    ll = iota((256, 64), 1)
    pack_a = jnp.where((rr & 7) == (ll >> 3), pack_a, 0.0).astype(BF16)
    rr = iota((16, 32), 0)
    ll = iota((16, 32), 1)
    pack_b1 = onehot(ll == (rr >> 2) * 8 + (rr & 3))
    pack_b = dot_nt(spread_b, dot_nt(wide, sel).astype(BF16))
    rr = iota((256, 128), 0)
    ll = iota((256, 128), 1)
    pack_b = jnp.where(((rr & 15) >> 1) == (ll >> 4), pack_b, 0.0)

    block = GROUP * ROWS
    row_of = iota((block, 128), 0) & 3
    key_copy.wait()
    for j in range(KV_HEADS):
        qj = qs[j * block : (j + 1) * block, :].astype(BF16)
        total = jnp.zeros((block, 128), F32)
        for r in range(ROWS):
            part = dot_nt(qj, kbuf[r, :, j * 128 : (j + 1) * 128])
            total = jnp.where(row_of == r, part, total)
        scores[j * block : (j + 1) * block, :] = total

    pos = iota((HEADS * ROWS, 128), 1)
    row_all = iota((HEADS * ROWS, 128), 0) & 3
    limit = jnp.zeros((HEADS * ROWS, 128), jnp.int32)
    for r in range(ROWS):
        limit = jnp.where(row_all == r, clen[r], limit)
    scale = 1.0 / HEAD_DIM**0.5
    s = jnp.where(pos < limit, scores[...] * scale, -1e30)
    own = jnp.concatenate(
        [
            jnp.sum(
                qs[j * block : (j + 1) * block, :] * own_key[:, j * 128 : (j + 1) * 128],
                axis=-1,
                keepdims=True,
            )
            for j in range(KV_HEADS)
        ],
        axis=0,
    )
    own = own * scale
    top = jnp.maximum(jnp.max(s, axis=-1, keepdims=True), own)
    expo = jnp.exp(s - top)
    expo_own = jnp.exp(own - top)
    total = jnp.sum(expo, axis=-1, keepdims=True) + expo_own
    scores[...] = expo / total
    prob_own = (expo_own / total).astype(BF16).astype(F32)
    value_copy.wait()
    for j in range(KV_HEADS):
        pj = scores[j * block : (j + 1) * block, :]
        acc = prob_own[j * block : (j + 1) * block, :] * own_value[:, j * 128 : (j + 1) * 128]
        for r in range(ROWS):
            pr = jnp.where(row_of == r, pj, 0.0).astype(BF16)
            acc = acc + dot(pr, vbuf[r, :, j * 128 : (j + 1) * 128])
        heads_out[j * block : (j + 1) * block, :] = acc
    for copy in small_copies[6:]:
        copy.wait()
    stream[...] = jnp.zeros((8, D), F32)
    for head in range(HEADS):
        cols = slice(head * 128, head * 128 + 128)
        stream[0:4, cols] = resid[:, cols].astype(F32) + heads_out[head * 4 : head * 4 + 4, :]
    st = stream[...]
    mean = jnp.sum(st, axis=-1, keepdims=True) * (1.0 / D)
    centred = st - mean
    variance = jnp.sum(centred * centred, axis=-1, keepdims=True) * (1.0 / D)
    normed = centred * lax.rsqrt(variance + 1e-05) * gain[...]
    for xs, (first, chunks) in zip((xsa0, xsa1), IN_PARTS):
        width = chunks * CHUNK // 8
        for p in range(8):
            start = first * CHUNK + p * width
            xs[p * 8 : p * 8 + 8, :] = normed[:, start : start + width]
    for p in range(4):
        start = IN_A + p * PIECE
        xsb[p * 8 : p * 8 + 8, :] = normed[:, start : start + PIECE]

    bm = dot(pack_b1, xsb[...].astype(BF16)).astype(BF16)
    bmsg[...] = bm
    xb1[tp] = bm
    pl.semaphore_wait(barrier, 22)

    def send_b1(step, carry):
        peer, device = column(step)
        remote(bmsg, xb1.at[tp], b1s, b1r, device).start()
        return carry

    lax.fori_loop(1, 8, send_b1, 0)
    for h, (xs, apack, arecv) in enumerate(((xsa0, apack0, arecv0), (xsa1, apack1, arecv1))):
        packed = dot(pack_a, xs[...].astype(BF16)).astype(BF16)
        apack[...] = packed.reshape(16, 16, packed.shape[1])
        arecv[me] = apack[me]
        for dy, dz in PLANE:
            peer, device = plane(dy * 4 + dz)
            remote(apack.at[peer], arecv.at[me], a1s.at[h], a1r.at[h], device).start()

    rr = iota((256, 256), 0)
    ll = iota((256, 256), 1)
    unpack_a = onehot(ll == (rr & 31) * 8 + (rr >> 5))

    def arrive_a(h):
        arecv = (arecv0, arecv1)[h]
        first, chunks = IN_PARTS[h]
        width = chunks * CHUNK // 8
        whole(arecv, 15, a1s.at[h], a1r.at[h]).wait_recv()
        got = dot(unpack_a, arecv[...].reshape(256, width)).astype(BF16)
        for p in range(8):
            n, start = divmod(p * width, CHUNK)
            xa[first + n, core, x, :, start : start + width] = got[p * 32 : p * 32 + 32, :]

    def near_in(n):
        mine_ref = xa.at[n, core, x]
        to_right = remote(mine_ref, mine_ref, ns, nr.at[0, n], right_dev)
        to_left = remote(mine_ref, mine_ref, ns, nr.at[1, n], left_dev)
        return to_right, to_left

    def near_arrivals(n):
        from_left = xa.at[n, core, left]
        from_right = xa.at[n, core, right]
        a = remote(from_left, from_left, ns, nr.at[0, n], right_dev)
        b = remote(from_right, from_right, ns, nr.at[1, n], left_dev)
        return a, b

    def far_sends(n):
        low = xa.at[n, core, left, pl.ds(0, 16), :]
        high = xa.at[n, core, right, pl.ds(16, 16), :]
        a = remote(low, low, fs, fr.at[0, n], right_dev)
        b = remote(high, high, fs, fr.at[1, n], left_dev)
        return a, b

    def far_arrivals(n):
        low = xa.at[n, core, opposite, pl.ds(0, 16), :]
        high = xa.at[n, core, opposite, pl.ds(16, 16), :]
        a = remote(low, low, fs, fr.at[0, n], right_dev)
        b = remote(high, high, fs, fr.at[1, n], left_dev)
        return a, b

    def core_send(n, place):
        block = xa.at[n, core, place]
        remote(block, block, acs, acr.at[n], other_dev).start()

    def core_arrival(n):
        half = xa.at[n, 1 - core]
        return remote(half, half, acs, acr.at[n], other_dev)

    def near_send(n):
        for copy in near_in(n):
            copy.start()
        core_send(n, x)

    def wait_rows():
        whole(xb1, 7, b1s, b1r).wait_recv()

    def send_b2(k):
        i, start, width = B_PARTS[k]
        bpack, xbh = bpacks[k], xbhs[k]
        lane = iota((256, 128), 1)
        pick = jnp.where(((lane & 15) >> 2) == core * 2 + i, pack_b, 0.0).astype(BF16)
        piece = xb1[:, :, start : start + width].reshape(128, width)
        bpack[...] = dot(pick, piece).astype(BF16).reshape(16, 16, width)
        xbh[core, me] = bpack[me]
        for dy, dz in PLANE:
            peer, device = plane(dy * 4 + dz)
            remote(bpack.at[peer], xbh.at[core, me], b2s.at[k], b2r.at[k], device).start()

    arrive_a(0)
    near_send(0)
    wait_rows()
    send_b2(0)
    arrive_a(1)
    near_send(1)
    send_b2(1)
    accg[...] = jnp.zeros((HIDDEN, 256), F32)
    accu[...] = jnp.zeros((HIDDEN, 256), F32)
    pltpu.make_async_copy(wg_hbm.at[0], wg, local_sem.at[2]).wait()
    pltpu.make_async_copy(wu_hbm.at[0], wu, local_sem.at[3]).wait()

    def project(value, offset):
        cols = pl.ds(offset, value.shape[1])
        accg[...] += dot_nt(wg[:, cols], value)
        accu[...] += dot_nt(wu[:, cols], value)

    def project_a(n):
        core_arrival(n).wait_recv()
        project(xa[n].reshape(256, CHUNK), n * CHUNK)

    def relay(n):
        for arrival, send, place in zip(near_arrivals(n), far_sends(n), (left, right)):
            arrival.wait_recv()
            send.start()
            core_send(n, place)

    def forward(n):
        for copy in far_arrivals(n):
            copy.wait_recv()
        core_send(n, opposite)

    def b2_core(k, half):
        block = xbhs[k].at[half]
        return remote(block, block, bcs.at[k], bcr.at[k], other_dev)

    def forward_b(k):
        whole(xbhs[k].at[core], 15, b2s.at[k], b2r.at[k]).wait_recv()
        b2_core(k, core).start()

    tau = rr >> 5
    unpack_b = onehot(
        ll == ((rr & 31) >> 1) * 16 + ((tau & 3) * 2 + (tau >> 2)) * 2 + (rr & 1)
    )

    def project_b(half, k):
        i, start, width = B_PARTS[k]
        offset = pl.multiple_of(IN_A + half * 2 * PIECE + i * PIECE + start, 256)
        project(dot(unpack_b, xbhs[k][half].reshape(256, width)).astype(BF16), offset)

    def project_own(k):
        project_b(core, k)

    def project_other(k):
        b2_core(k, 1 - core).wait_recv()
        project_b(1 - core, k)

    relay(0)
    near_send(2)
    send_b2(2)
    relay(1)
    forward_b(0)
    project_own(0)

    @pl.when(core == 1)
    def early():
        forward(0)
        relay(2)
        forward_b(1)

    project_other(0)

    @pl.when(core == 0)
    def late():
        forward(0)

    project_a(0)

    @pl.when(core == 0)
    def later():
        relay(2)
        forward_b(1)

    project_own(1)
    forward(1)
    project_other(1)
    project_a(1)
    forward(2)
    forward_b(2)
    project_own(2)
    project_a(2)
    project_other(2)
    g = accg[...]
    hidden = (g * jax.nn.sigmoid(g) * accu[...]).astype(BF16)
    hid[...] = dot_nt(onehot(rr == ll), hidden).astype(BF16)
    t_of = (rr & 15) >> 1
    to_b = onehot(ll == ((t_of & 1) * 4 + (t_of >> 1)) * 32 + (rr >> 4) * 2 + (rr & 1))
    pltpu.make_async_copy(wd_hbm.at[0], wd, local_sem.at[4]).wait()

    def drain():
        whole(xb1, 7, b1s, b1r).wait_send()
        whole(arecv0, 15, a1s.at[0], a1r.at[0]).wait_send()
        whole(arecv1, 15, a1s.at[1], a1r.at[1]).wait_send()
        for k in range(3):
            whole(xbhs[k].at[core], 15, b2s.at[k], b2r.at[k]).wait_send()
            b2_core(k, core).wait_send()
        sent = xa.at[0:IN_CHUNKS, 0, 0:2]
        remote(sent, sent, ns, nr.at[0, 0], other_dev).wait_send()
        sent = xa.at[0:IN_CHUNKS, 0, 0]
        remote(sent, sent, fs, fr.at[0, 0], other_dev).wait_send()
        sent = xa.at[0:IN_CHUNKS, 0]
        remote(sent, sent, acs, acr.at[0], other_dev).wait_send()
        remote(cr, cr, rcs, rcr.at[0], other_dev).wait_send()
        b_core().wait_send()
        whole(bback, 15, rbs, rbr).wait_send()
        remote(far, far, rfs, rfr.at[0], other_dev).wait_send()
        remote(near, near, rns, rnr.at[0], other_dev).wait_send()
        whole(frecv, 7, rfis, rfir).wait_send()

    def down_a(n):
        y = dot(hid[...], wd[:, n * CHUNK : (n + 1) * CHUNK])
        pa[n] = y.astype(BF16).reshape(2, 128, CHUNK)
        pm[n] = jnp.where(core == 0, y[:128], y[128:])
        remote(pa.at[n, 1 - core], cr.at[n], rcs, rcr.at[n], other_dev).start()

    def chip_sum(n):
        remote(pa.at[n, 1 - core], cr.at[n], rcs, rcr.at[n], other_dev).wait_recv()
        both = pm[n] + cr[n].astype(F32)
        pm[n] = both
        cs[n] = both.astype(BF16).reshape(4, 32, CHUNK)
        for copy in ret_far(n):
            copy.start()

    def ret_far(n):
        a = remote(
            cs.at[n, opposite, pl.ds(0, 16), :], far.at[0, n], rfs, rfr.at[n], right_dev
        )
        b = remote(
            cs.at[n, opposite, pl.ds(16, 16), :], far.at[1, n], rfs, rfr.at[n], left_dev
        )
        return a, b

    def ret_near(n):
        a = remote(cs.at[n, right], near.at[0, n], rns, rnr.at[n], right_dev)
        b = remote(cs.at[n, left], near.at[1, n], rns, rnr.at[n], left_dev)
        return a, b

    def ret_relay(n):
        both = near.at[0, n]
        remote(both, both, rfs, rfr.at[n], right_dev).wait_recv()
        to_right = pl.ds(pl.multiple_of(right * 32, 32), 16)
        to_left = pl.ds(pl.multiple_of(left * 32 + 16, 16), 16)
        cs[n, right, 0:16, :] = (pm[n, to_right, :] + far[0, n].astype(F32)).astype(BF16)
        cs[n, left, 16:32, :] = (pm[n, to_left, :] + far[1, n].astype(F32)).astype(BF16)
        for copy in ret_near(n):
            copy.start()

    def ret_sum(n):
        both = pa.at[n, 0, 0:64]
        remote(both, both, rns, rnr.at[n], right_dev).wait_recv()
        rows = pl.ds(pl.multiple_of(x * 32, 32), 32)
        y = pm[n, rows, :] + near[0, n].astype(F32) + near[1, n].astype(F32)
        y = y.astype(BF16)
        for (first, chunks), y2 in zip(OUT_PARTS, y2s):
            if first <= n < first + chunks:
                width = chunks * CHUNK // 8
                for q in range(CHUNK // width):
                    row = ((n - first) * (CHUNK // width) + q) * 32
                    y2[row : row + 32, :] = y[:, q * width : (q + 1) * width]

    def b_core():
        return remote(pbs, cbr, rbcs, rbcr, other_dev)

    def down_b(half):
        cols = pl.ds(pl.multiple_of(A_COLS + half * CHUNK, CHUNK), CHUNK)
        return dot(hidb[...], wd[:, cols])

    def b_other():
        hidb[...] = dot_nt(to_b, hidden).astype(BF16)
        pbs[...] = down_b(1 - core).astype(BF16)
        b_core().start()

    def b_mine():
        pbm[...] = down_b(core)

    def b_home():
        b_core().wait_recv()
        bsend[...] = (pbm[...] + cbr[...].astype(F32)).astype(BF16).reshape(16, 16, CHUNK)
        bback[me] = bsend[me]
        for dy, dz in PLANE:
            peer, device = plane(dy * 4 + dz)
            remote(bsend.at[peer], bback.at[me], rbs, rbr, device).start()

    rr = iota((256, 256), 0)
    ll = iota((256, 256), 1)
    repack_a = onehot(ll == (rr & 7) * 32 + (rr >> 3))

    def a_home(h):
        asend, aback = asends[h], abacks[h]
        value = dot(repack_a, y2s[h][...]).astype(BF16)
        asend[...] = value.reshape(16, 16, value.shape[1])
        aback[me] = asend[me]
        for dy, dz in PLANE:
            peer, device = plane(dy * 4 + dz)
            remote(asend.at[peer], aback.at[me], ras.at[h], rar.at[h], device).start()

    def home_tables():
        rr = iota((128, 256), 0)
        ll = iota((128, 256), 1)
        wide_hi = dot_nt(dot_nt(wide, whi).astype(BF16), spread_b)
        wide_lo = dot_nt(dot_nt(wide, wlo).astype(BF16), spread_b)
        for q in range(4):
            keep = ((rr >> 4) == ((ll & 15) >> 1)) & (((rr & 15) >> 2) == q)
            mix_b[2 * q] = jnp.where(keep, wide_hi, 0.0).astype(BF16)
            mix_b[2 * q + 1] = jnp.where(keep, wide_lo, 0.0).astype(BF16)
        rr = iota((64, 256), 0)
        ll = iota((64, 256), 1)
        keep = (rr >> 3) == (ll & 7)
        home_hi = dot_nt(dot_nt(mine, whi).astype(BF16), spread_a)
        home_lo = dot_nt(dot_nt(mine, wlo).astype(BF16), spread_a)
        mix_a[0] = jnp.where(keep, home_hi, 0.0).astype(BF16)
        mix_a[1] = jnp.where(keep, home_lo, 0.0).astype(BF16)
        rr = iota((64, 128), 0)
        ll = iota((64, 128), 1)
        gather[...] = onehot(
            ((rr >> 5) == ((ll >> 4) & 1))
            & (((rr >> 3) & 3) == ((ll & 15) >> 2))
            & ((rr & 7) == (ll & 3))
        )

    down_a(0)
    b_other()
    down_a(1)
    chip_sum(0)
    b_mine()
    down_a(2)
    chip_sum(1)
    down_a(3)
    b_home()
    chip_sum(2)
    chip_sum(3)
    ret_relay(0)
    ret_relay(1)
    ret_relay(2)
    ret_relay(3)
    home_tables()
    ret_sum(0)
    ret_sum(1)
    a_home(0)
    ret_sum(2)
    a_home(1)

    whole(bback, 15, rbs, rbr).wait_recv()
    partial = jnp.zeros((128, 256), F32)
    for q in range(4):
        piece = bback[:, :, q * 256 : q * 256 + 256].reshape(256, 256)
        partial = partial + dot(mix_b[2 * q], piece) + dot(mix_b[2 * q + 1], piece)
    fsend[...] = partial.astype(BF16).reshape(8, 16, 256)
    frecv[tp] = fsend[tp]

    def send_b4(step, carry):
        peer, device = column(step)
        remote(fsend.at[peer], frecv.at[tp], rfis, rfir, device).start()
        return carry

    lax.fori_loop(1, 8, send_b4, 0)
    ret_sum(3)
    a_home(2)
    drain()

    def finish_a(h):
        first, chunks = OUT_PARTS[h]
        width = chunks * CHUNK // 8
        whole(abacks[h], 15, ras.at[h], rar.at[h]).wait_recv()
        back = abacks[h][...].reshape(256, width)
        home_a = dot(mix_a[0], back) + dot(mix_a[1], back)
        for p in range(8):
            start = first * CHUNK + p * width
            cols = slice(start, start + width)
            out[:, cols] = (stream[0:4, cols] + home_a[p * 8 : p * 8 + 4, :]).astype(BF16)

    finish_a(0)
    finish_a(1)
    whole(frecv, 7, rfis, rfir).wait_recv()
    home_b = dot(gather[...], frecv[...].reshape(128, 256))
    for piece in range(8):
        start = A_COLS + piece * 256
        out[:, start : start + 256] = (
            stream[0:4, start : start + 256] + home_b[piece * 8 : piece * 8 + 4, :]
        ).astype(BF16)
    finish_a(2)
    for h, aback in enumerate(abacks):
        whole(aback, 15, ras.at[h], rar.at[h]).wait_send()


def layer(
    resid,
    query,
    key_cache,
    value_cache,
    new_key,
    new_value,
    cache_len,
    norm_gain,
    routes,
    gate_fixed,
    w_gate,
    w_up,
    w_down,
):
    vmem = pl.BlockSpec(memory_space=pltpu.VMEM)
    anywhere = pl.BlockSpec(memory_space=pl.ANY)
    dma = pltpu.SemaphoreType.DMA
    n = A_CHUNKS
    scratch = [
        pltpu.SMEM((ROWS,), jnp.int32),
        pltpu.VMEM((ROWS, D), BF16),
        pltpu.VMEM((ROWS, D), BF16),
        pltpu.VMEM((ROWS, 1024), BF16),
        pltpu.VMEM((ROWS, 1024), BF16),
        pltpu.VMEM((1, D), F32),
        pltpu.VMEM((4, 32), jnp.int32),
        pltpu.VMEM((4, 32), jnp.int32),
        pltpu.VMEM((ROWS, LENGTH, 1024), BF16),
        pltpu.VMEM((ROWS, LENGTH, 1024), BF16),
        pltpu.VMEM((HIDDEN, D), BF16),
        pltpu.VMEM((HIDDEN, D), BF16),
        pltpu.VMEM((HIDDEN, D), BF16),
        pltpu.VMEM((HEADS * ROWS, 128), F32),
        pltpu.VMEM((HEADS * ROWS, 128), F32),
        pltpu.VMEM((GROUP * ROWS, 1024), F32),
        pltpu.VMEM((GROUP * ROWS, 1024), F32),
        pltpu.VMEM((HEADS * ROWS, 128), F32),
        pltpu.VMEM((8, D), F32),
        pltpu.VMEM((64, 128), F32),
        pltpu.VMEM((64, 256), F32),
        pltpu.VMEM((32, PIECE), F32),
        pltpu.VMEM((16, 16, 128), BF16),
        pltpu.VMEM((16, 16, 256), BF16),
        pltpu.VMEM((16, 16, 128), BF16),
        pltpu.VMEM((16, 16, 256), BF16),
        pltpu.VMEM((16, PIECE), BF16),
        pltpu.VMEM((8, 16, PIECE), BF16),
        *[pltpu.VMEM((16, 16, width), BF16) for _, _, width in B_PARTS],
        *[pltpu.VMEM((2, 16, 16, width), BF16) for _, _, width in B_PARTS],
        pltpu.VMEM((IN_CHUNKS, 2, 4, 32, CHUNK), BF16),
        pltpu.VMEM((HIDDEN, 256), F32),
        pltpu.VMEM((HIDDEN, 256), F32),
        pltpu.VMEM((256, HIDDEN), BF16),
        pltpu.VMEM((256, HIDDEN), BF16),
        pltpu.VMEM((n, 2, 128, CHUNK), BF16),
        pltpu.VMEM((n, 128, CHUNK), F32),
        pltpu.VMEM((n, 128, CHUNK), BF16),
        pltpu.VMEM((n, 4, 32, CHUNK), BF16),
        pltpu.VMEM((2, n, 16, CHUNK), BF16),
        pltpu.VMEM((2, n, 32, CHUNK), BF16),
        *[pltpu.VMEM((256, c * CHUNK // 8), BF16) for _, c in OUT_PARTS],
        *[pltpu.VMEM((16, 16, c * CHUNK // 8), BF16) for _, c in OUT_PARTS],
        *[pltpu.VMEM((16, 16, c * CHUNK // 8), BF16) for _, c in OUT_PARTS],
        pltpu.VMEM((256, CHUNK), BF16),
        pltpu.VMEM((256, CHUNK), F32),
        pltpu.VMEM((256, CHUNK), BF16),
        pltpu.VMEM((16, 16, CHUNK), BF16),
        pltpu.VMEM((16, 16, CHUNK), BF16),
        pltpu.VMEM((8, 16, 256), BF16),
        pltpu.VMEM((8, 16, 256), BF16),
        pltpu.VMEM((2, 64, 256), BF16),
        pltpu.VMEM((8, 128, 256), BF16),
        pltpu.VMEM((64, 128), BF16),
        dma((13,)),
        dma((2,)),
        dma((2,)),
        dma,
        dma,
        dma((3,)),
        dma((3,)),
        dma((3,)),
        dma((3,)),
        dma,
        dma((2, IN_CHUNKS)),
        dma,
        dma((2, IN_CHUNKS)),
        dma,
        dma((IN_CHUNKS,)),
        dma,
        dma((n,)),
        dma,
        dma((n,)),
        dma,
        dma((n,)),
        dma((3,)),
        dma((3,)),
        dma,
        dma,
        dma,
        dma,
        dma,
        dma,
    ]
    return pl.pallas_call(
        kernel,
        out_shape=jax.ShapeDtypeStruct((ROWS, D), BF16),
        in_specs=[anywhere] * 13,
        out_specs=vmem,
        scratch_shapes=scratch,
        compiler_params=pltpu.CompilerParams(
            collective_id=0, has_side_effects=True, vmem_limit_bytes=60 * 1024 * 1024
        ),
        cost_estimate=pl.CostEstimate(
            flops=2 * 3 * 256 * HIDDEN * D, bytes_accessed=27 * 1024 * 1024, transcendentals=0
        ),
    )(
        cache_len,
        resid,
        query,
        new_key,
        new_value,
        norm_gain.reshape(1, D),
        routes.T,
        gate_fixed.T,
        key_cache,
        value_cache,
        w_gate,
        w_up,
        w_down,
    )


def solution(mesh):
    placed = (
        P(("side", "expert", "tp"), None),
        P(("side", "expert", "tp"), None),
        P(("side", "expert", "tp"), None, None),
        P(("side", "expert", "tp"), None, None),
        P(("side", "expert", "tp"), None),
        P(("side", "expert", "tp"), None),
        P(("side", "expert", "tp")),
        P(),
        P(("side", "expert"), None),
        P(("side", "expert"), None),
        P(("side", "expert"), "tp", None),
        P(("side", "expert"), "tp", None),
        P(("side", "expert"), "tp", None),
    )
    return jax.shard_map(
        layer,
        mesh=mesh,
        in_specs=placed,
        out_specs=P(("side", "expert", "tp"), None),
        check_vma=False,
    )
```

```python
import functools

import jax
import jax.numpy as jnp
from jax import lax
from jax.experimental import pallas as pl
from jax.experimental.pallas import tpu as pltpu
from jax.sharding import PartitionSpec as P

D = 6144
HEADS = 48
KV_HEADS = 8
HEAD_DIM = 128
GROUP = HEADS // KV_HEADS
ROWS = 4
LENGTH = 128
HIDDEN = 672
CHUNK = 1024
IN_CHUNKS = 3
IN_A = IN_CHUNKS * CHUNK
IN_PARTS = ((0, 1), (1, 2))
PIECE = (D - IN_A) // 4
B_PARTS = ((0, 0, 256), (0, 256, 512), (1, 0, 768))
A_CHUNKS = 4
A_COLS = A_CHUNKS * CHUNK
OUT_PARTS = ((0, 2), (2, 1), (3, 1))
F32 = jnp.float32
BF16 = jnp.bfloat16
MESH = pl.DeviceIdType.MESH
W_PARTS = 3
W_ROWS = HIDDEN // W_PARTS
PLANE = ((1, 0), (0, 1), (3, 0), (0, 3), (1, 1), (3, 3), (1, 3), (3, 1), (2, 0), (0, 2), (2, 1), (1, 2), (2, 3), (3, 2), (2, 2))


def iota(shape, dim):
    return lax.broadcasted_iota(jnp.int32, shape, dim)


def dot(a, b):
    return lax.dot_general(a, b, (((1,), (0,)), ((), ())), preferred_element_type=F32)


def dot_nt(a, b):
    return lax.dot_general(a, b, (((1,), (1,)), ((), ())), preferred_element_type=F32)


def onehot(condition):
    return jnp.where(condition, 1.0, 0.0).astype(BF16)


def remote(src, dst, send_sem, recv_sem, device):
    return pltpu.make_async_remote_copy(
        src_ref=src,
        dst_ref=dst,
        send_sem=send_sem,
        recv_sem=recv_sem,
        device_id=device,
        device_id_type=MESH,
    )


def kernel(
    clen_hbm,
    resid_hbm,
    query_hbm,
    new_key_hbm,
    new_value_hbm,
    gain_hbm,
    routes_hbm,
    gates_hbm,
    key_hbm,
    value_hbm,
    wg_hbm,
    wu_hbm,
    wd_hbm,
    out,
    clen,
    resid,
    query,
    new_key,
    new_value,
    gain,
    routes,
    gates,
    kbuf,
    vbuf,
    wg,
    wu,
    wd,
    qs,
    scores,
    own_key,
    own_value,
    heads_out,
    stream,
    xsa0,
    xsa1,
    xsb,
    apack0,
    apack1,
    arecv0,
    arecv1,
    bmsg,
    xb1,
    bpack0,
    bpack1,
    bpack2,
    xbh0,
    xbh1,
    xbh2,
    xa,
    accg,
    accu,
    hid,
    hidb,
    pa,
    pm,
    cr,
    cs,
    far,
    near,
    y20,
    y21,
    y22,
    asend0,
    asend1,
    asend2,
    aback0,
    aback1,
    aback2,
    pbs,
    pbm,
    cbr,
    bsend,
    bback,
    fsend,
    frecv,
    mix_a,
    mix_b,
    gather,
    local_sem,
    a1s,
    a1r,
    b1s,
    b1r,
    b2s,
    b2r,
    bcs,
    bcr,
    ns,
    nr,
    fs,
    fr,
    acs,
    acr,
    rcs,
    rcr,
    rfs,
    rfr,
    rns,
    rnr,
    ras,
    rar,
    rbcs,
    rbcr,
    rbs,
    rbr,
    rfis,
    rfir,
):
    side = lax.axis_index("side")
    expert = lax.axis_index("expert")
    tp = lax.axis_index("tp")
    me = side * 8 + expert
    my_y = me // 4
    my_z = me % 4
    x = tp // 2
    core = tp % 2
    right = lax.rem(x + 1, 4)
    left = lax.rem(x + 3, 4)
    opposite = lax.rem(x + 2, 4)
    other_dev = (side, expert, x * 2 + 1 - core)
    right_dev = (side, expert, right * 2 + core)
    left_dev = (side, expert, left * 2 + core)

    def plane(step):
        y = lax.rem(my_y + step // 4, 4)
        z = lax.rem(my_z + step % 4, 4)
        peer = y * 4 + z
        return peer, (peer // 8, peer % 8, tp)

    def column(step):
        peer = lax.rem(tp + step, 8)
        return peer, (side, expert, peer)

    def whole(buffer, count, send_sem, recv_sem):
        part = buffer.at[pl.ds(0, count)]
        return remote(part, part, send_sem, recv_sem, other_dev)

    bpacks = (bpack0, bpack1, bpack2)
    y2s = (y20, y21, y22)
    asends = (asend0, asend1, asend2)
    abacks = (aback0, aback1, aback2)
    xbhs = (xbh0, xbh1, xbh2)
    barrier = pltpu.get_barrier_semaphore()

    def greet_plane(step, carry):
        pl.semaphore_signal(barrier, inc=1, device_id=plane(step)[1], device_id_type=MESH)
        return carry

    def greet_column(step, carry):
        pl.semaphore_signal(barrier, inc=1, device_id=column(step)[1], device_id_type=MESH)
        return carry

    small_copies = [
        pltpu.make_async_copy(src, dst, local_sem.at[5 + number])
        for number, (src, dst) in enumerate(
            (
                (query_hbm, query),
                (new_key_hbm, new_key),
                (new_value_hbm, new_value),
                (routes_hbm, routes),
                (gates_hbm, gates),
                (clen_hbm, clen),
                (resid_hbm, resid),
                (gain_hbm, gain),
            )
        )
    ]
    for copy in small_copies[:6]:
        copy.start()
    key_copy = pltpu.make_async_copy(key_hbm, kbuf, local_sem.at[0])
    value_copy = pltpu.make_async_copy(value_hbm, vbuf, local_sem.at[1])
    key_copy.start()
    value_copy.start()
    for copy in small_copies[6:]:
        copy.start()
    lax.fori_loop(1, 16, greet_plane, 0)
    lax.fori_loop(1, 8, greet_column, 0)
    weight_copies = []
    for number, (src, dst) in enumerate(((wg_hbm, wg), (wu_hbm, wu), (wd_hbm, wd))):
        for part in range(W_PARTS):
            rows = pl.ds(part * W_ROWS, W_ROWS)
            weight_copies.append(
                pltpu.make_async_copy(
                    src.at[0, rows, :],
                    dst.at[rows, :],
                    local_sem.at[2 + number],
                )
            )
    for copy in weight_copies:
        copy.start()

    for copy in small_copies[:3]:
        copy.wait()
    q32 = query[...].astype(F32)
    for head in range(HEADS):
        qs[head * 4 : head * 4 + 4, :] = q32[:, head * 128 : head * 128 + 128]
    nk32 = new_key[...].astype(F32)
    nv32 = new_value[...].astype(F32)
    for copy_no in range(GROUP):
        own_key[copy_no * 4 : copy_no * 4 + 4, :] = nk32
        own_value[copy_no * 4 : copy_no * 4 + 4, :] = nv32
    for copy in small_copies[3:6]:
        copy.wait()
    lane32 = iota((32, 32), 1)
    row32 = iota((32, 32), 0)
    fixed = gates[...].astype(F32)
    weights = fixed / jnp.sum(fixed, axis=0, keepdims=True)
    chosen = jnp.zeros((32, 32), F32)
    weighted = jnp.zeros((32, 32), F32)
    route = routes[...]
    for k in range(4):
        same = route[k : k + 1, :] == (row32 >> 1)
        chosen = chosen + jnp.where(same, 1.0, 0.0)
        weighted = weighted + jnp.where(same, weights[k : k + 1, :], 0.0)
    earlier = onehot(((row32 >> 2) == (lane32 >> 2)) & (row32 < lane32))
    before = dot(chosen.astype(BF16), earlier)
    picked = (chosen > 0.5) & (jnp.abs(before - (row32 & 1).astype(F32)) < 0.5)
    sel = onehot(picked)
    wsel = jnp.where(picked, weighted, 0.0)
    whi = wsel.astype(BF16)
    wlo = (wsel - whi.astype(F32)).astype(BF16)

    rr = iota((256, 32), 0)
    ll = iota((256, 32), 1)
    spread_a = onehot((rr >> 3) == ll)
    rr = iota((64, 32), 0)
    ll = iota((64, 32), 1)
    mine = onehot((ll == tp * 4 + (rr & 7)) & ((rr & 7) < 4))
    pack_a = dot_nt(spread_a, dot_nt(mine, sel).astype(BF16))
    rr = iota((256, 64), 0)
    ll = iota((256, 64), 1)
    pack_a = jnp.where((rr & 7) == (ll >> 3), pack_a, 0.0).astype(BF16)
    rr = iota((16, 32), 0)
    ll = iota((16, 32), 1)
    pack_b1 = onehot(ll == (rr >> 2) * 8 + (rr & 3))

    block = GROUP * ROWS
    row_of = iota((block, 128), 0) & 3
    key_copy.wait()
    for j in range(KV_HEADS):
        qj = qs[j * block : (j + 1) * block, :].astype(BF16)
        total = jnp.zeros((block, 128), F32)
        for r in range(ROWS):
            part = dot_nt(qj, kbuf[r, :, j * 128 : (j + 1) * 128])
            total = jnp.where(row_of == r, part, total)
        scores[j * block : (j + 1) * block, :] = total

    pos = iota((HEADS * ROWS, 128), 1)
    row_all = iota((HEADS * ROWS, 128), 0) & 3
    limit = jnp.zeros((HEADS * ROWS, 128), jnp.int32)
    for r in range(ROWS):
        limit = jnp.where(row_all == r, clen[r], limit)
    scale = 1.0 / HEAD_DIM**0.5
    s = jnp.where(pos < limit, scores[...] * scale, -1e30)
    own = jnp.concatenate(
        [
            jnp.sum(
                qs[j * block : (j + 1) * block, :] * own_key[:, j * 128 : (j + 1) * 128],
                axis=-1,
                keepdims=True,
            )
            for j in range(KV_HEADS)
        ],
        axis=0,
    )
    own = own * scale
    top = jnp.maximum(jnp.max(s, axis=-1, keepdims=True), own)
    expo = jnp.exp(s - top)
    expo_own = jnp.exp(own - top)
    total = jnp.sum(expo, axis=-1, keepdims=True) + expo_own
    scores[...] = expo / total
    prob_own = (expo_own / total).astype(BF16).astype(F32)
    value_copy.wait()
    for j in range(KV_HEADS):
        pj = scores[j * block : (j + 1) * block, :]
        acc = prob_own[j * block : (j + 1) * block, :] * own_value[:, j * 128 : (j + 1) * 128]
        for r in range(ROWS):
            pr = jnp.where(row_of == r, pj, 0.0).astype(BF16)
            acc = acc + dot(pr, vbuf[r, :, j * 128 : (j + 1) * 128])
        heads_out[j * block : (j + 1) * block, :] = acc
    for copy in small_copies[6:]:
        copy.wait()
    stream[...] = jnp.zeros((8, D), F32)
    for head in range(HEADS):
        cols = slice(head * 128, head * 128 + 128)
        stream[0:4, cols] = resid[:, cols].astype(F32) + heads_out[head * 4 : head * 4 + 4, :]
    st = stream[...]
    mean = jnp.sum(st, axis=-1, keepdims=True) * (1.0 / D)
    centred = st - mean
    variance = jnp.sum(centred * centred, axis=-1, keepdims=True) * (1.0 / D)
    normed = centred * lax.rsqrt(variance + 1e-05) * gain[...]
    for xs, (first, chunks) in zip((xsa0, xsa1), IN_PARTS):
        width = chunks * CHUNK // 8
        for p in range(8):
            start = first * CHUNK + p * width
            xs[p * 8 : p * 8 + 8, :] = normed[:, start : start + width]
    for p in range(4):
        start = IN_A + p * PIECE
        xsb[p * 8 : p * 8 + 8, :] = normed[:, start : start + PIECE]

    bm = dot(pack_b1, xsb[...].astype(BF16)).astype(BF16)
    bmsg[...] = bm
    xb1[tp] = bm
    pl.semaphore_wait(barrier, 22)

    def send_b1(step, carry):
        peer, device = column(step)
        remote(bmsg, xb1.at[tp], b1s, b1r, device).start()
        return carry

    lax.fori_loop(1, 8, send_b1, 0)
    for h, (xs, apack, arecv) in enumerate(((xsa0, apack0, arecv0), (xsa1, apack1, arecv1))):
        packed = dot(pack_a, xs[...].astype(BF16)).astype(BF16)
        apack[...] = packed.reshape(16, 16, packed.shape[1])
        arecv[me] = apack[me]
        for dy, dz in PLANE:
            peer, device = plane(dy * 4 + dz)
            remote(apack.at[peer], arecv.at[me], a1s.at[h], a1r.at[h], device).start()

    rr = iota((256, 32), 0)
    ll = iota((256, 32), 1)
    spread_b = onehot(ll == ((rr >> 4) * 2 + (rr & 1)))
    rr = iota((128, 32), 0)
    ll = iota((128, 32), 1)
    wide = onehot(ll == ((rr >> 4) * 4 + (rr & 3)))
    pack_b = dot_nt(spread_b, dot_nt(wide, sel).astype(BF16))
    rr = iota((256, 128), 0)
    ll = iota((256, 128), 1)
    pack_b = jnp.where(((rr & 15) >> 1) == (ll >> 4), pack_b, 0.0)
    rr = iota((256, 256), 0)
    ll = iota((256, 256), 1)
    unpack_a = onehot(ll == (rr & 31) * 8 + (rr >> 5))

    def arrive_a(h):
        arecv = (arecv0, arecv1)[h]
        first, chunks = IN_PARTS[h]
        width = chunks * CHUNK // 8
        whole(arecv, 15, a1s.at[h], a1r.at[h]).wait_recv()
        got = dot(unpack_a, arecv[...].reshape(256, width)).astype(BF16)
        for p in range(8):
            n, start = divmod(p * width, CHUNK)
            xa[first + n, core, x, :, start : start + width] = got[p * 32 : p * 32 + 32, :]

    def near_in(n):
        mine_ref = xa.at[n, core, x]
        to_right = remote(mine_ref, mine_ref, ns, nr.at[0, n], right_dev)
        to_left = remote(mine_ref, mine_ref, ns, nr.at[1, n], left_dev)
        return to_right, to_left

    def near_arrivals(n):
        from_left = xa.at[n, core, left]
        from_right = xa.at[n, core, right]
        a = remote(from_left, from_left, ns, nr.at[0, n], right_dev)
        b = remote(from_right, from_right, ns, nr.at[1, n], left_dev)
        return a, b

    def far_sends(n):
        low = xa.at[n, core, left, pl.ds(0, 16), :]
        high = xa.at[n, core, right, pl.ds(16, 16), :]
        a = remote(low, low, fs, fr.at[0, n], right_dev)
        b = remote(high, high, fs, fr.at[1, n], left_dev)
        return a, b

    def far_arrivals(n):
        low = xa.at[n, core, opposite, pl.ds(0, 16), :]
        high = xa.at[n, core, opposite, pl.ds(16, 16), :]
        a = remote(low, low, fs, fr.at[0, n], right_dev)
        b = remote(high, high, fs, fr.at[1, n], left_dev)
        return a, b

    def core_send(n, place):
        block = xa.at[n, core, place]
        remote(block, block, acs, acr.at[n], other_dev).start()

    def core_arrival(n):
        half = xa.at[n, 1 - core]
        return remote(half, half, acs, acr.at[n], other_dev)

    def near_send(n):
        for copy in near_in(n):
            copy.start()
        core_send(n, x)

    def wait_rows():
        whole(xb1, 7, b1s, b1r).wait_recv()

    def send_b2(k):
        i, start, width = B_PARTS[k]
        bpack, xbh = bpacks[k], xbhs[k]
        lane = iota((256, 128), 1)
        pick = jnp.where(((lane & 15) >> 2) == core * 2 + i, pack_b, 0.0).astype(BF16)
        piece = xb1[:, :, start : start + width].reshape(128, width)
        bpack[...] = dot(pick, piece).astype(BF16).reshape(16, 16, width)
        xbh[core, me] = bpack[me]
        for dy, dz in PLANE:
            peer, device = plane(dy * 4 + dz)
            remote(bpack.at[peer], xbh.at[core, me], b2s.at[k], b2r.at[k], device).start()

    arrive_a(0)
    near_send(0)
    wait_rows()
    send_b2(0)
    arrive_a(1)
    near_send(1)
    send_b2(1)
    accg[...] = jnp.zeros((HIDDEN, 256), F32)
    accu[...] = jnp.zeros((HIDDEN, 256), F32)
    pltpu.make_async_copy(wg_hbm.at[0], wg, local_sem.at[2]).wait()
    pltpu.make_async_copy(wu_hbm.at[0], wu, local_sem.at[3]).wait()

    def project(value, offset):
        cols = pl.ds(offset, value.shape[1])
        accg[...] += dot_nt(wg[:, cols], value)
        accu[...] += dot_nt(wu[:, cols], value)

    def project_a(n):
        core_arrival(n).wait_recv()
        project(xa[n].reshape(256, CHUNK), n * CHUNK)

    def relay(n):
        for arrival, send, place in zip(near_arrivals(n), far_sends(n), (left, right)):
            arrival.wait_recv()
            send.start()
            core_send(n, place)

    def forward(n):
        for copy in far_arrivals(n):
            copy.wait_recv()
        core_send(n, opposite)

    def b2_core(k, half):
        block = xbhs[k].at[half]
        return remote(block, block, bcs.at[k], bcr.at[k], other_dev)

    def forward_b(k):
        whole(xbhs[k].at[core], 15, b2s.at[k], b2r.at[k]).wait_recv()
        b2_core(k, core).start()

    tau = rr >> 5
    unpack_b = onehot(
        ll == ((rr & 31) >> 1) * 16 + ((tau & 3) * 2 + (tau >> 2)) * 2 + (rr & 1)
    )

    def project_b(half, k):
        i, start, width = B_PARTS[k]
        offset = pl.multiple_of(IN_A + half * 2 * PIECE + i * PIECE + start, 256)
        project(dot(unpack_b, xbhs[k][half].reshape(256, width)).astype(BF16), offset)

    def project_own(k):
        project_b(core, k)

    def project_other(k):
        b2_core(k, 1 - core).wait_recv()
        project_b(1 - core, k)

    relay(0)
    near_send(2)
    send_b2(2)
    relay(1)
    forward_b(0)
    project_own(0)

    @pl.when(core == 1)
    def early():
        forward(0)
        relay(2)
        forward_b(1)

    project_other(0)

    @pl.when(core == 0)
    def late():
        forward(0)

    project_a(0)

    @pl.when(core == 0)
    def later():
        relay(2)
        forward_b(1)

    project_own(1)
    forward(1)
    project_other(1)
    project_a(1)
    forward(2)
    forward_b(2)
    project_own(2)
    project_a(2)
    project_other(2)
    g = accg[...]
    hidden = (g * jax.nn.sigmoid(g) * accu[...]).astype(BF16)
    hid[...] = dot_nt(onehot(rr == ll), hidden).astype(BF16)
    t_of = (rr & 15) >> 1
    to_b = onehot(ll == ((t_of & 1) * 4 + (t_of >> 1)) * 32 + (rr >> 4) * 2 + (rr & 1))
    pltpu.make_async_copy(wd_hbm.at[0], wd, local_sem.at[4]).wait()

    def drain():
        whole(xb1, 7, b1s, b1r).wait_send()
        whole(arecv0, 15, a1s.at[0], a1r.at[0]).wait_send()
        whole(arecv1, 15, a1s.at[1], a1r.at[1]).wait_send()
        for k in range(3):
            whole(xbhs[k].at[core], 15, b2s.at[k], b2r.at[k]).wait_send()
            b2_core(k, core).wait_send()
        sent = xa.at[0:IN_CHUNKS, 0, 0:2]
        remote(sent, sent, ns, nr.at[0, 0], other_dev).wait_send()
        sent = xa.at[0:IN_CHUNKS, 0, 0]
        remote(sent, sent, fs, fr.at[0, 0], other_dev).wait_send()
        sent = xa.at[0:IN_CHUNKS, 0]
        remote(sent, sent, acs, acr.at[0], other_dev).wait_send()
        remote(cr, cr, rcs, rcr.at[0], other_dev).wait_send()
        b_core().wait_send()
        whole(bback, 15, rbs, rbr).wait_send()
        remote(far, far, rfs, rfr.at[0], other_dev).wait_send()
        remote(near, near, rns, rnr.at[0], other_dev).wait_send()
        whole(frecv, 7, rfis, rfir).wait_send()

    def down_a(n):
        y = dot(hid[...], wd[:, n * CHUNK : (n + 1) * CHUNK])
        pa[n] = y.astype(BF16).reshape(2, 128, CHUNK)
        pm[n] = jnp.where(core == 0, y[:128], y[128:])
        remote(pa.at[n, 1 - core], cr.at[n], rcs, rcr.at[n], other_dev).start()

    def chip_sum(n):
        remote(pa.at[n, 1 - core], cr.at[n], rcs, rcr.at[n], other_dev).wait_recv()
        both = pm[n] + cr[n].astype(F32)
        pm[n] = both
        cs[n] = both.astype(BF16).reshape(4, 32, CHUNK)
        for copy in ret_far(n):
            copy.start()

    def ret_far(n):
        a = remote(
            cs.at[n, opposite, pl.ds(0, 16), :], far.at[0, n], rfs, rfr.at[n], right_dev
        )
        b = remote(
            cs.at[n, opposite, pl.ds(16, 16), :], far.at[1, n], rfs, rfr.at[n], left_dev
        )
        return a, b

    def ret_near(n):
        a = remote(cs.at[n, right], near.at[0, n], rns, rnr.at[n], right_dev)
        b = remote(cs.at[n, left], near.at[1, n], rns, rnr.at[n], left_dev)
        return a, b

    def ret_relay(n):
        both = near.at[0, n]
        remote(both, both, rfs, rfr.at[n], right_dev).wait_recv()
        to_right = pl.ds(pl.multiple_of(right * 32, 32), 16)
        to_left = pl.ds(pl.multiple_of(left * 32 + 16, 16), 16)
        cs[n, right, 0:16, :] = (pm[n, to_right, :] + far[0, n].astype(F32)).astype(BF16)
        cs[n, left, 16:32, :] = (pm[n, to_left, :] + far[1, n].astype(F32)).astype(BF16)
        for copy in ret_near(n):
            copy.start()

    def ret_sum(n):
        both = pa.at[n, 0, 0:64]
        remote(both, both, rns, rnr.at[n], right_dev).wait_recv()
        rows = pl.ds(pl.multiple_of(x * 32, 32), 32)
        y = pm[n, rows, :] + near[0, n].astype(F32) + near[1, n].astype(F32)
        y = y.astype(BF16)
        for (first, chunks), y2 in zip(OUT_PARTS, y2s):
            if first <= n < first + chunks:
                width = chunks * CHUNK // 8
                for q in range(CHUNK // width):
                    row = ((n - first) * (CHUNK // width) + q) * 32
                    y2[row : row + 32, :] = y[:, q * width : (q + 1) * width]

    def b_core():
        return remote(pbs, cbr, rbcs, rbcr, other_dev)

    def down_b(half):
        cols = pl.ds(pl.multiple_of(A_COLS + half * CHUNK, CHUNK), CHUNK)
        return dot(hidb[...], wd[:, cols])

    def b_other():
        hidb[...] = dot_nt(to_b, hidden).astype(BF16)
        pbs[...] = down_b(1 - core).astype(BF16)
        b_core().start()

    def b_mine():
        pbm[...] = down_b(core)

    def b_home():
        b_core().wait_recv()
        bsend[...] = (pbm[...] + cbr[...].astype(F32)).astype(BF16).reshape(16, 16, CHUNK)
        bback[me] = bsend[me]
        for dy, dz in PLANE:
            peer, device = plane(dy * 4 + dz)
            remote(bsend.at[peer], bback.at[me], rbs, rbr, device).start()

    rr = iota((256, 256), 0)
    ll = iota((256, 256), 1)
    repack_a = onehot(ll == (rr & 7) * 32 + (rr >> 3))

    def a_home(h):
        asend, aback = asends[h], abacks[h]
        value = dot(repack_a, y2s[h][...]).astype(BF16)
        asend[...] = value.reshape(16, 16, value.shape[1])
        aback[me] = asend[me]
        for dy, dz in PLANE:
            peer, device = plane(dy * 4 + dz)
            remote(asend.at[peer], aback.at[me], ras.at[h], rar.at[h], device).start()

    def home_tables():
        rr = iota((128, 256), 0)
        ll = iota((128, 256), 1)
        wide_hi = dot_nt(dot_nt(wide, whi).astype(BF16), spread_b)
        wide_lo = dot_nt(dot_nt(wide, wlo).astype(BF16), spread_b)
        for q in range(4):
            keep = ((rr >> 4) == ((ll & 15) >> 1)) & (((rr & 15) >> 2) == q)
            mix_b[2 * q] = jnp.where(keep, wide_hi, 0.0).astype(BF16)
            mix_b[2 * q + 1] = jnp.where(keep, wide_lo, 0.0).astype(BF16)
        rr = iota((64, 256), 0)
        ll = iota((64, 256), 1)
        keep = (rr >> 3) == (ll & 7)
        home_hi = dot_nt(dot_nt(mine, whi).astype(BF16), spread_a)
        home_lo = dot_nt(dot_nt(mine, wlo).astype(BF16), spread_a)
        mix_a[0] = jnp.where(keep, home_hi, 0.0).astype(BF16)
        mix_a[1] = jnp.where(keep, home_lo, 0.0).astype(BF16)
        rr = iota((64, 128), 0)
        ll = iota((64, 128), 1)
        gather[...] = onehot(
            ((rr >> 5) == ((ll >> 4) & 1))
            & (((rr >> 3) & 3) == ((ll & 15) >> 2))
            & ((rr & 7) == (ll & 3))
        )

    down_a(0)
    b_other()
    down_a(1)
    chip_sum(0)
    b_mine()
    down_a(2)
    chip_sum(1)
    down_a(3)
    b_home()
    chip_sum(2)
    chip_sum(3)
    ret_relay(0)
    ret_relay(1)
    ret_relay(2)
    ret_relay(3)
    home_tables()
    ret_sum(0)
    ret_sum(1)
    a_home(0)
    ret_sum(2)
    a_home(1)

    whole(bback, 15, rbs, rbr).wait_recv()
    partial = jnp.zeros((128, 256), F32)
    for q in range(4):
        piece = bback[:, :, q * 256 : q * 256 + 256].reshape(256, 256)
        partial = partial + dot(mix_b[2 * q], piece) + dot(mix_b[2 * q + 1], piece)
    fsend[...] = partial.astype(BF16).reshape(8, 16, 256)
    frecv[tp] = fsend[tp]

    def send_b4(step, carry):
        peer, device = column(step)
        remote(fsend.at[peer], frecv.at[tp], rfis, rfir, device).start()
        return carry

    lax.fori_loop(1, 8, send_b4, 0)
    ret_sum(3)
    a_home(2)
    drain()

    def finish_a(h):
        first, chunks = OUT_PARTS[h]
        width = chunks * CHUNK // 8
        whole(abacks[h], 15, ras.at[h], rar.at[h]).wait_recv()
        back = abacks[h][...].reshape(256, width)
        home_a = dot(mix_a[0], back) + dot(mix_a[1], back)
        for p in range(8):
            start = first * CHUNK + p * width
            cols = slice(start, start + width)
            out[:, cols] = (stream[0:4, cols] + home_a[p * 8 : p * 8 + 4, :]).astype(BF16)

    finish_a(0)
    finish_a(1)
    whole(frecv, 7, rfis, rfir).wait_recv()
    home_b = dot(gather[...], frecv[...].reshape(128, 256))
    for piece in range(8):
        start = A_COLS + piece * 256
        out[:, start : start + 256] = (
            stream[0:4, start : start + 256] + home_b[piece * 8 : piece * 8 + 4, :]
        ).astype(BF16)
    finish_a(2)
    for h, aback in enumerate(abacks):
        whole(aback, 15, ras.at[h], rar.at[h]).wait_send()


def layer(
    resid,
    query,
    key_cache,
    value_cache,
    new_key,
    new_value,
    cache_len,
    norm_gain,
    routes,
    gate_fixed,
    w_gate,
    w_up,
    w_down,
):
    vmem = pl.BlockSpec(memory_space=pltpu.VMEM)
    anywhere = pl.BlockSpec(memory_space=pl.ANY)
    dma = pltpu.SemaphoreType.DMA
    n = A_CHUNKS
    scratch = [
        pltpu.SMEM((ROWS,), jnp.int32),
        pltpu.VMEM((ROWS, D), BF16),
        pltpu.VMEM((ROWS, D), BF16),
        pltpu.VMEM((ROWS, 1024), BF16),
        pltpu.VMEM((ROWS, 1024), BF16),
        pltpu.VMEM((1, D), F32),
        pltpu.VMEM((4, 32), jnp.int32),
        pltpu.VMEM((4, 32), jnp.int32),
        pltpu.VMEM((ROWS, LENGTH, 1024), BF16),
        pltpu.VMEM((ROWS, LENGTH, 1024), BF16),
        pltpu.VMEM((HIDDEN, D), BF16),
        pltpu.VMEM((HIDDEN, D), BF16),
        pltpu.VMEM((HIDDEN, D), BF16),
        pltpu.VMEM((HEADS * ROWS, 128), F32),
        pltpu.VMEM((HEADS * ROWS, 128), F32),
        pltpu.VMEM((GROUP * ROWS, 1024), F32),
        pltpu.VMEM((GROUP * ROWS, 1024), F32),
        pltpu.VMEM((HEADS * ROWS, 128), F32),
        pltpu.VMEM((8, D), F32),
        pltpu.VMEM((64, 128), F32),
        pltpu.VMEM((64, 256), F32),
        pltpu.VMEM((32, PIECE), F32),
        pltpu.VMEM((16, 16, 128), BF16),
        pltpu.VMEM((16, 16, 256), BF16),
        pltpu.VMEM((16, 16, 128), BF16),
        pltpu.VMEM((16, 16, 256), BF16),
        pltpu.VMEM((16, PIECE), BF16),
        pltpu.VMEM((8, 16, PIECE), BF16),
        *[pltpu.VMEM((16, 16, width), BF16) for _, _, width in B_PARTS],
        *[pltpu.VMEM((2, 16, 16, width), BF16) for _, _, width in B_PARTS],
        pltpu.VMEM((IN_CHUNKS, 2, 4, 32, CHUNK), BF16),
        pltpu.VMEM((HIDDEN, 256), F32),
        pltpu.VMEM((HIDDEN, 256), F32),
        pltpu.VMEM((256, HIDDEN), BF16),
        pltpu.VMEM((256, HIDDEN), BF16),
        pltpu.VMEM((n, 2, 128, CHUNK), BF16),
        pltpu.VMEM((n, 128, CHUNK), F32),
        pltpu.VMEM((n, 128, CHUNK), BF16),
        pltpu.VMEM((n, 4, 32, CHUNK), BF16),
        pltpu.VMEM((2, n, 16, CHUNK), BF16),
        pltpu.VMEM((2, n, 32, CHUNK), BF16),
        *[pltpu.VMEM((256, c * CHUNK // 8), BF16) for _, c in OUT_PARTS],
        *[pltpu.VMEM((16, 16, c * CHUNK // 8), BF16) for _, c in OUT_PARTS],
        *[pltpu.VMEM((16, 16, c * CHUNK // 8), BF16) for _, c in OUT_PARTS],
        pltpu.VMEM((256, CHUNK), BF16),
        pltpu.VMEM((256, CHUNK), F32),
        pltpu.VMEM((256, CHUNK), BF16),
        pltpu.VMEM((16, 16, CHUNK), BF16),
        pltpu.VMEM((16, 16, CHUNK), BF16),
        pltpu.VMEM((8, 16, 256), BF16),
        pltpu.VMEM((8, 16, 256), BF16),
        pltpu.VMEM((2, 64, 256), BF16),
        pltpu.VMEM((8, 128, 256), BF16),
        pltpu.VMEM((64, 128), BF16),
        dma((13,)),
        dma((2,)),
        dma((2,)),
        dma,
        dma,
        dma((3,)),
        dma((3,)),
        dma((3,)),
        dma((3,)),
        dma,
        dma((2, IN_CHUNKS)),
        dma,
        dma((2, IN_CHUNKS)),
        dma,
        dma((IN_CHUNKS,)),
        dma,
        dma((n,)),
        dma,
        dma((n,)),
        dma,
        dma((n,)),
        dma((3,)),
        dma((3,)),
        dma,
        dma,
        dma,
        dma,
        dma,
        dma,
    ]
    return pl.pallas_call(
        kernel,
        out_shape=jax.ShapeDtypeStruct((ROWS, D), BF16),
        in_specs=[anywhere] * 13,
        out_specs=vmem,
        scratch_shapes=scratch,
        compiler_params=pltpu.CompilerParams(
            collective_id=0, has_side_effects=True, vmem_limit_bytes=60 * 1024 * 1024
        ),
        cost_estimate=pl.CostEstimate(
            flops=2 * 3 * 256 * HIDDEN * D, bytes_accessed=27 * 1024 * 1024, transcendentals=0
        ),
    )(
        cache_len,
        resid,
        query,
        new_key,
        new_value,
        norm_gain.reshape(1, D),
        routes.T,
        gate_fixed.T,
        key_cache,
        value_cache,
        w_gate,
        w_up,
        w_down,
    )


def solution(mesh):
    placed = (
        P(("side", "expert", "tp"), None),
        P(("side", "expert", "tp"), None),
        P(("side", "expert", "tp"), None, None),
        P(("side", "expert", "tp"), None, None),
        P(("side", "expert", "tp"), None),
        P(("side", "expert", "tp"), None),
        P(("side", "expert", "tp")),
        P(),
        P(("side", "expert"), None),
        P(("side", "expert"), None),
        P(("side", "expert"), "tp", None),
        P(("side", "expert"), "tp", None),
        P(("side", "expert"), "tp", None),
    )
    return jax.shard_map(
        layer,
        mesh=mesh,
        in_specs=placed,
        out_specs=P(("side", "expert", "tp"), None),
        check_vma=False,
    )
```

```python
import functools

import jax
import jax.numpy as jnp
from jax import lax
from jax.experimental import pallas as pl
from jax.experimental.pallas import tpu as pltpu
from jax.sharding import PartitionSpec as P

D = 6144
HEADS = 48
KV_HEADS = 8
HEAD_DIM = 128
GROUP = HEADS // KV_HEADS
ROWS = 4
LENGTH = 128
HIDDEN = 672
CHUNK = 1024
IN_CHUNKS = 3
IN_A = IN_CHUNKS * CHUNK
IN_PARTS = ((0, 1), (1, 2))
PIECE = (D - IN_A) // 4
B_PARTS = ((0, 0, 256), (0, 256, 512), (1, 0, 768))
A_CHUNKS = 4
A_COLS = A_CHUNKS * CHUNK
OUT_PARTS = ((0, 2), (2, 1), (3, 1))
F32 = jnp.float32
BF16 = jnp.bfloat16
MESH = pl.DeviceIdType.MESH
W_PARTS = 3
W_ROWS = HIDDEN // W_PARTS
PLANE = ((1, 0), (0, 1), (3, 0), (0, 3), (1, 1), (3, 3), (1, 3), (3, 1), (2, 0), (0, 2), (2, 1), (1, 2), (2, 3), (3, 2), (2, 2))


def iota(shape, dim):
    return lax.broadcasted_iota(jnp.int32, shape, dim)


def dot(a, b):
    return lax.dot_general(a, b, (((1,), (0,)), ((), ())), preferred_element_type=F32)


def dot_nt(a, b):
    return lax.dot_general(a, b, (((1,), (1,)), ((), ())), preferred_element_type=F32)


def onehot(condition):
    return jnp.where(condition, 1.0, 0.0).astype(BF16)


def remote(src, dst, send_sem, recv_sem, device):
    return pltpu.make_async_remote_copy(
        src_ref=src,
        dst_ref=dst,
        send_sem=send_sem,
        recv_sem=recv_sem,
        device_id=device,
        device_id_type=MESH,
    )


def kernel(
    clen_hbm,
    resid_hbm,
    query_hbm,
    new_key_hbm,
    new_value_hbm,
    gain_hbm,
    routes_hbm,
    gates_hbm,
    key_hbm,
    value_hbm,
    wg_hbm,
    wu_hbm,
    wd_hbm,
    out,
    clen,
    resid,
    query,
    new_key,
    new_value,
    gain,
    routes,
    gates,
    kbuf,
    vbuf,
    wg,
    wu,
    wd,
    qs,
    scores,
    own_key,
    own_value,
    heads_out,
    stream,
    xsa0,
    xsa1,
    xsb,
    apack0,
    apack1,
    arecv0,
    arecv1,
    bmsg,
    xb1,
    bpack0,
    bpack1,
    bpack2,
    xbh0,
    xbh1,
    xbh2,
    xa,
    accg,
    accu,
    hid,
    hidb,
    pa,
    pm,
    cr,
    cs,
    far,
    near,
    y20,
    y21,
    y22,
    asend0,
    asend1,
    asend2,
    aback0,
    aback1,
    aback2,
    pbs,
    pbm,
    cbr,
    bsend,
    bback,
    fsend,
    frecv,
    mix_a,
    mix_b,
    gather,
    local_sem,
    a1s,
    a1r,
    b1s,
    b1r,
    b2s,
    b2r,
    bcs,
    bcr,
    ns,
    nr,
    fs,
    fr,
    acs,
    acr,
    rcs,
    rcr,
    rfs,
    rfr,
    rns,
    rnr,
    ras,
    rar,
    rbcs,
    rbcr,
    rbs,
    rbr,
    rfis,
    rfir,
):
    side = lax.axis_index("side")
    expert = lax.axis_index("expert")
    tp = lax.axis_index("tp")
    me = side * 8 + expert
    my_y = me // 4
    my_z = me % 4
    x = tp // 2
    core = tp % 2
    right = lax.rem(x + 1, 4)
    left = lax.rem(x + 3, 4)
    opposite = lax.rem(x + 2, 4)
    other_dev = (side, expert, x * 2 + 1 - core)
    right_dev = (side, expert, right * 2 + core)
    left_dev = (side, expert, left * 2 + core)

    def plane(step):
        y = lax.rem(my_y + step // 4, 4)
        z = lax.rem(my_z + step % 4, 4)
        peer = y * 4 + z
        return peer, (peer // 8, peer % 8, tp)

    def column(step):
        peer = lax.rem(tp + step, 8)
        return peer, (side, expert, peer)

    def whole(buffer, count, send_sem, recv_sem):
        part = buffer.at[pl.ds(0, count)]
        return remote(part, part, send_sem, recv_sem, other_dev)

    bpacks = (bpack0, bpack1, bpack2)
    y2s = (y20, y21, y22)
    asends = (asend0, asend1, asend2)
    abacks = (aback0, aback1, aback2)
    xbhs = (xbh0, xbh1, xbh2)
    barrier = pltpu.get_barrier_semaphore()

    def greet_plane(step, carry):
        pl.semaphore_signal(barrier, inc=1, device_id=plane(step)[1], device_id_type=MESH)
        return carry

    def greet_column(step, carry):
        pl.semaphore_signal(barrier, inc=1, device_id=column(step)[1], device_id_type=MESH)
        return carry

    small_copies = [
        pltpu.make_async_copy(src, dst, local_sem.at[5 + number])
        for number, (src, dst) in enumerate(
            (
                (query_hbm, query),
                (new_key_hbm, new_key),
                (new_value_hbm, new_value),
                (routes_hbm, routes),
                (gates_hbm, gates),
                (clen_hbm, clen),
                (resid_hbm, resid),
                (gain_hbm, gain),
            )
        )
    ]
    for copy in small_copies[:6]:
        copy.start()
    key_copy = pltpu.make_async_copy(key_hbm, kbuf, local_sem.at[0])
    value_copy = pltpu.make_async_copy(value_hbm, vbuf, local_sem.at[1])
    key_copy.start()
    value_copy.start()
    for copy in small_copies[6:]:
        copy.start()
    lax.fori_loop(1, 16, greet_plane, 0)
    lax.fori_loop(1, 8, greet_column, 0)
    weight_copies = []
    for number, (src, dst) in enumerate(((wg_hbm, wg), (wu_hbm, wu), (wd_hbm, wd))):
        for part in range(W_PARTS):
            rows = pl.ds(part * W_ROWS, W_ROWS)
            weight_copies.append(
                pltpu.make_async_copy(
                    src.at[0, rows, :],
                    dst.at[rows, :],
                    local_sem.at[2 + number],
                )
            )
    for copy in weight_copies:
        copy.start()

    for copy in small_copies[:3]:
        copy.wait()
    q32 = query[...].astype(F32)
    for head in range(HEADS):
        qs[head * 4 : head * 4 + 4, :] = q32[:, head * 128 : head * 128 + 128]
    nk32 = new_key[...].astype(F32)
    nv32 = new_value[...].astype(F32)
    for copy_no in range(GROUP):
        own_key[copy_no * 4 : copy_no * 4 + 4, :] = nk32
        own_value[copy_no * 4 : copy_no * 4 + 4, :] = nv32
    for copy in small_copies[3:6]:
        copy.wait()
    lane32 = iota((32, 32), 1)
    row32 = iota((32, 32), 0)
    chosen = jnp.zeros((32, 32), F32)
    route = routes[...]
    for k in range(4):
        same = route[k : k + 1, :] == (row32 >> 1)
        chosen = chosen + jnp.where(same, 1.0, 0.0)
    earlier = onehot(((row32 >> 2) == (lane32 >> 2)) & (row32 < lane32))
    before = dot(chosen.astype(BF16), earlier)
    picked = (chosen > 0.5) & (jnp.abs(before - (row32 & 1).astype(F32)) < 0.5)
    sel = onehot(picked)

    rr = iota((256, 32), 0)
    ll = iota((256, 32), 1)
    spread_a = onehot((rr >> 3) == ll)
    rr = iota((64, 32), 0)
    ll = iota((64, 32), 1)
    mine = onehot((ll == tp * 4 + (rr & 7)) & ((rr & 7) < 4))
    pack_a = dot_nt(spread_a, dot_nt(mine, sel).astype(BF16))
    rr = iota((256, 64), 0)
    ll = iota((256, 64), 1)
    pack_a = jnp.where((rr & 7) == (ll >> 3), pack_a, 0.0).astype(BF16)
    rr = iota((16, 32), 0)
    ll = iota((16, 32), 1)
    pack_b1 = onehot(ll == (rr >> 2) * 8 + (rr & 3))

    block = GROUP * ROWS
    row_of = iota((block, 128), 0) & 3
    key_copy.wait()
    for j in range(KV_HEADS):
        qj = qs[j * block : (j + 1) * block, :].astype(BF16)
        total = jnp.zeros((block, 128), F32)
        for r in range(ROWS):
            part = dot_nt(qj, kbuf[r, :, j * 128 : (j + 1) * 128])
            total = jnp.where(row_of == r, part, total)
        scores[j * block : (j + 1) * block, :] = total

    pos = iota((HEADS * ROWS, 128), 1)
    row_all = iota((HEADS * ROWS, 128), 0) & 3
    limit = jnp.zeros((HEADS * ROWS, 128), jnp.int32)
    for r in range(ROWS):
        limit = jnp.where(row_all == r, clen[r], limit)
    scale = 1.0 / HEAD_DIM**0.5
    s = jnp.where(pos < limit, scores[...] * scale, -1e30)
    own = jnp.concatenate(
        [
            jnp.sum(
                qs[j * block : (j + 1) * block, :] * own_key[:, j * 128 : (j + 1) * 128],
                axis=-1,
                keepdims=True,
            )
            for j in range(KV_HEADS)
        ],
        axis=0,
    )
    own = own * scale
    top = jnp.maximum(jnp.max(s, axis=-1, keepdims=True), own)
    expo = jnp.exp(s - top)
    expo_own = jnp.exp(own - top)
    total = jnp.sum(expo, axis=-1, keepdims=True) + expo_own
    scores[...] = expo / total
    prob_own = (expo_own / total).astype(BF16).astype(F32)
    value_copy.wait()
    for j in range(KV_HEADS):
        pj = scores[j * block : (j + 1) * block, :]
        acc = prob_own[j * block : (j + 1) * block, :] * own_value[:, j * 128 : (j + 1) * 128]
        for r in range(ROWS):
            pr = jnp.where(row_of == r, pj, 0.0).astype(BF16)
            acc = acc + dot(pr, vbuf[r, :, j * 128 : (j + 1) * 128])
        heads_out[j * block : (j + 1) * block, :] = acc
    for copy in small_copies[6:]:
        copy.wait()
    stream[...] = jnp.zeros((8, D), F32)
    for head in range(HEADS):
        cols = slice(head * 128, head * 128 + 128)
        stream[0:4, cols] = resid[:, cols].astype(F32) + heads_out[head * 4 : head * 4 + 4, :]
    st = stream[...]
    mean = jnp.sum(st, axis=-1, keepdims=True) * (1.0 / D)
    centred = st - mean
    variance = jnp.sum(centred * centred, axis=-1, keepdims=True) * (1.0 / D)
    normed = centred * lax.rsqrt(variance + 1e-05) * gain[...]
    for xs, (first, chunks) in zip((xsa0, xsa1), IN_PARTS):
        width = chunks * CHUNK // 8
        for p in range(8):
            start = first * CHUNK + p * width
            xs[p * 8 : p * 8 + 8, :] = normed[:, start : start + width]
    for p in range(4):
        start = IN_A + p * PIECE
        xsb[p * 8 : p * 8 + 8, :] = normed[:, start : start + PIECE]

    bm = dot(pack_b1, xsb[...].astype(BF16)).astype(BF16)
    bmsg[...] = bm
    xb1[tp] = bm
    pl.semaphore_wait(barrier, 22)

    def send_b1(step, carry):
        peer, device = column(step)
        remote(bmsg, xb1.at[tp], b1s, b1r, device).start()
        return carry

    lax.fori_loop(1, 8, send_b1, 0)
    for h, (xs, apack, arecv) in enumerate(((xsa0, apack0, arecv0), (xsa1, apack1, arecv1))):
        packed = dot(pack_a, xs[...].astype(BF16)).astype(BF16)
        apack[...] = packed.reshape(16, 16, packed.shape[1])
        arecv[me] = apack[me]
        for dy, dz in PLANE:
            peer, device = plane(dy * 4 + dz)
            remote(apack.at[peer], arecv.at[me], a1s.at[h], a1r.at[h], device).start()

    rr = iota((256, 32), 0)
    ll = iota((256, 32), 1)
    spread_b = onehot(ll == ((rr >> 4) * 2 + (rr & 1)))
    rr = iota((128, 32), 0)
    ll = iota((128, 32), 1)
    wide = onehot(ll == ((rr >> 4) * 4 + (rr & 3)))
    pack_b = dot_nt(spread_b, dot_nt(wide, sel).astype(BF16))
    rr = iota((256, 128), 0)
    ll = iota((256, 128), 1)
    pack_b = jnp.where(((rr & 15) >> 1) == (ll >> 4), pack_b, 0.0)
    rr = iota((256, 256), 0)
    ll = iota((256, 256), 1)
    unpack_a = onehot(ll == (rr & 31) * 8 + (rr >> 5))

    def arrive_a(h):
        arecv = (arecv0, arecv1)[h]
        first, chunks = IN_PARTS[h]
        width = chunks * CHUNK // 8
        whole(arecv, 15, a1s.at[h], a1r.at[h]).wait_recv()
        got = dot(unpack_a, arecv[...].reshape(256, width)).astype(BF16)
        for p in range(8):
            n, start = divmod(p * width, CHUNK)
            xa[first + n, core, x, :, start : start + width] = got[p * 32 : p * 32 + 32, :]

    def near_in(n):
        mine_ref = xa.at[n, core, x]
        to_right = remote(mine_ref, mine_ref, ns, nr.at[0, n], right_dev)
        to_left = remote(mine_ref, mine_ref, ns, nr.at[1, n], left_dev)
        return to_right, to_left

    def near_arrivals(n):
        from_left = xa.at[n, core, left]
        from_right = xa.at[n, core, right]
        a = remote(from_left, from_left, ns, nr.at[0, n], right_dev)
        b = remote(from_right, from_right, ns, nr.at[1, n], left_dev)
        return a, b

    def far_sends(n):
        low = xa.at[n, core, left, pl.ds(0, 16), :]
        high = xa.at[n, core, right, pl.ds(16, 16), :]
        a = remote(low, low, fs, fr.at[0, n], right_dev)
        b = remote(high, high, fs, fr.at[1, n], left_dev)
        return a, b

    def far_arrivals(n):
        low = xa.at[n, core, opposite, pl.ds(0, 16), :]
        high = xa.at[n, core, opposite, pl.ds(16, 16), :]
        a = remote(low, low, fs, fr.at[0, n], right_dev)
        b = remote(high, high, fs, fr.at[1, n], left_dev)
        return a, b

    def core_send(n, place):
        block = xa.at[n, core, place]
        remote(block, block, acs, acr.at[n], other_dev).start()

    def core_arrival(n):
        half = xa.at[n, 1 - core]
        return remote(half, half, acs, acr.at[n], other_dev)

    def near_send(n):
        for copy in near_in(n):
            copy.start()
        core_send(n, x)

    def wait_rows():
        whole(xb1, 7, b1s, b1r).wait_recv()

    def send_b2(k):
        i, start, width = B_PARTS[k]
        bpack, xbh = bpacks[k], xbhs[k]
        lane = iota((256, 128), 1)
        pick = jnp.where(((lane & 15) >> 2) == core * 2 + i, pack_b, 0.0).astype(BF16)
        piece = xb1[:, :, start : start + width].reshape(128, width)
        bpack[...] = dot(pick, piece).astype(BF16).reshape(16, 16, width)
        xbh[core, me] = bpack[me]
        for dy, dz in PLANE:
            peer, device = plane(dy * 4 + dz)
            remote(bpack.at[peer], xbh.at[core, me], b2s.at[k], b2r.at[k], device).start()

    arrive_a(0)
    near_send(0)
    wait_rows()
    send_b2(0)
    arrive_a(1)
    near_send(1)
    send_b2(1)
    accg[...] = jnp.zeros((HIDDEN, 256), F32)
    accu[...] = jnp.zeros((HIDDEN, 256), F32)
    pltpu.make_async_copy(wg_hbm.at[0], wg, local_sem.at[2]).wait()
    pltpu.make_async_copy(wu_hbm.at[0], wu, local_sem.at[3]).wait()

    def project(value, offset):
        cols = pl.ds(offset, value.shape[1])
        accg[...] += dot_nt(wg[:, cols], value)
        accu[...] += dot_nt(wu[:, cols], value)

    def project_a(n):
        core_arrival(n).wait_recv()
        project(xa[n].reshape(256, CHUNK), n * CHUNK)

    def relay(n):
        for arrival, send, place in zip(near_arrivals(n), far_sends(n), (left, right)):
            arrival.wait_recv()
            send.start()
            core_send(n, place)

    def forward(n):
        for copy in far_arrivals(n):
            copy.wait_recv()
        core_send(n, opposite)

    def b2_core(k, half):
        block = xbhs[k].at[half]
        return remote(block, block, bcs.at[k], bcr.at[k], other_dev)

    def forward_b(k):
        whole(xbhs[k].at[core], 15, b2s.at[k], b2r.at[k]).wait_recv()
        b2_core(k, core).start()

    tau = rr >> 5
    unpack_b = onehot(
        ll == ((rr & 31) >> 1) * 16 + ((tau & 3) * 2 + (tau >> 2)) * 2 + (rr & 1)
    )

    def project_b(half, k):
        i, start, width = B_PARTS[k]
        offset = pl.multiple_of(IN_A + half * 2 * PIECE + i * PIECE + start, 256)
        project(dot(unpack_b, xbhs[k][half].reshape(256, width)).astype(BF16), offset)

    def project_own(k):
        project_b(core, k)

    def project_other(k):
        b2_core(k, 1 - core).wait_recv()
        project_b(1 - core, k)

    relay(0)
    near_send(2)
    send_b2(2)
    relay(1)
    forward_b(0)
    project_own(0)

    @pl.when(core == 1)
    def early():
        forward(0)
        relay(2)
        forward_b(1)

    project_other(0)

    @pl.when(core == 0)
    def late():
        forward(0)

    project_a(0)

    @pl.when(core == 0)
    def later():
        relay(2)
        forward_b(1)

    project_own(1)
    forward(1)
    project_other(1)
    project_a(1)
    forward(2)
    forward_b(2)
    project_own(2)
    project_a(2)
    project_other(2)
    g = accg[...]
    hidden = (g * jax.nn.sigmoid(g) * accu[...]).astype(BF16)
    hid[...] = dot_nt(onehot(rr == ll), hidden).astype(BF16)
    t_of = (rr & 15) >> 1
    to_b = onehot(ll == ((t_of & 1) * 4 + (t_of >> 1)) * 32 + (rr >> 4) * 2 + (rr & 1))
    pltpu.make_async_copy(wd_hbm.at[0], wd, local_sem.at[4]).wait()

    def drain():
        whole(xb1, 7, b1s, b1r).wait_send()
        whole(arecv0, 15, a1s.at[0], a1r.at[0]).wait_send()
        whole(arecv1, 15, a1s.at[1], a1r.at[1]).wait_send()
        for k in range(3):
            whole(xbhs[k].at[core], 15, b2s.at[k], b2r.at[k]).wait_send()
            b2_core(k, core).wait_send()
        sent = xa.at[0:IN_CHUNKS, 0, 0:2]
        remote(sent, sent, ns, nr.at[0, 0], other_dev).wait_send()
        sent = xa.at[0:IN_CHUNKS, 0, 0]
        remote(sent, sent, fs, fr.at[0, 0], other_dev).wait_send()
        sent = xa.at[0:IN_CHUNKS, 0]
        remote(sent, sent, acs, acr.at[0], other_dev).wait_send()
        remote(cr, cr, rcs, rcr.at[0], other_dev).wait_send()
        b_core().wait_send()
        whole(bback, 15, rbs, rbr).wait_send()
        remote(far, far, rfs, rfr.at[0], other_dev).wait_send()
        remote(near, near, rns, rnr.at[0], other_dev).wait_send()
        whole(frecv, 7, rfis, rfir).wait_send()

    def down_a(n):
        y = dot(hid[...], wd[:, n * CHUNK : (n + 1) * CHUNK])
        pa[n] = y.astype(BF16).reshape(2, 128, CHUNK)
        pm[n] = jnp.where(core == 0, y[:128], y[128:])
        remote(pa.at[n, 1 - core], cr.at[n], rcs, rcr.at[n], other_dev).start()

    def chip_sum(n):
        remote(pa.at[n, 1 - core], cr.at[n], rcs, rcr.at[n], other_dev).wait_recv()
        both = pm[n] + cr[n].astype(F32)
        pm[n] = both
        cs[n] = both.astype(BF16).reshape(4, 32, CHUNK)
        for copy in ret_far(n):
            copy.start()

    def ret_far(n):
        a = remote(
            cs.at[n, opposite, pl.ds(0, 16), :], far.at[0, n], rfs, rfr.at[n], right_dev
        )
        b = remote(
            cs.at[n, opposite, pl.ds(16, 16), :], far.at[1, n], rfs, rfr.at[n], left_dev
        )
        return a, b

    def ret_near(n):
        a = remote(cs.at[n, right], near.at[0, n], rns, rnr.at[n], right_dev)
        b = remote(cs.at[n, left], near.at[1, n], rns, rnr.at[n], left_dev)
        return a, b

    def ret_relay(n):
        both = near.at[0, n]
        remote(both, both, rfs, rfr.at[n], right_dev).wait_recv()
        to_right = pl.ds(pl.multiple_of(right * 32, 32), 16)
        to_left = pl.ds(pl.multiple_of(left * 32 + 16, 16), 16)
        cs[n, right, 0:16, :] = (pm[n, to_right, :] + far[0, n].astype(F32)).astype(BF16)
        cs[n, left, 16:32, :] = (pm[n, to_left, :] + far[1, n].astype(F32)).astype(BF16)
        for copy in ret_near(n):
            copy.start()

    def ret_sum(n):
        both = pa.at[n, 0, 0:64]
        remote(both, both, rns, rnr.at[n], right_dev).wait_recv()
        rows = pl.ds(pl.multiple_of(x * 32, 32), 32)
        y = pm[n, rows, :] + near[0, n].astype(F32) + near[1, n].astype(F32)
        y = y.astype(BF16)
        for (first, chunks), y2 in zip(OUT_PARTS, y2s):
            if first <= n < first + chunks:
                width = chunks * CHUNK // 8
                for q in range(CHUNK // width):
                    row = ((n - first) * (CHUNK // width) + q) * 32
                    y2[row : row + 32, :] = y[:, q * width : (q + 1) * width]

    def b_core():
        return remote(pbs, cbr, rbcs, rbcr, other_dev)

    def down_b(half):
        cols = pl.ds(pl.multiple_of(A_COLS + half * CHUNK, CHUNK), CHUNK)
        return dot(hidb[...], wd[:, cols])

    def b_other():
        hidb[...] = dot_nt(to_b, hidden).astype(BF16)
        pbs[...] = down_b(1 - core).astype(BF16)
        b_core().start()

    def b_mine():
        pbm[...] = down_b(core)

    def b_home():
        b_core().wait_recv()
        bsend[...] = (pbm[...] + cbr[...].astype(F32)).astype(BF16).reshape(16, 16, CHUNK)
        bback[me] = bsend[me]
        for dy, dz in PLANE:
            peer, device = plane(dy * 4 + dz)
            remote(bsend.at[peer], bback.at[me], rbs, rbr, device).start()

    rr = iota((256, 256), 0)
    ll = iota((256, 256), 1)
    repack_a = onehot(ll == (rr & 7) * 32 + (rr >> 3))

    def a_home(h):
        asend, aback = asends[h], abacks[h]
        value = dot(repack_a, y2s[h][...]).astype(BF16)
        asend[...] = value.reshape(16, 16, value.shape[1])
        aback[me] = asend[me]
        for dy, dz in PLANE:
            peer, device = plane(dy * 4 + dz)
            remote(asend.at[peer], aback.at[me], ras.at[h], rar.at[h], device).start()

    def home_tables():
        fixed = gates[...].astype(F32)
        weights = fixed / jnp.sum(fixed, axis=0, keepdims=True)
        weighted = jnp.zeros((32, 32), F32)
        for k in range(4):
            same = routes[k : k + 1, :] == (row32 >> 1)
            weighted = weighted + jnp.where(same, weights[k : k + 1, :], 0.0)
        wsel = weighted * sel.astype(F32)
        whi = wsel.astype(BF16)
        wlo = (wsel - whi.astype(F32)).astype(BF16)
        rr = iota((128, 256), 0)
        ll = iota((128, 256), 1)
        wide_hi = dot_nt(dot_nt(wide, whi).astype(BF16), spread_b)
        wide_lo = dot_nt(dot_nt(wide, wlo).astype(BF16), spread_b)
        for q in range(4):
            keep = ((rr >> 4) == ((ll & 15) >> 1)) & (((rr & 15) >> 2) == q)
            mix_b[2 * q] = jnp.where(keep, wide_hi, 0.0).astype(BF16)
            mix_b[2 * q + 1] = jnp.where(keep, wide_lo, 0.0).astype(BF16)
        rr = iota((64, 256), 0)
        ll = iota((64, 256), 1)
        keep = (rr >> 3) == (ll & 7)
        home_hi = dot_nt(dot_nt(mine, whi).astype(BF16), spread_a)
        home_lo = dot_nt(dot_nt(mine, wlo).astype(BF16), spread_a)
        mix_a[0] = jnp.where(keep, home_hi, 0.0).astype(BF16)
        mix_a[1] = jnp.where(keep, home_lo, 0.0).astype(BF16)
        rr = iota((64, 128), 0)
        ll = iota((64, 128), 1)
        gather[...] = onehot(
            ((rr >> 5) == ((ll >> 4) & 1))
            & (((rr >> 3) & 3) == ((ll & 15) >> 2))
            & ((rr & 7) == (ll & 3))
        )

    down_a(0)
    b_other()
    down_a(1)
    chip_sum(0)
    b_mine()
    down_a(2)
    chip_sum(1)
    down_a(3)
    b_home()
    chip_sum(2)
    chip_sum(3)
    ret_relay(0)
    ret_relay(1)
    ret_relay(2)
    ret_relay(3)
    home_tables()
    ret_sum(0)
    ret_sum(1)
    a_home(0)
    ret_sum(2)
    a_home(1)

    whole(bback, 15, rbs, rbr).wait_recv()
    partial = jnp.zeros((128, 256), F32)
    for q in range(4):
        piece = bback[:, :, q * 256 : q * 256 + 256].reshape(256, 256)
        partial = partial + dot(mix_b[2 * q], piece) + dot(mix_b[2 * q + 1], piece)
    fsend[...] = partial.astype(BF16).reshape(8, 16, 256)
    frecv[tp] = fsend[tp]

    def send_b4(step, carry):
        peer, device = column(step)
        remote(fsend.at[peer], frecv.at[tp], rfis, rfir, device).start()
        return carry

    lax.fori_loop(1, 8, send_b4, 0)
    ret_sum(3)
    a_home(2)
    drain()

    def finish_a(h):
        first, chunks = OUT_PARTS[h]
        width = chunks * CHUNK // 8
        whole(abacks[h], 15, ras.at[h], rar.at[h]).wait_recv()
        back = abacks[h][...].reshape(256, width)
        home_a = dot(mix_a[0], back) + dot(mix_a[1], back)
        for p in range(8):
            start = first * CHUNK + p * width
            cols = slice(start, start + width)
            out[:, cols] = (stream[0:4, cols] + home_a[p * 8 : p * 8 + 4, :]).astype(BF16)

    finish_a(0)
    finish_a(1)
    whole(frecv, 7, rfis, rfir).wait_recv()
    home_b = dot(gather[...], frecv[...].reshape(128, 256))
    for piece in range(8):
        start = A_COLS + piece * 256
        out[:, start : start + 256] = (
            stream[0:4, start : start + 256] + home_b[piece * 8 : piece * 8 + 4, :]
        ).astype(BF16)
    finish_a(2)
    for h, aback in enumerate(abacks):
        whole(aback, 15, ras.at[h], rar.at[h]).wait_send()


def layer(
    resid,
    query,
    key_cache,
    value_cache,
    new_key,
    new_value,
    cache_len,
    norm_gain,
    routes,
    gate_fixed,
    w_gate,
    w_up,
    w_down,
):
    vmem = pl.BlockSpec(memory_space=pltpu.VMEM)
    anywhere = pl.BlockSpec(memory_space=pl.ANY)
    dma = pltpu.SemaphoreType.DMA
    n = A_CHUNKS
    scratch = [
        pltpu.SMEM((ROWS,), jnp.int32),
        pltpu.VMEM((ROWS, D), BF16),
        pltpu.VMEM((ROWS, D), BF16),
        pltpu.VMEM((ROWS, 1024), BF16),
        pltpu.VMEM((ROWS, 1024), BF16),
        pltpu.VMEM((1, D), F32),
        pltpu.VMEM((4, 32), jnp.int32),
        pltpu.VMEM((4, 32), jnp.int32),
        pltpu.VMEM((ROWS, LENGTH, 1024), BF16),
        pltpu.VMEM((ROWS, LENGTH, 1024), BF16),
        pltpu.VMEM((HIDDEN, D), BF16),
        pltpu.VMEM((HIDDEN, D), BF16),
        pltpu.VMEM((HIDDEN, D), BF16),
        pltpu.VMEM((HEADS * ROWS, 128), F32),
        pltpu.VMEM((HEADS * ROWS, 128), F32),
        pltpu.VMEM((GROUP * ROWS, 1024), F32),
        pltpu.VMEM((GROUP * ROWS, 1024), F32),
        pltpu.VMEM((HEADS * ROWS, 128), F32),
        pltpu.VMEM((8, D), F32),
        pltpu.VMEM((64, 128), F32),
        pltpu.VMEM((64, 256), F32),
        pltpu.VMEM((32, PIECE), F32),
        pltpu.VMEM((16, 16, 128), BF16),
        pltpu.VMEM((16, 16, 256), BF16),
        pltpu.VMEM((16, 16, 128), BF16),
        pltpu.VMEM((16, 16, 256), BF16),
        pltpu.VMEM((16, PIECE), BF16),
        pltpu.VMEM((8, 16, PIECE), BF16),
        *[pltpu.VMEM((16, 16, width), BF16) for _, _, width in B_PARTS],
        *[pltpu.VMEM((2, 16, 16, width), BF16) for _, _, width in B_PARTS],
        pltpu.VMEM((IN_CHUNKS, 2, 4, 32, CHUNK), BF16),
        pltpu.VMEM((HIDDEN, 256), F32),
        pltpu.VMEM((HIDDEN, 256), F32),
        pltpu.VMEM((256, HIDDEN), BF16),
        pltpu.VMEM((256, HIDDEN), BF16),
        pltpu.VMEM((n, 2, 128, CHUNK), BF16),
        pltpu.VMEM((n, 128, CHUNK), F32),
        pltpu.VMEM((n, 128, CHUNK), BF16),
        pltpu.VMEM((n, 4, 32, CHUNK), BF16),
        pltpu.VMEM((2, n, 16, CHUNK), BF16),
        pltpu.VMEM((2, n, 32, CHUNK), BF16),
        *[pltpu.VMEM((256, c * CHUNK // 8), BF16) for _, c in OUT_PARTS],
        *[pltpu.VMEM((16, 16, c * CHUNK // 8), BF16) for _, c in OUT_PARTS],
        *[pltpu.VMEM((16, 16, c * CHUNK // 8), BF16) for _, c in OUT_PARTS],
        pltpu.VMEM((256, CHUNK), BF16),
        pltpu.VMEM((256, CHUNK), F32),
        pltpu.VMEM((256, CHUNK), BF16),
        pltpu.VMEM((16, 16, CHUNK), BF16),
        pltpu.VMEM((16, 16, CHUNK), BF16),
        pltpu.VMEM((8, 16, 256), BF16),
        pltpu.VMEM((8, 16, 256), BF16),
        pltpu.VMEM((2, 64, 256), BF16),
        pltpu.VMEM((8, 128, 256), BF16),
        pltpu.VMEM((64, 128), BF16),
        dma((13,)),
        dma((2,)),
        dma((2,)),
        dma,
        dma,
        dma((3,)),
        dma((3,)),
        dma((3,)),
        dma((3,)),
        dma,
        dma((2, IN_CHUNKS)),
        dma,
        dma((2, IN_CHUNKS)),
        dma,
        dma((IN_CHUNKS,)),
        dma,
        dma((n,)),
        dma,
        dma((n,)),
        dma,
        dma((n,)),
        dma((3,)),
        dma((3,)),
        dma,
        dma,
        dma,
        dma,
        dma,
        dma,
    ]
    return pl.pallas_call(
        kernel,
        out_shape=jax.ShapeDtypeStruct((ROWS, D), BF16),
        in_specs=[anywhere] * 13,
        out_specs=vmem,
        scratch_shapes=scratch,
        compiler_params=pltpu.CompilerParams(
            collective_id=0, has_side_effects=True, vmem_limit_bytes=60 * 1024 * 1024
        ),
        cost_estimate=pl.CostEstimate(
            flops=2 * 3 * 256 * HIDDEN * D, bytes_accessed=27 * 1024 * 1024, transcendentals=0
        ),
    )(
        cache_len,
        resid,
        query,
        new_key,
        new_value,
        norm_gain.reshape(1, D),
        routes.T,
        gate_fixed.T,
        key_cache,
        value_cache,
        w_gate,
        w_up,
        w_down,
    )


def solution(mesh):
    placed = (
        P(("side", "expert", "tp"), None),
        P(("side", "expert", "tp"), None),
        P(("side", "expert", "tp"), None, None),
        P(("side", "expert", "tp"), None, None),
        P(("side", "expert", "tp"), None),
        P(("side", "expert", "tp"), None),
        P(("side", "expert", "tp")),
        P(),
        P(("side", "expert"), None),
        P(("side", "expert"), None),
        P(("side", "expert"), "tp", None),
        P(("side", "expert"), "tp", None),
        P(("side", "expert"), "tp", None),
    )
    return jax.shard_map(
        layer,
        mesh=mesh,
        in_specs=placed,
        out_specs=P(("side", "expert", "tp"), None),
        check_vma=False,
    )
```
